512 devices in a mesh: tp: 8 (over x, y_hi), dp: 16 (over z, core), edp: 4 (over y_lo).
Axes of the slice: x: 4, y: 8 (y_hi: 2, y_lo: 4; y = y_hi * 4 + y_lo), z: 8, core: 2. Of those that a mesh axis runs over, the one named last changes fastest.
Arguments:
- grad_out: bfloat16 [8192, 4096], P(('dp', 'edp')), may hold values from -0.29882812 to 0.29882812
- routes: int32 [8192, 8], P(('dp', 'edp')), may hold values from 0 to 63, all different within a row; in each aligned block of 128 rows (0 to 127, 128 to 255, ...) at most 20 rows name the same one
- gates: bfloat16 [8192, 8], P(('dp', 'edp')), may hold values from 0.099609375 to 1
- hidden: bfloat16 [64, 1536, 1280], P(('dp', 'edp'), 'tp'), may hold values from -40 to 40
- w_down: bfloat16 [64, 1536, 4096], P(('dp', 'edp'), 'tp'), may hold values from -0.15625 to 0.15625
Outputs:
- down_grad: bfloat16 [64, 1536, 4096], P(('dp', 'edp'), 'tp')
- gate_grad: float32 [8192, 8], P(('dp', 'edp'))
The draws below stay inside these ranges and needn't reach their ends.
Inputs may be any that keep to these rules, and one draw needn't show every extreme that they name: `routes`: each row names 8 different experts. Within the 128 rows of one index of dp+edp no expert is named more than 20 times, and in every draw some expert is named exactly 20 times in some block.
All inputs are finite; a program needn't handle non-finite values.
Results may differ from the reference program's by a relative error of at most 0.0049.
Values may be sent and summed in bfloat16 or wider, within the bound.
A program may use at most 128 MiB of HBM per device.

```python
import math
import jax
import jax.numpy as jnp
import numpy as np
from jax import lax

D = 4096
FF = 1536
TOP = 8
TOK_DEV = 128
EXPERTS = 64
CAP = 20
SLOTS = 1280
TOKENS = 8192


def draw_hidden(key, part):
    key = jax.random.fold_in(key, 7)
    expert_scale = 1.0 + 2.0 * jnp.arange(EXPERTS, dtype=jnp.float32) / max(EXPERTS - 1, 1)
    unit_scale = 1.0 + jnp.arange(FF, dtype=jnp.float32) / FF
    scale = expert_scale[:, None, None] * unit_scale[None, :, None]
    value = jnp.clip(jax.random.normal(key, (EXPERTS, FF, SLOTS), jnp.float32), -4.0, 4.0) * scale
    return value.astype(jnp.bfloat16)


def shard_levels(stream_key, extent, shards, smallest, high):
    def one(axis_at, shards_of):
        heights = jax.random.uniform(jax.random.fold_in(jax.random.fold_in(stream_key, 6), axis_at), (shards_of,), jnp.float32, smallest / len(shards), high / len(shards))
        return jnp.repeat(jnp.exp(heights), extent[axis_at] // shards_of).reshape((-1,) + (1,) * (len(extent) - axis_at - 1))

    loudness = one(*shards[0])
    for cut in shards[1:]:
        loudness = loudness * one(*cut)
    return loudness


def deal_out(rng, own, number, rows, amount, top, most, slope):
    order = jax.random.permutation(rng, amount)
    crowded, ordinary = load_shares(amount, rows * top, most, slope, True), load_shares(amount, rows * top, most, slope, False)
    places = jnp.arange(amount)

    def named(sizes, turn):
        used = int((sizes > 0).sum())
        fixed = max(1, used // 4)
        passed = fixed + (places - fixed + turn * (used - fixed)) % max(1, amount - fixed)
        return jnp.zeros((amount,), jnp.int32).at[order[jnp.where(places < fixed, places, passed)]].set(jnp.asarray(sizes, jnp.int32))

    sizes = jnp.where(number % 4 == 0, named(crowded, number // 4), named(ordinary, number - number // 4 - 1))
    mixed = jax.random.permutation(jax.random.fold_in(own, 3), amount)
    giver, receiver = mixed[0:amount // 2 * 2:2], mixed[1:amount // 2 * 2:2]
    slack = jnp.minimum(sizes[giver] - 1, most - sizes[receiver]) // 2
    slack = jnp.where((giver == order[0]) | (receiver == order[0]) | (sizes[receiver] == 0), 0, jnp.maximum(slack, 0))
    passed = jax.random.randint(jax.random.fold_in(own, 4), (amount // 2,), 0, 1 << 20) % (slack + 1)
    sizes = sizes.at[giver].add(-passed).at[receiver].add(passed)
    items = jnp.searchsorted(jnp.cumsum(sizes), jnp.arange(rows * top), side="right").astype(jnp.int32)
    table = items.reshape(top, rows).T
    table = table[jax.random.permutation(jax.random.fold_in(own, 1), rows)]
    turn = jax.random.randint(jax.random.fold_in(own, 2), (rows, 1), 0, top)
    return jnp.take_along_axis(table, (jnp.arange(top)[None, :] + turn) % top, axis=1)


def load_shares(number_of, total, most, lean, full):
    weights = [(1 << 20) // math.isqrt(rank ** lean) + 1 for rank in range(1, number_of + 1)]
    largest = most if full else min(most, max(-(-total // number_of), total * weights[0] // sum(weights)))
    least = 1 if total - largest >= number_of - 1 else 0
    holding, spare = [largest] + [least] * (number_of - 1), total - largest - least * (number_of - 1)
    while spare > 0:
        candidates = [i for i in range(1, number_of) if holding[i] < largest] or [i for i in range(1, number_of) if holding[i] < most]
        mass, left = sum([weights[i] for i in candidates]), spare
        for i in candidates:
            extra = min(most - holding[i], max(1, left * weights[i] // mass), spare)
            holding[i] = holding[i] + extra
            spare = spare - extra
    return np.array(holding)


def noise(rng, dims, spread, most, shards=(), kind=jnp.bfloat16):
    drawn = jax.random.normal(rng, dims, jnp.float32) * spread
    if len(shards) > 0:
        drawn = shard_levels(rng, dims, shards, -0.22, 0.18) * drawn
    return jnp.clip(drawn, min=-most, max=most).astype(kind)


def setup_inputs(seed: int = 0) -> dict:
    splits = jax.random.split(jax.random.key(seed), 6)
    grad_out = noise(splits[0], (TOKENS, D), 0.05, 0.29882812, ((0, 64),))
    routes_keys = jax.random.split(jax.random.fold_in(splits[1], 1), TOKENS // TOK_DEV)
    routes_turns = jax.random.permutation(jax.random.fold_in(splits[1], 3), TOKENS // TOK_DEV)
    routes = jax.vmap(lambda own, number: deal_out(jax.random.fold_in(splits[1], 2), own, number, TOK_DEV, EXPERTS, TOP, CAP, 2))(routes_keys, routes_turns).reshape((TOKENS, TOP))
    gates = jnp.clip(jnp.exp(math.log(1.0) - 2.306499 * jax.random.uniform(splits[2], (TOKENS, TOP), jnp.float32) ** shard_levels(splits[2], (TOKENS, TOP), ((0, 64),), -0.2, 0.2)), 0.099609375, 1.0).astype(jnp.bfloat16)
    hidden = draw_hidden(jax.random.fold_in(splits[5], 71), 0)
    w_down = noise(splits[4], (EXPERTS, FF, D), FF ** -0.5, 0.15625, ((0, 64), (1, 8)))
    return dict(grad_out=grad_out, routes=routes, gates=gates, hidden=hidden, w_down=w_down)


clip_ratio = 0.25

def slot_tables(routes):
    source_blocks = routes.reshape(EXPERTS, TOK_DEV * TOP)

    def plan_block(source_block):
        onehot = (source_block[:, None] == jnp.arange(EXPERTS, dtype=jnp.int32)[None, :]).astype(jnp.int32)
        before = jnp.cumsum(onehot, axis=0) - onehot
        position = lax.optimization_barrier(jnp.sum(before * onehot, axis=1))
        target = source_block * CAP + position
        filler = jnp.zeros((EXPERTS * CAP,), jnp.int32).at[target].set(jnp.arange(TOK_DEV * TOP, dtype=jnp.int32))
        filled = jnp.zeros((EXPERTS * CAP,), jnp.int32).at[target].set(1)
        return (target, filler, filled)
    return lax.map(plan_block, source_blocks)

def reference(grad_out, routes, gates, hidden, w_down):
    target, filler, filled = slot_tables(routes)
    flat_gates = gates.reshape(-1)
    source_ids = jnp.arange(EXPERTS, dtype=jnp.int32)[:, None]

    def one_expert(operands):
        expert_id, hidden_part, weight_part = operands
        fill_part = lax.dynamic_slice_in_dim(filler, expert_id * CAP, CAP, 1)
        live_part = lax.dynamic_slice_in_dim(filled, expert_id * CAP, CAP, 1).reshape(-1).astype(jnp.bfloat16)
        token_ids = (source_ids * TOK_DEV + fill_part // TOP).reshape(-1)
        pair_ids = (source_ids * (TOK_DEV * TOP) + fill_part).reshape(-1)
        row_block = grad_out[token_ids] * live_part[:, None]
        gate_rows = flat_gates[pair_ids] * live_part
        back_proj = jnp.dot(weight_part, row_block.T, preferred_element_type=jnp.float32)
        partial_value = lax.optimization_barrier(jnp.sum(hidden_part.astype(jnp.float32) * back_proj, axis=0))
        scaled = (hidden_part.astype(jnp.float32) * gate_rows.astype(jnp.float32)[None, :]).astype(jnp.bfloat16)
        weight_grad = jnp.dot(scaled, row_block, preferred_element_type=jnp.float32)
        return (weight_grad, partial_value)
    weight_grads, partials = lax.map(one_expert, (jnp.arange(EXPERTS, dtype=jnp.int32), hidden, w_down))
    by_source = partials.reshape(EXPERTS, EXPERTS, CAP).transpose(1, 0, 2).reshape(EXPERTS, EXPERTS * CAP)
    gate_grad = jnp.take_along_axis(by_source, target, axis=1).reshape(TOKENS, TOP)
    norm = jnp.sqrt(jnp.sum(weight_grads * weight_grads))
    limit = clip_ratio * math.sqrt(EXPERTS * FF * D)
    factor = jnp.minimum(1.0, limit / (norm + 1e-06))
    down_grad = (weight_grads * factor).astype(jnp.bfloat16)
    return (down_grad, gate_grad)
```

```python
import functools
import math

import jax
import jax.numpy as jnp
from jax import lax
from jax.experimental import pallas as pl
from jax.experimental.pallas import tpu as pltpu
from jax.sharding import PartitionSpec as P

clip_ratio = 0.25

XS, HS, ZS, CS, YS = 4, 2, 8, 2, 4
NQ = 4
CAP = 20
MESH = pl.DeviceIdType.MESH
F32, BF16 = jnp.float32, jnp.bfloat16

K_Q, K_G, K_GY, K_PA, K_PB, K_PC, K_RY, K_RZ, K_GG = range(9)


def iota(shape, dim):
    return lax.broadcasted_iota(jnp.int32, shape, dim)


def kernel(
    routes_ref, gates_ref, grad_hbm, hid_hbm, w_hbm,
    out_hbm, total_ref, gg_ref,
    tok, sel, sendb, rows, qsend, qrecv, gsend, grecv, gsy, gtab,
    hraw, perm, hx, hs, hxt, wv, wgs, acc, pa, pb, pc, rsend, ry, rzs, rz, gg,
    loc, zs, zr, ys, yr, ws, wr, hsn, hr, osn, orc, sms, smr,
):
    E8 = CS * YS
    TPS = XS * HS
    EXP = ZS * E8
    TOK, TOP = routes_ref.shape[1], routes_ref.shape[0]
    FFD = hid_hbm.shape[1]
    SLOTS = hid_hbm.shape[2]
    DX = w_hbm.shape[2] // XS
    DQ = DX // NQ
    BLK = ZS * CAP
    GZ = min(4, ZS)
    HALF = ZS // 2

    tp = lax.axis_index("tp")
    dp = lax.axis_index("dp")
    y = lax.axis_index("edp")
    x, h = lax.div(tp, HS), lax.rem(tp, HS)
    z, c = lax.div(dp, CS), lax.rem(dp, CS)
    yy = h * YS + y
    me8 = c * YS + y

    def at_y(delta, core):
        there = lax.rem(yy + delta + HS * YS, HS * YS)
        ylo = lax.rem(there, YS)
        return (x * HS + lax.div(there, YS), z * CS + core, ylo), core * YS + ylo

    def at_z(delta):
        zz = lax.rem(z + delta + ZS, ZS)
        return (tp, zz * CS + c, y), zz

    def at_x(delta):
        xx = lax.rem(x + delta, XS)
        return (xx * HS + h, dp, y), xx

    def at_tp(delta):
        tt = lax.rem(tp + delta, TPS)
        return (tt, dp, y), tt

    far = 2 - 4 * c
    out_y = [at_y(0, 1 - c), at_y(1, 0), at_y(-1, 0), at_y(1, 1), at_y(-1, 1), at_y(2, 0), at_y(-2, 1)]
    back_y = out_y[:5] + [at_y(-far, 0), at_y(-far, 1)]
    peers_z = [at_z(i) for i in range(1, ZS)]
    peers_x = [at_x(i) for i in range(1, XS)]
    peers_tp = [at_tp(i) for i in range(1, TPS)]

    barrier = pltpu.get_barrier_semaphore()
    hello = [d for d, _ in peers_z] + [d for d, _ in peers_tp] + [d for d, _ in out_y]
    hello = hello + [at_y(-far, c)[0]]
    for d in hello:
        pl.semaphore_signal(barrier, inc=1, device_id=d, device_id_type=MESH)

    def col(start):
        return pl.ds(pl.multiple_of(start, DQ), DQ)

    def blk(start, size):
        return pl.ds(pl.multiple_of(start * size, size), size)

    get_h = pltpu.make_async_copy(hid_hbm.at[0], hraw, loc.at[0])
    get_h.start()
    get_t = [
        pltpu.make_async_copy(grad_hbm.at[:, col(x * DX + q * DQ)], tok.at[q, blk(z, TOK)], loc.at[1 + q])
        for q in range(NQ)
    ]
    for d in get_t:
        d.start()

    def own_w(q):
        return pltpu.make_async_copy(
            w_hbm.at[0, :, col(x * DX + q * DQ)], wv.at[q, blk(x, FFD)], loc.at[1 + NQ + q])

    for q in range(NQ):
        own_w(q).start()

    eidx = iota((EXP, TOK), 0)
    chosen = jnp.zeros((EXP, TOK), F32)
    gate_t = jnp.zeros((EXP, TOK), F32)
    gates_f = gates_ref[...].astype(F32)
    for k in range(TOP):
        hit = routes_ref[k:k + 1, :] == eidx
        chosen = jnp.where(hit, 1.0, chosen)
        gate_t = jnp.where(hit, gates_f[k:k + 1, :], gate_t)
    earlier = (iota((TOK, TOK), 0) < iota((TOK, TOK), 1)).astype(F32).astype(BF16)
    count = jnp.dot(chosen.astype(BF16), earlier, preferred_element_type=F32)
    qt = jnp.where(chosen > 0.5, count, -1.0)
    for i in range(ZS):
        qsend[i] = qt[i * E8:(i + 1) * E8]
    qrecv[z] = qsend[z]

    pl.semaphore_wait(barrier, len(hello))

    def small(kind, i, src, dst, mine, dev):
        return pltpu.make_async_remote_copy(
            src_ref=src, dst_ref=dst.at[mine], send_sem=sms.at[kind, i], recv_sem=smr.at[kind, mine],
            device_id=dev, device_id_type=MESH)

    def small_start(kind, peers, src_of, dst, mine):
        for i, (dev, there) in enumerate(peers):
            small(kind, i, src_of(there), dst, mine, dev).start()

    def small_wait(kind, peers, dst):
        for i, (dev, there) in enumerate(peers):
            small(kind, i, dst.at[there], dst, there, dev).wait_recv()

    def small_done(kind, peers, src_of, dst, mine):
        for i, (dev, there) in enumerate(peers):
            small(kind, i, src_of(there), dst, mine, dev).wait_send()

    def ring(q, block, right, i):
        dev = peers_z[0][0] if right else peers_z[ZS - 2][0]
        part = tok.at[q, blk(block, TOK)]
        return pltpu.make_async_remote_copy(
            src_ref=part, dst_ref=part, send_sem=zs.at[q, i], recv_sem=zr.at[q, block],
            device_id=dev, device_id_type=MESH)

    def zb(delta):
        return lax.rem(z + delta + ZS, ZS)

    sent = []

    def ring_step(q, s):
        ways = [True, False] if s < HALF else [q % 2 == 0]
        for right in ways:
            block = zb(-(s - 1)) if right else zb(s - 1)
            if s > 1:
                ring(q, block, right, 0).wait_recv()
            i = 2 * (s - 1) + (0 if right else 1)
            if s == HALF:
                i = 2 * (s - 1)
            d = ring(q, block, right, i)
            d.start()
            sent.append(d)

    def ring_end(q):
        if HALF > 1:
            left_over = zb(HALF - 1) if q % 2 == 0 else zb(-(HALF - 1))
            ring(q, left_over, True, 0).wait_recv()
        ring(q, zb(HALF), True, 0).wait_recv()

    def send_w(q, i):
        dev, there = peers_x[i]
        return pltpu.make_async_remote_copy(
            src_ref=w_hbm.at[0, :, col(there * DX + q * DQ)], dst_ref=wv.at[q, blk(x, FFD)],
            send_sem=ws.at[q, i], recv_sem=wr.at[q, x], device_id=dev, device_id_type=MESH)

    def send_h(i):
        dev, there = peers_x[i]
        part = hx.at[blk(x, FFD)]
        return pltpu.make_async_remote_copy(
            src_ref=part, dst_ref=part, send_sem=hsn.at[i], recv_sem=hr.at[x], device_id=dev, device_id_type=MESH)

    for q in range(NQ):
        if q < 1:
            get_t[q].wait()
            ring_step(q, 1)
    small_start(K_Q, peers_z, lambda there: qsend.at[there], qrecv, z)
    for i in range(XS - 1):
        send_w(0, i).start()

    lane = (iota((1, SLOTS), 1).astype(F32) + 0.5)
    group = jnp.floor(lane * (1.0 / BLK))
    inner = lane - group * BLK
    zpart = jnp.floor(inner * (1.0 / CAP))
    place = inner - zpart * CAP - 0.5
    native = (zpart * (E8 * CAP) + group * CAP + place).astype(jnp.int32)
    source = (group * ZS + zpart).astype(jnp.int32)
    place = place.astype(jnp.int32)

    PB = 128

    def build_perm(i, carry):
        perm[pl.ds(pl.multiple_of(i * PB, PB), PB), :] = (
            (iota((PB, SLOTS), 0) + i * PB) == native).astype(F32).astype(BF16)
        return carry

    lax.fori_loop(0, SLOTS // PB, build_perm, 0)
    get_h.wait()
    hx[blk(x, FFD), :] = jnp.dot(hraw[...], perm[...], preferred_element_type=F32).astype(BF16)
    for i in range(XS - 1):
        send_h(i).start()
    for q in range(1, NQ):
        for i in range(XS - 1):
            send_w(q, i).start()

    table = jnp.zeros((EXP, TOK), F32)
    pidx = iota((EXP, TOK), 1)
    for p in range(CAP):
        value = jnp.sum(jnp.where(qt == float(p), gate_t, 0.0), axis=1, keepdims=True)
        table = jnp.where(pidx == p, value, table)
    for i in range(ZS):
        gsend[i] = table[i * E8:(i + 1) * E8]
    grecv[z] = gsend[z]
    small_start(K_G, peers_z, lambda there: gsend.at[there], grecv, z)

    def build_sel():
        small_wait(K_Q, peers_z, qrecv)
        ridx = iota((GZ * CAP, TOK), 0).astype(F32)
        for g in range(ZS // GZ):
            for i in range(GZ):
                tile = qrecv[g * GZ + i]
                want = jnp.where(tile >= 0.0, tile + float(i * CAP), -1.0)
                for e in range(E8):
                    sel[g, e * GZ * CAP:(e + 1) * GZ * CAP, i * TOK:(i + 1) * TOK] = (
                        ridx == want[e:e + 1, :]).astype(F32).astype(BF16)

    def send_y(q, i):
        dev, there = out_y[i]
        return pltpu.make_async_remote_copy(
            src_ref=sendb.at[q, there], dst_ref=rows.at[q, blk(me8, BLK)],
            send_sem=ys.at[q, i], recv_sem=yr.at[q, me8], device_id=dev, device_id_type=MESH)

    def own_rows(q):
        return pltpu.make_async_copy(sendb.at[q, me8], rows.at[q, blk(me8, BLK)], loc.at[1 + 2 * NQ + q])

    def select(q):
        for g in range(ZS // GZ):
            got = jnp.dot(sel[g], tok[q, g * GZ * TOK:(g + 1) * GZ * TOK, :], preferred_element_type=F32).astype(BF16)
            for e in range(E8):
                sendb[q, e, g * GZ * CAP:(g + 1) * GZ * CAP, :] = got[e * GZ * CAP:(e + 1) * GZ * CAP]
        for i in range(E8 - 1):
            send_y(q, i).start()
        own_rows(q).start()

    for t in range(2, HALF + NQ + 1):
        for q in range(NQ):
            s = t - q
            if s == 1:
                get_t[q].wait()
            if 1 <= s <= HALF:
                ring_step(q, s)
            if s == HALF + 1:
                if q == 0:
                    build_sel()
                ring_end(q)
                select(q)
                if q == 0:
                    small_wait(K_G, peers_z, grecv)
                    for zz in range(ZS):
                        for e in range(E8):
                            gsy[e, zz:zz + 1, :] = grecv[zz, e:e + 1, :]
                    gtab[me8] = gsy[me8]
                    small_start(K_GY, out_y, lambda there: gsy.at[there], gtab, me8)

    small_wait(K_GY, out_y, gtab)
    spread = (iota((TOK, SLOTS), 0) == place).astype(F32).astype(BF16)
    gsrc = gtab[...].reshape(EXP, TOK).astype(BF16)
    gate_all = jnp.dot(gsrc, spread, preferred_element_type=F32)
    pick = iota((EXP, SLOTS), 0) == source
    gate_lane = jnp.sum(jnp.where(pick, gate_all, 0.0), axis=0, keepdims=True)
    for i in range(XS):
        if i > 0:
            dev, there = peers_x[i - 1]
            pltpu.make_async_remote_copy(
                src_ref=hx.at[blk(there, FFD)], dst_ref=hx.at[blk(there, FFD)], send_sem=hsn.at[0],
                recv_sem=hr.at[there], device_id=dev, device_id_type=MESH).wait_recv()
    for i in range(XS):
        part = slice(i * FFD, (i + 1) * FFD)
        hs[part, :] = (hx[part, :].astype(F32) * gate_lane).astype(BF16)
    for j in range(SLOTS // PB):
        hxt[j * PB:(j + 1) * PB, :] = hx[:, j * PB:(j + 1) * PB].T

    def wait_w(q):
        own_w(q).wait()
        for i in range(XS - 1):
            dev, there = peers_x[i]
            pltpu.make_async_remote_copy(
                src_ref=w_hbm.at[0, :, col(x * DX + q * DQ)], dst_ref=wv.at[q, blk(there, FFD)],
                send_sem=ws.at[q, 0], recv_sem=wr.at[q, there], device_id=dev, device_id_type=MESH).wait_recv()

    def wait_rows(q):
        own_rows(q).wait()
        for i in range(E8 - 1):
            dev, there = out_y[i]
            pltpu.make_async_remote_copy(
                src_ref=sendb.at[q, there], dst_ref=rows.at[q, blk(there, BLK)],
                send_sem=ys.at[q, 0], recv_sem=yr.at[q, there], device_id=dev, device_id_type=MESH).wait_recv()

    def send_o(q, i):
        dev, there = peers_x[i]
        return pltpu.make_async_remote_copy(
            src_ref=wgs.at[q, blk(there, FFD)], dst_ref=out_hbm.at[0, :, col(x * DX + q * DQ)],
            send_sem=osn.at[q, i], recv_sem=orc.at[q, x], device_id=dev, device_id_type=MESH)

    def own_o(q):
        return pltpu.make_async_copy(
            wgs.at[q, blk(x, FFD)], out_hbm.at[0, :, col(x * DX + q * DQ)], loc.at[1 + 3 * NQ + q])

    acc[...] = jnp.zeros_like(acc)
    order = [1, 0, 2, 3][:XS - 1] if XS == 4 else list(range(XS - 1))
    order = [i for i in order if i < XS - 1] + [None]

    def chunk(q, squares):
        wait_rows(q)
        for i in order:
            there = x if i is None else peers_x[i][1]
            wg = jnp.dot(hs[blk(there, FFD), :], rows[q], preferred_element_type=F32)
            wgs[q, blk(there, FFD), :] = wg.astype(BF16)
            if i is None:
                own_o(q).start()
            else:
                send_o(q, i).start()
            squares = squares + jnp.sum((wg * wg).reshape(FFD // 8, 8, DQ), axis=0)
        wait_w(q)
        gback = jnp.dot(hxt[...], wv[q], preferred_element_type=F32)
        both = gback * rows[q].astype(F32)
        for i in range(DQ // 128):
            acc[...] += both[:, i * 128:(i + 1) * 128]
        return squares

    squares = lax.fori_loop(0, NQ, chunk, jnp.zeros((8, DQ), F32))
    tile = squares[:, 0:128]
    for i in range(1, DQ // 128):
        tile = tile + squares[:, i * 128:(i + 1) * 128]

    pa[tp] = tile
    small_start(K_PA, peers_tp, lambda there: pa.at[tp], pa, tp)

    partial = jnp.sum(acc[...], axis=1, keepdims=True)
    place_t = place_col(SLOTS, CAP)
    by_place = jnp.where(iota((SLOTS, TOK), 1) == place_t, partial, 0.0)
    back = jnp.dot(pick.astype(F32), by_place, preferred_element_type=F32, precision=lax.Precision.HIGHEST)
    for e in range(E8):
        rsend[e] = back[e * ZS:(e + 1) * ZS]
    ry[me8] = rsend[me8]
    small_start(K_RY, back_y, lambda there: rsend.at[there], ry, me8)

    small_wait(K_PA, peers_tp, pa)
    pb[me8] = jnp.sum(pa[...], axis=0)
    small_start(K_PB, out_y, lambda there: pb.at[me8], pb, me8)

    small_wait(K_RY, out_y, ry)
    for zz in range(ZS):
        for e in range(E8):
            rzs[zz, e:e + 1, :] = ry[e, zz:zz + 1, :]
    rz[z] = rzs[z]
    small_start(K_RZ, peers_z, lambda there: rzs.at[there], rz, z)

    small_wait(K_PB, out_y, pb)
    pc[z] = jnp.sum(pb[...], axis=0)
    small_start(K_PC, peers_z, lambda there: pc.at[z], pc, z)

    small_wait(K_RZ, peers_z, rz)
    by_expert = rz[...].reshape(EXP, TOK)
    qt2 = qsend[...].reshape(EXP, TOK)
    value = jnp.zeros((EXP, TOK), F32)
    for p in range(CAP):
        value = jnp.where(qt2 == float(p), by_expert[:, p:p + 1], value)
    found = [
        jnp.sum(jnp.where(routes_ref[k:k + 1, :] == eidx, value, 0.0), axis=0, keepdims=True) for k in range(TOP)
    ]
    gg[tp] = jnp.concatenate(found, axis=0)
    small_start(K_GG, peers_tp, lambda there: gg.at[tp], gg, tp)

    small_wait(K_PC, peers_z, pc)
    total_ref[...] = jnp.sum(pc[...], axis=0)
    small_wait(K_GG, peers_tp, gg)
    gg_ref[...] = jnp.sum(gg[...], axis=0)

    for q in range(NQ):
        own_o(q).wait()
        for i in range(XS - 1):
            dev, there = peers_x[i]
            pltpu.make_async_remote_copy(
                src_ref=wgs.at[q, blk(there, FFD)], dst_ref=out_hbm.at[0, :, col(there * DX + q * DQ)],
                send_sem=osn.at[q, 0], recv_sem=orc.at[q, there], device_id=dev, device_id_type=MESH).wait_recv()
            send_o(q, i).wait_send()
            send_w(q, i).wait_send()
        for i in range(E8 - 1):
            send_y(q, i).wait_send()
    for i in range(XS - 1):
        send_h(i).wait_send()
    for d in sent:
        d.wait_send()
    small_done(K_Q, peers_z, lambda there: qsend.at[there], qrecv, z)
    small_done(K_G, peers_z, lambda there: gsend.at[there], grecv, z)
    small_done(K_GY, out_y, lambda there: gsy.at[there], gtab, me8)
    small_done(K_PA, peers_tp, lambda there: pa.at[tp], pa, tp)
    small_done(K_PB, out_y, lambda there: pb.at[me8], pb, me8)
    small_done(K_PC, peers_z, lambda there: pc.at[z], pc, z)
    small_done(K_RY, back_y, lambda there: rsend.at[there], ry, me8)
    small_done(K_RZ, peers_z, lambda there: rzs.at[there], rz, z)
    small_done(K_GG, peers_tp, lambda there: gg.at[tp], gg, tp)


def place_col(slots, cap):
    at = iota((slots, 1), 0).astype(F32) + 0.5
    return (at - jnp.floor(at * (1.0 / cap)) * cap - 0.5).astype(jnp.int32)


def per_device(grad_out, routes, gates, hidden, w_down):
    E8, TPS = CS * YS, XS * HS
    EXP = ZS * E8
    TOK, D = grad_out.shape
    TOP = routes.shape[1]
    FFD, SLOTS = hidden.shape[1], hidden.shape[2]
    DX = D // XS
    DQ = DX // NQ
    GZ = min(4, ZS)
    BLK = ZS * CAP
    vm = pltpu.VMEM
    dma = pltpu.SemaphoreType.DMA
    most = max(TPS, E8, ZS)
    any_space = pl.BlockSpec(memory_space=pl.ANY)
    in_vmem = pl.BlockSpec(memory_space=pltpu.VMEM)
    part, squares, gate_grad = pl.pallas_call(
        kernel,
        out_shape=(
            jax.ShapeDtypeStruct((1, FFD, D), BF16),
            jax.ShapeDtypeStruct((8, 128), F32),
            jax.ShapeDtypeStruct((TOP, TOK), F32),
        ),
        in_specs=[in_vmem, in_vmem, any_space, any_space, any_space],
        out_specs=(any_space, in_vmem, in_vmem),
        scratch_shapes=[
            vm((NQ, ZS * TOK, DQ), BF16),
            vm((ZS // GZ, E8 * GZ * CAP, GZ * TOK), BF16),
            vm((NQ, E8, BLK, DQ), BF16),
            vm((NQ, SLOTS, DQ), BF16),
            vm((ZS, E8, TOK), F32),
            vm((ZS, E8, TOK), F32),
            vm((ZS, E8, TOK), F32),
            vm((ZS, E8, TOK), F32),
            vm((E8, ZS, TOK), F32),
            vm((E8, ZS, TOK), F32),
            vm((FFD, SLOTS), BF16),
            vm((SLOTS, SLOTS), BF16),
            vm((XS * FFD, SLOTS), BF16),
            vm((XS * FFD, SLOTS), BF16),
            vm((SLOTS, XS * FFD), BF16),
            vm((NQ, XS * FFD, DQ), BF16),
            vm((NQ, XS * FFD, DQ), BF16),
            vm((SLOTS, 128), F32),
            vm((TPS, 8, 128), F32),
            vm((E8, 8, 128), F32),
            vm((ZS, 8, 128), F32),
            vm((E8, ZS, TOK), F32),
            vm((E8, ZS, TOK), F32),
            vm((ZS, E8, TOK), F32),
            vm((ZS, E8, TOK), F32),
            vm((TPS, TOP, TOK), F32),
            dma((1 + 4 * NQ,)),
            dma((NQ, ZS)),
            dma((NQ, ZS)),
            dma((NQ, E8)),
            dma((NQ, E8)),
            dma((NQ, XS)),
            dma((NQ, XS)),
            dma((XS,)),
            dma((XS,)),
            dma((NQ, XS)),
            dma((NQ, XS)),
            dma((9, most)),
            dma((9, most)),
        ],
        compiler_params=pltpu.CompilerParams(
            collective_id=0, has_side_effects=True, vmem_limit_bytes=56 * 1024 * 1024),
        cost_estimate=pl.CostEstimate(
            flops=2 * 2 * SLOTS * FFD * D, bytes_accessed=8 * 1024 * 1024, transcendentals=0),
        name="moe_down_backward",
    )(routes.T, gates.T, grad_out, hidden, w_down)
    entries = FFD * D * TPS * EXP
    clip_limit = clip_ratio * math.sqrt(entries)
    factor = jnp.minimum(1.0, clip_limit / (jnp.sqrt(jnp.sum(squares)) + 1e-06))
    down_grad = (part.astype(F32) * factor).astype(BF16)
    return (down_grad, gate_grad.T)


def solution(mesh):
    in_specs = (
        P(("dp", "edp"), None),
        P(("dp", "edp"), None),
        P(("dp", "edp"), None),
        P(("dp", "edp"), "tp", None),
        P(("dp", "edp"), "tp", None),
    )
    out_specs = (P(("dp", "edp"), "tp", None), P(("dp", "edp"), None))
    return jax.shard_map(
        per_device, mesh=mesh, in_specs=in_specs, out_specs=out_specs, check_vma=False
    )
```

```python
import functools
import math

import jax
import jax.numpy as jnp
from jax import lax
from jax.experimental import pallas as pl
from jax.experimental.pallas import tpu as pltpu
from jax.sharding import PartitionSpec as P

clip_ratio = 0.25

XS, HS, ZS, CS, YS = 4, 2, 8, 2, 4
NQ = 2
NR = 4
CAP = 20
AWAY = {8: [0, 1, -1, -2, 2, 3, -3, 4], 4: [0, 1, -1, 2], 2: [0, 1]}
MESH = pl.DeviceIdType.MESH
F32, BF16 = jnp.float32, jnp.bfloat16


def slot_groups():
    whole = CAP // 16 * 16
    rest = lambda parts: [(r, whole, CAP) for r in parts if CAP > whole]
    head = lambda parts: [(r, 0, whole) for r in parts]
    if ZS == 8:
        return [head([0, 1, 2]), head([3, 4]) + rest([0, 1, 2, 3]), head([5, 6]), head([7]) + rest([4, 5, 6, 7])]
    if ZS == 4:
        return [head([0, 1, 2]), head([3]) + rest([0, 1, 2, 3])]
    return [head([0, 1]) + rest([0, 1])]


K_Q, K_GY, K_RY, K_RZ, K_GG = range(5)


def iota(shape, dim):
    return lax.broadcasted_iota(jnp.int32, shape, dim)


def kernel(
    routes_hbm, gates_hbm, grad_hbm, hid_hbm, w_hbm,
    out_hbm, factor_ref, gg_ref,
    routes_ref, gates_ref, tok, sel, sendb, rows, qsend, qrecv, gsy, gtab,
    hraw, perm, hx, hs, hxt, wv, wgs, gbk, acc, bp, spread_t, rsend, ry, rzs, rz, gg,
    loc, zs, zr, ys, yr, ws, wr, hsn, hr, hfs, hfr, osn, orc, sms, smr,
):
    E8 = CS * YS
    TPS = XS * HS
    EXP = ZS * E8
    TOK, TOP = routes_ref.shape[1], routes_ref.shape[0]
    FFD = hid_hbm.shape[1]
    SLOTS = hid_hbm.shape[2]
    D = w_hbm.shape[2]
    DX = D // XS
    DQ = DX // NQ
    DR = DX // NR
    BLK = ZS * CAP
    HALF = ZS // 2
    away = AWAY[ZS]
    groups = slot_groups()
    GROUPS = len(groups)
    sizes = [sum(b - a for _, a, b in g) for g in groups]
    firsts = [sum(sizes[:i]) for i in range(GROUPS)]
    spans = [(min(r for r, _, _ in g), max(r for r, _, _ in g) + 1) for g in groups]

    def slot(d):
        return away.index(d + ZS if d <= -HALF else d)

    tp = lax.axis_index("tp")
    dp = lax.axis_index("dp")
    y = lax.axis_index("edp")
    x, h = lax.div(tp, HS), lax.rem(tp, HS)
    z, c = lax.div(dp, CS), lax.rem(dp, CS)
    yy = h * YS + y
    me8 = c * YS + y

    def at_y(delta, core):
        there = lax.rem(yy + delta + HS * YS, HS * YS)
        ylo = lax.rem(there, YS)
        return (x * HS + lax.div(there, YS), z * CS + core, ylo), core * YS + ylo

    def at_z(delta):
        zz = lax.rem(z + delta + ZS, ZS)
        return (tp, zz * CS + c, y), zz

    def at_x(delta):
        xx = lax.rem(x + delta, XS)
        return (xx * HS + h, dp, y), xx

    out_y = [at_y(2, 0), at_y(-2, 1), at_y(1, 0), at_y(-1, 0), at_y(1, 1), at_y(-1, 1), at_y(0, 1 - c)]
    all_y = [at_y(delta, core) for delta in (4, 3, -3, 2, -2, 1, -1) for core in range(CS)] + [at_y(0, 1 - c)]
    peers_z = [at_z(away[r]) for r in range(ZS - 1, 0, -1)]
    slots_z = list(range(ZS - 1, 0, -1))
    peers_x = [at_x(i) for i in ((2, 1, 3) if XS == 4 else range(1, XS))]
    near_x = [i for i in range(XS - 1) if XS < 4 or i > 0]

    barrier = pltpu.get_barrier_semaphore()
    hello = [d for d, _ in peers_z] + [d for d, _ in peers_x] + [d for d, _ in all_y]
    for d in hello:
        pl.semaphore_signal(barrier, inc=1, device_id=d, device_id_type=MESH)

    def col(start, size):
        return pl.ds(pl.multiple_of(start, size), size)

    def blk(start, size):
        return pl.ds(pl.multiple_of(start * size, size), size)

    get_r = pltpu.make_async_copy(routes_hbm, routes_ref, loc.at[1 + NR + 2 * NQ + NQ * GROUPS])
    get_r.start()
    get_g = pltpu.make_async_copy(gates_hbm, gates_ref, loc.at[2 + NR + 2 * NQ + NQ * GROUPS])
    get_g.start()
    get_t = [
        pltpu.make_async_copy(grad_hbm.at[:, col(x * DX + p * DR, DR)], tok.at[p, 0:TOK], loc.at[1 + p])
        for p in range(NR)
    ]
    for d in get_t:
        d.start()
    get_h = pltpu.make_async_copy(hid_hbm.at[0], hraw, loc.at[0])
    get_h.start()

    def own_w(q):
        return pltpu.make_async_copy(
            w_hbm.at[0, :, col(x * DX + q * DQ, DQ)], wv.at[q, blk(x, FFD)], loc.at[1 + NR + q])

    for q in range(NQ):
        own_w(q).start()

    get_r.wait()
    get_g.wait()
    eidx = iota((EXP, TOK), 0)
    chosen = jnp.zeros((EXP, TOK), F32)
    gate_t = jnp.zeros((EXP, TOK), F32)
    gates_f = gates_ref[...].astype(F32)
    for k in range(TOP):
        hit = routes_ref[k:k + 1, :] == eidx
        chosen = jnp.where(hit, 1.0, chosen)
        gate_t = jnp.where(hit, gates_f[k:k + 1, :], gate_t)
    earlier = (iota((TOK, TOK), 0) < iota((TOK, TOK), 1)).astype(F32).astype(BF16)
    count = jnp.dot(chosen.astype(BF16), earlier, preferred_element_type=F32)
    qt = jnp.where(chosen > 0.5, count, -1.0)
    table = jnp.zeros((EXP, TOK), F32)
    pidx = iota((EXP, TOK), 1)
    for p in range(CAP):
        value = jnp.sum(jnp.where(qt == float(p), gate_t, 0.0), axis=1, keepdims=True)
        table = jnp.where(pidx == p, value, table)
    for i in range(ZS):
        qsend[i, 0:E8] = qt[i * E8:(i + 1) * E8]
        qsend[i, E8:2 * E8] = table[i * E8:(i + 1) * E8]
    qrecv[0] = qsend[z]

    lane = (iota((1, SLOTS), 1).astype(F32) + 0.5)
    group = jnp.floor(lane * (1.0 / BLK))
    inner = (lane - group * BLK).astype(jnp.int32)
    group = group.astype(jnp.int32)
    part_z = jnp.zeros((1, SLOTS), jnp.int32)
    from_z = jnp.zeros((1, SLOTS), jnp.int32)
    place = jnp.zeros((1, SLOTS), jnp.int32)
    start = 0
    for r, a, b in [seg for g in groups for seg in g]:
        here = (inner >= start) & (inner < start + b - a)
        part_z = jnp.where(here, r, part_z)
        from_z = jnp.where(here, lax.rem(z + away[r] + ZS, ZS), from_z)
        place = jnp.where(here, inner - (start - a), place)
        start += b - a
    source = group * ZS + part_z
    native = from_z * (E8 * CAP) + group * CAP + place

    PB = 128

    def build_perm(i, carry):
        perm[pl.ds(pl.multiple_of(i * PB, PB), PB), :] = (
            (iota((PB, SLOTS), 0) + i * PB) == native).astype(F32).astype(BF16)
        return carry

    lax.fori_loop(0, SLOTS // PB, build_perm, 0)

    get_h.wait()
    hx[blk(x, FFD), :] = jnp.dot(hraw[...], perm[...], preferred_element_type=F32).astype(BF16)

    pl.semaphore_wait(barrier, len(hello))

    def remote(src, dst, send_sem, recv_sem, dev):
        return pltpu.make_async_remote_copy(
            src_ref=src, dst_ref=dst, send_sem=send_sem, recv_sem=recv_sem, device_id=dev, device_id_type=MESH)

    waited = set()

    def have(p, d):
        r = slot(d)
        if r > 0 and (p, r) not in waited:
            waited.add((p, r))
            part = tok.at[p, r * TOK:(r + 1) * TOK]
            remote(part, part, zs.at[p, 0], zr.at[p, r], peers_z[-1][0]).wait_recv()

    sent = []

    def ring(s, pieces):
        for p in pieces:
            if s > HALF:
                continue
            for right in ([True, False] if s < HALF else [p % 2 == 0]):
                d = -(s - 1) if right else s - 1
                have(p, d)
                to = slot(d - 1 if right else d + 1)
                a = slot(d)
                dev = at_z(1 if right else -1)[0]
                copy = remote(
                    tok.at[p, a * TOK:(a + 1) * TOK], tok.at[p, to * TOK:(to + 1) * TOK],
                    zs.at[p, to], zr.at[p, to], dev)
                copy.start()
                sent.append(copy)

    def q_copy(i):
        dev, there = peers_z[i]
        r = slot(-away[slots_z[i]])
        return remote(qsend.at[there], qrecv.at[r], sms.at[K_Q, i], smr.at[K_Q, r], dev)

    def send_w(q, i):
        dev, there = peers_x[i]
        return remote(
            w_hbm.at[0, :, col(there * DX + q * DQ, DQ)], wv.at[q, blk(x, FFD)], ws.at[q, i], wr.at[q, x], dev)

    def send_h(i):
        dev, there = peers_x[i]
        part = hx.at[blk(x, FFD)]
        return remote(part, part, hsn.at[i], hr.at[x], dev)

    pieces = list(range(NR))
    for p in pieces[:NR // 2]:
        get_t[p].wait()
    ring(1, pieces[:NR // 2])
    for i in range(ZS - 1):
        q_copy(i).start()
    for i in near_x:
        send_h(i).start()
    for p in pieces[NR // 2:]:
        get_t[p].wait()
    ring(1, pieces[NR // 2:])
    for i in near_x:
        send_w(0, i).start()

    def got_h(i):
        dev, there = peers_x[i]
        part = hx.at[blk(there, FFD)]
        remote(part, part, hsn.at[0], hr.at[there], dev).wait_recv()

    def pass_h(i):
        frm = peers_x[1 if i == 1 else 2][1]
        part = hx.at[pl.ds(pl.multiple_of(frm * FFD + i * (FFD // 2), FFD // 2), FFD // 2)]
        return remote(part, part, hfs.at[i], hfr.at[i], peers_x[2 if i == 1 else 1][0])

    def more_x():
        if XS == 4:
            for i in range(2):
                got_h(2 - i)
                pass_h(i).start()
            send_w(0, 0).start()
        for q in range(1, NQ):
            for i in range(XS - 1):
                send_w(q, i).start()

    heard = set()

    def build_sel(g):
        if g >= GROUPS:
            return
        lo, hi = spans[g]
        n = sizes[g]
        at = iota((n, TOK), 0)
        for r in range(lo, hi):
            if r > 0 and r not in heard:
                heard.add(r)
                remote(qsend.at[0], qrecv.at[r], sms.at[K_Q, 0], smr.at[K_Q, r], peers_z[0][0]).wait_recv()
            want = jnp.full((n, TOK), -7, jnp.int32)
            start = 0
            for rr, a, b in groups[g]:
                if rr == r:
                    want = jnp.where((at >= start) & (at < start + b - a), at - (start - a), want)
                start += b - a
            want = want.astype(F32)
            tile = qrecv[r, 0:E8]
            for e in range(E8):
                sel[g][e * n:(e + 1) * n, (r - lo) * TOK:(r - lo + 1) * TOK] = (
                    want == tile[e:e + 1, :]).astype(F32).astype(BF16)

    def part_of(expert, g):
        return pl.ds(pl.multiple_of(expert * BLK + firsts[g], 16), sizes[g])

    def send_y(q, g, i):
        dev, there = out_y[i]
        return remote(
            sendb.at[q, there, firsts[g]:firsts[g] + sizes[g]], rows.at[q, part_of(me8, g)],
            ys.at[q, g, i], yr.at[q, g, me8], dev)

    def own_rows(q, g):
        return pltpu.make_async_copy(
            sendb.at[q, me8, firsts[g]:firsts[g] + sizes[g]], rows.at[q, part_of(me8, g)],
            loc.at[1 + NR + NQ + q * GROUPS + g])

    def select(q, g):
        if g >= GROUPS:
            return
        lo, hi = spans[g]
        n = sizes[g]
        for p in range(q * NR // NQ, (q + 1) * NR // NQ):
            for r in range(lo, hi):
                have(p, away[r])
            got = jnp.dot(sel[g][...], tok[p, lo * TOK:hi * TOK, :], preferred_element_type=F32).astype(BF16)
            at = (p - q * NR // NQ) * DR
            for e in range(E8):
                sendb[q, e, firsts[g]:firsts[g] + n, at:at + DR] = got[e * n:(e + 1) * n]
        for i in range(E8 - 1):
            send_y(q, g, i).start()
        own_rows(q, g).start()

    def gy_copy(i):
        dev, there = out_y[i]
        return remote(gsy.at[there], gtab.at[me8], sms.at[K_GY, i], smr.at[K_GY, me8], dev)

    def gates_on():
        for r in range(1, ZS):
            if r not in heard:
                heard.add(r)
                remote(qsend.at[0], qrecv.at[r], sms.at[K_Q, 0], smr.at[K_Q, r], peers_z[0][0]).wait_recv()
        for r in range(ZS):
            for e in range(E8):
                gsy[e, r:r + 1, :] = qrecv[r, E8 + e:E8 + e + 1, :]
        gtab[me8] = gsy[me8]
        for i in range(E8 - 1):
            gy_copy(i).start()

    first, second = pieces[:NR // 2], pieces[NR // 2:]
    ring(2, first)
    build_sel(0)
    select(0, 0)
    ring(2, second)
    select(1, 0)
    ring(3, first)
    build_sel(1)
    select(0, 1)
    ring(3, second)
    select(1, 1)
    build_sel(2)
    gates_on()
    ring(4, first)
    select(0, 2)
    more_x()
    build_sel(3)
    ring(4, second)
    select(1, 2)
    select(0, 3)
    select(1, 3)

    if XS == 4:
        for i in range(2):
            part = hx.at[pl.ds(pl.multiple_of(peers_x[0][1] * FFD + i * (FFD // 2), FFD // 2), FFD // 2)]
            remote(part, part, hfs.at[i], hfr.at[i], peers_x[1][0]).wait_recv()
    else:
        for i in near_x:
            got_h(i)
    for j in range(SLOTS // PB):
        hxt[j * PB:(j + 1) * PB, :] = hx[:, j * PB:(j + 1) * PB].T
    for dev, there in out_y:
        remote(gsy.at[there], gtab.at[there], sms.at[K_GY, 0], smr.at[K_GY, there], dev).wait_recv()
    spread = (iota((TOK, SLOTS), 0) == place).astype(F32)
    for j in range(SLOTS // PB):
        spread_t[j * PB:(j + 1) * PB, :] = spread[:, j * PB:(j + 1) * PB].T
    spread = spread.astype(BF16)
    gate_all = jnp.dot(gtab[...].reshape(EXP, TOK).astype(BF16), spread, preferred_element_type=F32)
    pick = iota((EXP, SLOTS), 0) == source
    gate_lane = jnp.sum(jnp.where(pick, gate_all, 0.0), axis=0, keepdims=True)
    for i in range(XS):
        part = slice(i * FFD, (i + 1) * FFD)
        hs[part, :] = (hx[part, :].astype(F32) * gate_lane).astype(BF16)

    def wait_w(q):
        own_w(q).wait()
        for dev, there in peers_x:
            remote(
                w_hbm.at[0, :, col(x * DX + q * DQ, DQ)], wv.at[q, blk(there, FFD)],
                ws.at[q, 0], wr.at[q, there], dev).wait_recv()

    def wait_rows(q):
        for g in range(GROUPS):
            own_rows(q, g).wait()
            for dev, there in out_y:
                remote(
                    sendb.at[q, there, firsts[g]:firsts[g] + sizes[g]], rows.at[q, part_of(there, g)],
                    ys.at[q, g, 0], yr.at[q, g, there], dev).wait_recv()

    def send_o(q, i):
        dev, there = peers_x[i]
        return remote(
            wgs.at[q, blk(there, FFD)], out_hbm.at[0, :, col(x * DX + q * DQ, DQ)],
            osn.at[q, i], orc.at[q, x], dev)

    def own_o(q):
        return pltpu.make_async_copy(
            wgs.at[q, blk(x, FFD)], out_hbm.at[0, :, col(x * DX + q * DQ, DQ)],
            loc.at[1 + NR + NQ + NQ * GROUPS + q])

    def products(q, squares):
        wait_rows(q)
        for i in range(XS):
            there = x if i == XS - 1 else peers_x[i][1]
            wg = jnp.dot(hs[blk(there, FFD), :], rows[q], preferred_element_type=F32)
            wgs[q, blk(there, FFD), :] = wg.astype(BF16)
            if i == XS - 1:
                own_o(q).start()
            else:
                send_o(q, i).start()
            squares = squares + jnp.sum((wg * wg).reshape(FFD // 8, 8, DQ), axis=0)
        return squares

    def turned(q):
        wait_w(q)

        def body(j, carry):
            at = pl.ds(pl.multiple_of(j * PB, PB), PB)
            gbk[q, at, :] = jnp.dot(hxt[at, :], wv[q], preferred_element_type=F32)
            return carry

        lax.fori_loop(0, SLOTS // PB, body, 0)

    def fold(q, at):
        both = gbk[q, at, :] * rows[q, at, :].astype(F32)
        total = both[:, 0:128]
        for i in range(1, DQ // 128):
            total = total + both[:, i * 128:(i + 1) * 128]
        return total

    turned(0)
    squares = products(0, jnp.zeros((8, DQ), F32))

    def fold_first(j, carry):
        at = pl.ds(pl.multiple_of(j * PB, PB), PB)
        acc[at, :] = fold(0, at)
        return carry

    lax.fori_loop(0, SLOTS // PB, fold_first, 0)
    for q in range(1, NQ):
        squares = products(q, squares)
        turned(q)

    def fold_last(j, carry):
        at = pl.ds(pl.multiple_of(j * PB, PB), PB)
        total = acc[at, :]
        for q in range(1, NQ):
            total = total + fold(q, at)
        bp[at, :] = spread_t[at, :] * jnp.sum(total, axis=1, keepdims=True)
        return carry

    lax.fori_loop(0, SLOTS // PB, fold_last, 0)
    tile = squares[:, 0:128]
    for i in range(1, DQ // 128):
        tile = tile + squares[:, i * 128:(i + 1) * 128]

    back = jnp.dot(pick.astype(F32), bp[...], preferred_element_type=F32, precision=lax.Precision.HIGHEST)
    for e in range(E8):
        rsend[e, 0:ZS] = back[e * ZS:(e + 1) * ZS]
        rsend[e, ZS:ZS + 8] = tile

    def ry_copy(i):
        dev, there = all_y[i]
        return remote(rsend.at[there], ry.at[h * E8 + me8], sms.at[K_RY, i], smr.at[K_RY, h * E8 + me8], dev)

    def rz_copy(i):
        dev, there = peers_z[i]
        return remote(rzs.at[slots_z[i]], rz.at[z], sms.at[K_RZ, i], smr.at[K_RZ, z], dev)

    def gg_copy(i):
        dev, there = peers_x[i]
        return remote(gg.at[x], gg.at[x], sms.at[K_GG, i], smr.at[K_GG, x], dev)

    for i in range(len(all_y)):
        ry_copy(i).start()
    ry[h * E8 + me8] = rsend[me8]

    for q in range(NQ):
        for i in range(XS - 1):
            send_w(q, i).wait_send()
        for g in range(GROUPS):
            for i in range(E8 - 1):
                send_y(q, g, i).wait_send()
    for i in near_x:
        send_h(i).wait_send()
    if XS == 4:
        for i in range(2):
            pass_h(i).wait_send()
    for copy in sent:
        copy.wait_send()
    for i in range(ZS - 1):
        q_copy(i).wait_send()
    for i in range(E8 - 1):
        gy_copy(i).wait_send()

    for dev, there in all_y:
        there = lax.rem(dev[0], HS) * E8 + there
        remote(rsend.at[0], ry.at[there], sms.at[K_RY, 0], smr.at[K_RY, there], dev).wait_recv()

    tile = jnp.sum(ry[:, ZS:ZS + 8, :], axis=0)
    for r in range(ZS):
        for e in range(E8):
            rzs[r, e:e + 1, :] = ry[e, r:r + 1, :] + ry[E8 + e, r:r + 1, :]
        rzs[r, E8:E8 + 8] = tile
    for i in range(ZS - 1):
        rz_copy(i).start()
    rz[z] = rzs[0]
    for dev, there in peers_z:
        remote(rzs.at[0], rz.at[there], sms.at[K_RZ, 0], smr.at[K_RZ, there], dev).wait_recv()

    by_expert = rz[:, 0:E8, :].reshape(EXP, TOK)
    qt2 = qsend[:, 0:E8, :].reshape(EXP, TOK)
    value = jnp.zeros((EXP, TOK), F32)
    for p in range(CAP):
        value = jnp.where(qt2 == float(p), by_expert[:, p:p + 1], value)
    for k in range(TOP):
        gg[x, k:k + 1, :] = jnp.sum(
            jnp.where(routes_ref[k:k + 1, :] == eidx, value, 0.0), axis=0, keepdims=True)
    gg[x, 8:16, :] = jnp.sum(rz[:, E8:E8 + 8, :], axis=0)
    for i in range(XS - 1):
        gg_copy(i).start()
    for dev, there in peers_x:
        remote(gg.at[x], gg.at[there], sms.at[K_GG, 0], smr.at[K_GG, there], dev).wait_recv()

    total = jnp.sum(gg[:, 8:16, :], axis=0)
    total = jnp.sum(jnp.sum(total, axis=1, keepdims=True), axis=0, keepdims=True)
    limit = clip_ratio * math.sqrt(FFD * D * TPS * EXP)
    factor = jnp.minimum(1.0, limit / (jnp.sqrt(total) + 1e-06))
    factor_ref[...] = factor
    gg_ref[...] = jnp.sum(gg[:, 0:TOP, :], axis=0)

    for q in range(NQ):
        own_o(q).wait()
        for i in range(XS - 1):
            dev, there = peers_x[i]
            remote(
                wgs.at[q, blk(there, FFD)], out_hbm.at[0, :, col(there * DX + q * DQ, DQ)],
                osn.at[q, 0], orc.at[q, there], dev).wait_recv()
            send_o(q, i).wait_send()
    for i in range(ZS - 1):
        rz_copy(i).wait_send()
    for i in range(len(all_y)):
        ry_copy(i).wait_send()
    for i in range(XS - 1):
        gg_copy(i).wait_send()


def per_device(grad_out, routes, gates, hidden, w_down):
    E8, TPS = CS * YS, XS * HS
    TOK, D = grad_out.shape
    TOP = routes.shape[1]
    FFD, SLOTS = hidden.shape[1], hidden.shape[2]
    DX = D // XS
    DQ, DR = DX // NQ, DX // NR
    groups = slot_groups()
    GROUPS = len(groups)
    sizes = [sum(b - a for _, a, b in g) for g in groups]
    reach = [max(r for r, _, _ in g) + 1 - min(r for r, _, _ in g) for g in groups]
    vm = pltpu.VMEM
    dma = pltpu.SemaphoreType.DMA
    most = max(TPS, HS * E8, ZS)
    any_space = pl.BlockSpec(memory_space=pl.ANY)
    in_hbm = pl.BlockSpec(memory_space=pltpu.HBM)
    in_vmem = pl.BlockSpec(memory_space=pltpu.VMEM)
    part, factor, gate_grad = pl.pallas_call(
        kernel,
        out_shape=(
            jax.ShapeDtypeStruct((1, FFD, D), BF16),
            jax.ShapeDtypeStruct((1, 1), F32),
            jax.ShapeDtypeStruct((TOP, TOK), F32),
        ),
        in_specs=[in_hbm] * 5,
        out_specs=(any_space, in_vmem, in_vmem),
        scratch_shapes=[
            vm((TOP, TOK), jnp.int32),
            vm((TOP, TOK), BF16),
            vm((NR, ZS * TOK, DR), BF16),
            [vm((E8 * n, k * TOK), BF16) for n, k in zip(sizes, reach)],
            vm((NQ, E8, ZS * CAP, DQ), BF16),
            vm((NQ, SLOTS, DQ), BF16),
            vm((ZS, 2 * E8, TOK), F32),
            vm((ZS, 2 * E8, TOK), F32),
            vm((E8, ZS, TOK), F32),
            vm((E8, ZS, TOK), F32),
            vm((FFD, SLOTS), BF16),
            vm((SLOTS, SLOTS), BF16),
            vm((XS * FFD, SLOTS), BF16),
            vm((XS * FFD, SLOTS), BF16),
            vm((SLOTS, XS * FFD), BF16),
            vm((NQ, XS * FFD, DQ), BF16),
            vm((NQ, XS * FFD, DQ), BF16),
            vm((NQ, SLOTS, DQ), F32),
            vm((SLOTS, 128), F32),
            vm((SLOTS, TOK), F32),
            vm((SLOTS, TOK), F32),
            vm((E8, ZS + 8, TOK), F32),
            vm((HS * E8, ZS + 8, TOK), F32),
            vm((ZS, E8 + 8, TOK), F32),
            vm((ZS, E8 + 8, TOK), F32),
            vm((XS, 16, TOK), F32),
            dma((3 + NR + 2 * NQ + NQ * GROUPS,)),
            dma((NR, ZS)),
            dma((NR, ZS)),
            dma((NQ, GROUPS, E8)),
            dma((NQ, GROUPS, E8)),
            dma((NQ, XS)),
            dma((NQ, XS)),
            dma((XS,)),
            dma((XS,)),
            dma((2,)),
            dma((2,)),
            dma((NQ, XS)),
            dma((NQ, XS)),
            dma((5, most)),
            dma((5, most)),
        ],
        compiler_params=pltpu.CompilerParams(
            collective_id=0, has_side_effects=True, vmem_limit_bytes=40 * 1024 * 1024),
        cost_estimate=pl.CostEstimate(
            flops=2 * 2 * SLOTS * FFD * D, bytes_accessed=8 * 1024 * 1024, transcendentals=0),
        name="moe_down_backward",
    )(*[pltpu.with_memory_space_constraint(a, pltpu.HBM) for a in (routes.T, gates.T, grad_out, hidden, w_down)])
    down_grad = (part.astype(F32) * factor[0, 0]).astype(BF16)
    return (down_grad, gate_grad.T)


def solution(mesh):
    in_specs = (
        P(("dp", "edp"), None),
        P(("dp", "edp"), None),
        P(("dp", "edp"), None),
        P(("dp", "edp"), "tp", None),
        P(("dp", "edp"), "tp", None),
    )
    out_specs = (P(("dp", "edp"), "tp", None), P(("dp", "edp"), None))
    return jax.shard_map(
        per_device, mesh=mesh, in_specs=in_specs, out_specs=out_specs, check_vma=False
    )
```

```python
import functools
import math

import jax
import jax.numpy as jnp
from jax import lax
from jax.experimental import pallas as pl
from jax.experimental.pallas import tpu as pltpu
from jax.sharding import PartitionSpec as P

clip_ratio = 0.25

XS, HS, ZS, CS, YS = 4, 2, 8, 2, 4
NQ = 2
NR = 4
CAP = 20
AWAY = {8: [0, 1, -1, -2, 2, 3, -3, 4], 4: [0, 1, -1, 2], 2: [0, 1]}
MESH = pl.DeviceIdType.MESH
F32, BF16 = jnp.float32, jnp.bfloat16


def slot_groups():
    whole = CAP // 16 * 16
    rest = lambda parts: [(r, whole, CAP) for r in parts if CAP > whole]
    head = lambda parts: [(r, 0, whole) for r in parts]
    if ZS == 8:
        return [
            head([0]), head([1, 2]), head([3, 4]) + rest([0, 1, 2, 3]), head([5, 6]), head([7]) + rest([4, 5, 6, 7])]
    if ZS == 4:
        return [head([0]), head([1, 2]), head([3]) + rest([0, 1, 2, 3])]
    return [head([0]), head([1]) + rest([0, 1])]


def messages(q):
    count = len(slot_groups())
    if q == 0:
        return [(g, g) for g in range(count)]
    return [(0, 1), (2, 2), (3, 4)] if count == 5 else [(0, 1), (2, 2)] if count == 3 else [(0, 1)]


K_Q, K_GY, K_RY, K_RZ, K_GG = range(5)


def iota(shape, dim):
    return lax.broadcasted_iota(jnp.int32, shape, dim)


def kernel(
    routes_hbm, gates_hbm, grad_hbm, hid_hbm, w_hbm,
    out_hbm, factor_ref, gg_ref,
    routes_ref, gates_ref, tok, sel, sendb, rows, qsend, qrecv, gsy, gtab,
    hraw, perm, hx, hs, hxt, wv, wgs, gbk, acc, bp, spread_t, rsend, ry, rzs, rz, gg,
    loc, zs, zr, ys, yr, ws, wr, hsn, hr, hfs, hfr, osn, orc, sms, smr,
):
    E8 = CS * YS
    TPS = XS * HS
    EXP = ZS * E8
    TOK, TOP = routes_ref.shape[1], routes_ref.shape[0]
    FFD = hid_hbm.shape[1]
    SLOTS = hid_hbm.shape[2]
    D = w_hbm.shape[2]
    DX = D // XS
    DQ = DX // NQ
    DR = DX // NR
    BLK = ZS * CAP
    HALF = ZS // 2
    away = AWAY[ZS]
    groups = slot_groups()
    GROUPS = len(groups)
    sizes = [sum(b - a for _, a, b in g) for g in groups]
    firsts = [sum(sizes[:i]) for i in range(GROUPS)]
    spans = [(min(r for r, _, _ in g), max(r for r, _, _ in g) + 1) for g in groups]

    def slot(d):
        return away.index(d + ZS if d <= -HALF else d)

    tp = lax.axis_index("tp")
    dp = lax.axis_index("dp")
    y = lax.axis_index("edp")
    x, h = lax.div(tp, HS), lax.rem(tp, HS)
    z, c = lax.div(dp, CS), lax.rem(dp, CS)
    yy = h * YS + y
    me8 = c * YS + y

    def at_y(delta, core):
        there = lax.rem(yy + delta + HS * YS, HS * YS)
        ylo = lax.rem(there, YS)
        return (x * HS + lax.div(there, YS), z * CS + core, ylo), core * YS + ylo

    def at_z(delta):
        zz = lax.rem(z + delta + ZS, ZS)
        return (tp, zz * CS + c, y), zz

    def at_x(delta):
        xx = lax.rem(x + delta, XS)
        return (xx * HS + h, dp, y), xx

    out_y = [at_y(2, 0), at_y(-2, 1), at_y(1, 0), at_y(-1, 0), at_y(1, 1), at_y(-1, 1), at_y(0, 1 - c)]
    all_y = [at_y(delta, core) for delta in (4, 3, -3, 2, -2, 1, -1) for core in range(CS)] + [at_y(0, 1 - c)]
    peers_z = [at_z(away[r]) for r in range(ZS - 1, 0, -1)]
    slots_z = list(range(ZS - 1, 0, -1))
    peers_x = [at_x(i) for i in ((2, 1, 3) if XS == 4 else range(1, XS))]
    near_x = [i for i in range(XS - 1) if XS < 4 or i > 0]

    barrier = pltpu.get_barrier_semaphore()
    hello = [d for d, _ in peers_z] + [d for d, _ in peers_x] + [d for d, _ in all_y]
    for d in hello:
        pl.semaphore_signal(barrier, inc=1, device_id=d, device_id_type=MESH)

    def col(start, size):
        return pl.ds(pl.multiple_of(start, size), size)

    def blk(start, size):
        return pl.ds(pl.multiple_of(start * size, size), size)

    get_r = pltpu.make_async_copy(routes_hbm, routes_ref, loc.at[1 + NR + 2 * NQ + NQ * GROUPS])
    get_r.start()
    get_g = pltpu.make_async_copy(gates_hbm, gates_ref, loc.at[2 + NR + 2 * NQ + NQ * GROUPS])
    get_g.start()
    get_t = [
        pltpu.make_async_copy(grad_hbm.at[:, col(x * DX + p * DR, DR)], tok.at[p, 0:TOK], loc.at[1 + p])
        for p in range(NR)
    ]
    for d in get_t:
        d.start()
    get_h = pltpu.make_async_copy(hid_hbm.at[0], hraw, loc.at[0])
    get_h.start()

    def own_w(q):
        return pltpu.make_async_copy(
            w_hbm.at[0, :, col(x * DX + q * DQ, DQ)], wv.at[q, blk(x, FFD)], loc.at[1 + NR + q])

    for q in range(NQ):
        own_w(q).start()

    get_r.wait()
    get_g.wait()
    eidx = iota((EXP, TOK), 0)
    chosen = jnp.zeros((EXP, TOK), F32)
    gate_t = jnp.zeros((EXP, TOK), F32)
    gates_f = gates_ref[...].astype(F32)
    for k in range(TOP):
        hit = routes_ref[k:k + 1, :] == eidx
        chosen = jnp.where(hit, 1.0, chosen)
        gate_t = jnp.where(hit, gates_f[k:k + 1, :], gate_t)
    earlier = (iota((TOK, TOK), 0) < iota((TOK, TOK), 1)).astype(F32).astype(BF16)
    count = jnp.dot(chosen.astype(BF16), earlier, preferred_element_type=F32)
    qt = jnp.where(chosen > 0.5, count, -1.0)
    table = jnp.zeros((EXP, TOK), F32)
    pidx = iota((EXP, TOK), 1)
    for p in range(CAP):
        value = jnp.sum(jnp.where(qt == float(p), gate_t, 0.0), axis=1, keepdims=True)
        table = jnp.where(pidx == p, value, table)
    for i in range(ZS):
        qsend[i, 0:E8] = qt[i * E8:(i + 1) * E8]
        qsend[i, E8:2 * E8] = table[i * E8:(i + 1) * E8]
    qrecv[0] = qsend[z]

    lane = (iota((1, SLOTS), 1).astype(F32) + 0.5)
    group = jnp.floor(lane * (1.0 / BLK))
    inner = (lane - group * BLK).astype(jnp.int32)
    group = group.astype(jnp.int32)
    part_z = jnp.zeros((1, SLOTS), jnp.int32)
    from_z = jnp.zeros((1, SLOTS), jnp.int32)
    place = jnp.zeros((1, SLOTS), jnp.int32)
    start = 0
    for r, a, b in [seg for g in groups for seg in g]:
        here = (inner >= start) & (inner < start + b - a)
        part_z = jnp.where(here, r, part_z)
        from_z = jnp.where(here, lax.rem(z + away[r] + ZS, ZS), from_z)
        place = jnp.where(here, inner - (start - a), place)
        start += b - a
    source = group * ZS + part_z
    native = from_z * (E8 * CAP) + group * CAP + place

    PB = 128

    def build_perm(i, carry):
        perm[pl.ds(pl.multiple_of(i * PB, PB), PB), :] = (
            (iota((PB, SLOTS), 0) + i * PB) == native).astype(F32).astype(BF16)
        return carry

    lax.fori_loop(0, SLOTS // PB, build_perm, 0)

    get_h.wait()
    hx[blk(x, FFD), :] = jnp.dot(hraw[...], perm[...], preferred_element_type=F32).astype(BF16)

    pl.semaphore_wait(barrier, len(hello))

    def remote(src, dst, send_sem, recv_sem, dev):
        return pltpu.make_async_remote_copy(
            src_ref=src, dst_ref=dst, send_sem=send_sem, recv_sem=recv_sem, device_id=dev, device_id_type=MESH)

    waited = set()

    def have(p, d):
        r = slot(d)
        if r > 0 and (p, r) not in waited:
            waited.add((p, r))
            part = tok.at[p, r * TOK:(r + 1) * TOK]
            remote(part, part, zs.at[p, 0], zr.at[p, r], peers_z[-1][0]).wait_recv()

    sent = []

    def ring(s, pieces):
        for p in pieces:
            if s > HALF:
                continue
            for right in ([True, False] if s < HALF else [p % 2 == 0]):
                d = -(s - 1) if right else s - 1
                have(p, d)
                to = slot(d - 1 if right else d + 1)
                a = slot(d)
                dev = at_z(1 if right else -1)[0]
                copy = remote(
                    tok.at[p, a * TOK:(a + 1) * TOK], tok.at[p, to * TOK:(to + 1) * TOK],
                    zs.at[p, to], zr.at[p, to], dev)
                copy.start()
                sent.append(copy)

    def q_copy(i):
        dev, there = peers_z[i]
        r = slot(-away[slots_z[i]])
        return remote(qsend.at[there], qrecv.at[r], sms.at[K_Q, i], smr.at[K_Q, r], dev)

    def send_w(q, i):
        dev, there = peers_x[i]
        return remote(
            w_hbm.at[0, :, col(there * DX + q * DQ, DQ)], wv.at[q, blk(x, FFD)], ws.at[q, i], wr.at[q, x], dev)

    def send_h(i):
        dev, there = peers_x[i]
        part = hx.at[blk(x, FFD)]
        return remote(part, part, hsn.at[i], hr.at[x], dev)

    pieces = list(range(NR))
    for p in pieces[:NR // 2]:
        get_t[p].wait()
    ring(1, pieces[:NR // 2])
    for i in range(ZS - 1):
        q_copy(i).start()
    for i in near_x:
        send_h(i).start()
    for p in pieces[NR // 2:]:
        get_t[p].wait()
    ring(1, pieces[NR // 2:])
    for q in range(NQ):
        for i in near_x:
            send_w(q, i).start()

    def got_h(i):
        dev, there = peers_x[i]
        part = hx.at[blk(there, FFD)]
        remote(part, part, hsn.at[0], hr.at[there], dev).wait_recv()

    def pass_h(i):
        frm = peers_x[1 if i == 1 else 2][1]
        part = hx.at[pl.ds(pl.multiple_of(frm * FFD + i * (FFD // 2), FFD // 2), FFD // 2)]
        return remote(part, part, hfs.at[i], hfr.at[i], peers_x[2 if i == 1 else 1][0])

    def more_x():
        if XS == 4:
            for i in range(2):
                got_h(2 - i)
                pass_h(i).start()
            for q in range(NQ):
                send_w(q, 0).start()

    heard = set()

    def build_sel(g):
        if g >= GROUPS:
            return
        lo, hi = spans[g]
        n = sizes[g]
        at = iota((n, TOK), 0)
        for r in range(lo, hi):
            if r > 0 and r not in heard:
                heard.add(r)
                remote(qsend.at[0], qrecv.at[r], sms.at[K_Q, 0], smr.at[K_Q, r], peers_z[0][0]).wait_recv()
            want = jnp.full((n, TOK), -7, jnp.int32)
            start = 0
            for rr, a, b in groups[g]:
                if rr == r:
                    want = jnp.where((at >= start) & (at < start + b - a), at - (start - a), want)
                start += b - a
            want = want.astype(F32)
            tile = qrecv[r, 0:E8]
            for e in range(E8):
                sel[g][e * n:(e + 1) * n, (r - lo) * TOK:(r - lo + 1) * TOK] = (
                    want == tile[e:e + 1, :]).astype(F32).astype(BF16)

    def span_of(m):
        return firsts[m[0]], firsts[m[1]] + sizes[m[1]]

    def part_of(expert, m):
        lo, hi = span_of(m)
        return pl.ds(pl.multiple_of(expert * BLK + lo, 16), hi - lo)

    def send_y(q, m, i):
        dev, there = out_y[i]
        lo, hi = span_of(m)
        return remote(
            sendb.at[q, there, lo:hi], rows.at[q, part_of(me8, m)], ys.at[q, m[1], i], yr.at[q, m[1], me8], dev)

    def own_rows(q, m):
        lo, hi = span_of(m)
        return pltpu.make_async_copy(
            sendb.at[q, me8, lo:hi], rows.at[q, part_of(me8, m)], loc.at[1 + NR + NQ + q * GROUPS + m[1]])

    def select(q, g):
        if g >= GROUPS:
            return
        lo, hi = spans[g]
        n = sizes[g]
        for p in range(q * NR // NQ, (q + 1) * NR // NQ):
            for r in range(lo, hi):
                have(p, away[r])
            got = jnp.dot(sel[g][...], tok[p, lo * TOK:hi * TOK, :], preferred_element_type=F32).astype(BF16)
            at = (p - q * NR // NQ) * DR
            for e in range(E8):
                sendb[q, e, firsts[g]:firsts[g] + n, at:at + DR] = got[e * n:(e + 1) * n]
        for m in messages(q):
            if m[1] == g:
                for i in range(E8 - 1):
                    send_y(q, m, i).start()
                own_rows(q, m).start()

    def gy_copy(i):
        dev, there = out_y[i]
        return remote(gsy.at[there], gtab.at[me8], sms.at[K_GY, i], smr.at[K_GY, me8], dev)

    def gates_on():
        for r in range(1, ZS):
            if r not in heard:
                heard.add(r)
                remote(qsend.at[0], qrecv.at[r], sms.at[K_Q, 0], smr.at[K_Q, r], peers_z[0][0]).wait_recv()
        for r in range(ZS):
            for e in range(E8):
                gsy[e, r:r + 1, :] = qrecv[r, E8 + e:E8 + e + 1, :]
        gtab[me8] = gsy[me8]
        for i in range(E8 - 1):
            gy_copy(i).start()

    first, second = pieces[:NR // 2], pieces[NR // 2:]
    build_sel(0)
    select(0, 0)
    select(1, 0)
    ring(2, first)
    build_sel(1)
    select(0, 1)
    ring(2, second)
    select(1, 1)
    ring(3, first)
    build_sel(2)
    select(0, 2)
    ring(3, second)
    select(1, 2)
    gates_on()
    build_sel(3)
    ring(4, first)
    select(0, 3)
    more_x()
    build_sel(4)
    ring(4, second)
    select(1, 3)
    select(0, 4)
    select(1, 4)

    if XS == 4:
        for i in range(2):
            part = hx.at[pl.ds(pl.multiple_of(peers_x[0][1] * FFD + i * (FFD // 2), FFD // 2), FFD // 2)]
            remote(part, part, hfs.at[i], hfr.at[i], peers_x[1][0]).wait_recv()
    else:
        for i in near_x:
            got_h(i)
    for j in range(SLOTS // PB):
        hxt[j * PB:(j + 1) * PB, :] = hx[:, j * PB:(j + 1) * PB].T
    for dev, there in out_y:
        remote(gsy.at[there], gtab.at[there], sms.at[K_GY, 0], smr.at[K_GY, there], dev).wait_recv()
    spread = (iota((TOK, SLOTS), 0) == place).astype(F32)
    for j in range(SLOTS // PB):
        spread_t[j * PB:(j + 1) * PB, :] = spread[:, j * PB:(j + 1) * PB].T
    spread = spread.astype(BF16)
    gate_all = jnp.dot(gtab[...].reshape(EXP, TOK).astype(BF16), spread, preferred_element_type=F32)
    pick = iota((EXP, SLOTS), 0) == source
    gate_lane = jnp.sum(jnp.where(pick, gate_all, 0.0), axis=0, keepdims=True)
    for i in range(XS):
        part = slice(i * FFD, (i + 1) * FFD)
        hs[part, :] = (hx[part, :].astype(F32) * gate_lane).astype(BF16)

    def wait_w(q):
        own_w(q).wait()
        for dev, there in peers_x:
            remote(
                w_hbm.at[0, :, col(x * DX + q * DQ, DQ)], wv.at[q, blk(there, FFD)],
                ws.at[q, 0], wr.at[q, there], dev).wait_recv()

    def wait_rows(q):
        for m in messages(q):
            own_rows(q, m).wait()
            lo, hi = span_of(m)
            for dev, there in out_y:
                remote(
                    sendb.at[q, there, lo:hi], rows.at[q, part_of(there, m)],
                    ys.at[q, m[1], 0], yr.at[q, m[1], there], dev).wait_recv()

    def send_o(q, i):
        dev, there = peers_x[i]
        return remote(
            wgs.at[q, blk(there, FFD)], out_hbm.at[0, :, col(x * DX + q * DQ, DQ)],
            osn.at[q, i], orc.at[q, x], dev)

    def own_o(q):
        return pltpu.make_async_copy(
            wgs.at[q, blk(x, FFD)], out_hbm.at[0, :, col(x * DX + q * DQ, DQ)],
            loc.at[1 + NR + NQ + NQ * GROUPS + q])

    def products(q, squares):
        wait_rows(q)
        for i in range(XS):
            there = x if i == XS - 1 else peers_x[i][1]
            wg = jnp.dot(hs[blk(there, FFD), :], rows[q], preferred_element_type=F32)
            wgs[q, blk(there, FFD), :] = wg.astype(BF16)
            if i == XS - 1:
                own_o(q).start()
            else:
                send_o(q, i).start()
            squares = squares + jnp.sum((wg * wg).reshape(FFD // 8, 8, DQ), axis=0)
        return squares

    def turned(q):
        wait_w(q)

        def body(j, carry):
            at = pl.ds(pl.multiple_of(j * PB, PB), PB)
            gbk[q, at, :] = jnp.dot(hxt[at, :], wv[q], preferred_element_type=F32)
            return carry

        lax.fori_loop(0, SLOTS // PB, body, 0)

    def fold(q, at):
        both = gbk[q, at, :] * rows[q, at, :].astype(F32)
        total = both[:, 0:128]
        for i in range(1, DQ // 128):
            total = total + both[:, i * 128:(i + 1) * 128]
        return total

    turned(0)
    squares = products(0, jnp.zeros((8, DQ), F32))

    def fold_first(j, carry):
        at = pl.ds(pl.multiple_of(j * PB, PB), PB)
        acc[at, :] = fold(0, at)
        return carry

    lax.fori_loop(0, SLOTS // PB, fold_first, 0)
    for q in range(1, NQ):
        squares = products(q, squares)
    for q in range(1, NQ):
        turned(q)

    def fold_last(j, carry):
        at = pl.ds(pl.multiple_of(j * PB, PB), PB)
        total = acc[at, :]
        for q in range(1, NQ):
            total = total + fold(q, at)
        bp[at, :] = spread_t[at, :] * jnp.sum(total, axis=1, keepdims=True)
        return carry

    lax.fori_loop(0, SLOTS // PB, fold_last, 0)
    tile = squares[:, 0:128]
    for i in range(1, DQ // 128):
        tile = tile + squares[:, i * 128:(i + 1) * 128]

    back = jnp.dot(pick.astype(F32), bp[...], preferred_element_type=F32, precision=lax.Precision.HIGHEST)
    for e in range(E8):
        rsend[e, 0:ZS] = back[e * ZS:(e + 1) * ZS]
        rsend[e, ZS:ZS + 8] = tile

    def ry_copy(i):
        dev, there = all_y[i]
        return remote(rsend.at[there], ry.at[h * E8 + me8], sms.at[K_RY, i], smr.at[K_RY, h * E8 + me8], dev)

    def rz_copy(i):
        dev, there = peers_z[i]
        return remote(rzs.at[slots_z[i]], rz.at[z], sms.at[K_RZ, i], smr.at[K_RZ, z], dev)

    def gg_copy(i):
        dev, there = peers_x[i]
        return remote(gg.at[x], gg.at[x], sms.at[K_GG, i], smr.at[K_GG, x], dev)

    for i in range(len(all_y)):
        ry_copy(i).start()
    ry[h * E8 + me8] = rsend[me8]

    for q in range(NQ):
        for i in range(XS - 1):
            send_w(q, i).wait_send()
        for m in messages(q):
            for i in range(E8 - 1):
                send_y(q, m, i).wait_send()
    for i in near_x:
        send_h(i).wait_send()
    if XS == 4:
        for i in range(2):
            pass_h(i).wait_send()
    for copy in sent:
        copy.wait_send()
    for i in range(ZS - 1):
        q_copy(i).wait_send()
    for i in range(E8 - 1):
        gy_copy(i).wait_send()

    for dev, there in all_y:
        there = lax.rem(dev[0], HS) * E8 + there
        remote(rsend.at[0], ry.at[there], sms.at[K_RY, 0], smr.at[K_RY, there], dev).wait_recv()

    tile = jnp.sum(ry[:, ZS:ZS + 8, :], axis=0)
    for r in range(ZS):
        for e in range(E8):
            rzs[r, e:e + 1, :] = ry[e, r:r + 1, :] + ry[E8 + e, r:r + 1, :]
        rzs[r, E8:E8 + 8] = tile
    for i in range(ZS - 1):
        rz_copy(i).start()
    rz[z] = rzs[0]
    for dev, there in peers_z:
        remote(rzs.at[0], rz.at[there], sms.at[K_RZ, 0], smr.at[K_RZ, there], dev).wait_recv()

    by_expert = rz[:, 0:E8, :].reshape(EXP, TOK)
    qt2 = qsend[:, 0:E8, :].reshape(EXP, TOK)
    value = jnp.zeros((EXP, TOK), F32)
    for p in range(CAP):
        value = jnp.where(qt2 == float(p), by_expert[:, p:p + 1], value)
    for k in range(TOP):
        gg[x, k:k + 1, :] = jnp.sum(
            jnp.where(routes_ref[k:k + 1, :] == eidx, value, 0.0), axis=0, keepdims=True)
    gg[x, 8:16, :] = jnp.sum(rz[:, E8:E8 + 8, :], axis=0)
    for i in range(XS - 1):
        gg_copy(i).start()
    for dev, there in peers_x:
        remote(gg.at[x], gg.at[there], sms.at[K_GG, 0], smr.at[K_GG, there], dev).wait_recv()

    total = jnp.sum(gg[:, 8:16, :], axis=0)
    total = jnp.sum(jnp.sum(total, axis=1, keepdims=True), axis=0, keepdims=True)
    limit = clip_ratio * math.sqrt(FFD * D * TPS * EXP)
    factor = jnp.minimum(1.0, limit / (jnp.sqrt(total) + 1e-06))
    factor_ref[...] = factor
    gg_ref[...] = jnp.sum(gg[:, 0:TOP, :], axis=0)

    for q in range(NQ):
        own_o(q).wait()
        for i in range(XS - 1):
            dev, there = peers_x[i]
            remote(
                wgs.at[q, blk(there, FFD)], out_hbm.at[0, :, col(there * DX + q * DQ, DQ)],
                osn.at[q, 0], orc.at[q, there], dev).wait_recv()
            send_o(q, i).wait_send()
    for i in range(ZS - 1):
        rz_copy(i).wait_send()
    for i in range(len(all_y)):
        ry_copy(i).wait_send()
    for i in range(XS - 1):
        gg_copy(i).wait_send()


def per_device(grad_out, routes, gates, hidden, w_down):
    E8, TPS = CS * YS, XS * HS
    TOK, D = grad_out.shape
    TOP = routes.shape[1]
    FFD, SLOTS = hidden.shape[1], hidden.shape[2]
    DX = D // XS
    DQ, DR = DX // NQ, DX // NR
    groups = slot_groups()
    GROUPS = len(groups)
    sizes = [sum(b - a for _, a, b in g) for g in groups]
    reach = [max(r for r, _, _ in g) + 1 - min(r for r, _, _ in g) for g in groups]
    vm = pltpu.VMEM
    dma = pltpu.SemaphoreType.DMA
    most = max(TPS, HS * E8, ZS)
    any_space = pl.BlockSpec(memory_space=pl.ANY)
    in_hbm = pl.BlockSpec(memory_space=pltpu.HBM)
    in_vmem = pl.BlockSpec(memory_space=pltpu.VMEM)
    part, factor, gate_grad = pl.pallas_call(
        kernel,
        out_shape=(
            jax.ShapeDtypeStruct((1, FFD, D), BF16),
            jax.ShapeDtypeStruct((1, 1), F32),
            jax.ShapeDtypeStruct((TOP, TOK), F32),
        ),
        in_specs=[in_hbm] * 5,
        out_specs=(any_space, in_vmem, in_vmem),
        scratch_shapes=[
            vm((TOP, TOK), jnp.int32),
            vm((TOP, TOK), BF16),
            vm((NR, ZS * TOK, DR), BF16),
            [vm((E8 * n, k * TOK), BF16) for n, k in zip(sizes, reach)],
            vm((NQ, E8, ZS * CAP, DQ), BF16),
            vm((NQ, SLOTS, DQ), BF16),
            vm((ZS, 2 * E8, TOK), F32),
            vm((ZS, 2 * E8, TOK), F32),
            vm((E8, ZS, TOK), F32),
            vm((E8, ZS, TOK), F32),
            vm((FFD, SLOTS), BF16),
            vm((SLOTS, SLOTS), BF16),
            vm((XS * FFD, SLOTS), BF16),
            vm((XS * FFD, SLOTS), BF16),
            vm((SLOTS, XS * FFD), BF16),
            vm((NQ, XS * FFD, DQ), BF16),
            vm((NQ, XS * FFD, DQ), BF16),
            vm((NQ, SLOTS, DQ), F32),
            vm((SLOTS, 128), F32),
            vm((SLOTS, TOK), F32),
            vm((SLOTS, TOK), F32),
            vm((E8, ZS + 8, TOK), F32),
            vm((HS * E8, ZS + 8, TOK), F32),
            vm((ZS, E8 + 8, TOK), F32),
            vm((ZS, E8 + 8, TOK), F32),
            vm((XS, 16, TOK), F32),
            dma((3 + NR + 2 * NQ + NQ * GROUPS,)),
            dma((NR, ZS)),
            dma((NR, ZS)),
            dma((NQ, GROUPS, E8)),
            dma((NQ, GROUPS, E8)),
            dma((NQ, XS)),
            dma((NQ, XS)),
            dma((XS,)),
            dma((XS,)),
            dma((2,)),
            dma((2,)),
            dma((NQ, XS)),
            dma((NQ, XS)),
            dma((5, most)),
            dma((5, most)),
        ],
        compiler_params=pltpu.CompilerParams(
            collective_id=0, has_side_effects=True, vmem_limit_bytes=40 * 1024 * 1024),
        cost_estimate=pl.CostEstimate(
            flops=2 * 2 * SLOTS * FFD * D, bytes_accessed=8 * 1024 * 1024, transcendentals=0),
        name="moe_down_backward",
    )(*[pltpu.with_memory_space_constraint(a, pltpu.HBM) for a in (routes.T, gates.T, grad_out, hidden, w_down)])
    down_grad = (part.astype(F32) * factor[0, 0]).astype(BF16)
    return (down_grad, gate_grad.T)


def solution(mesh):
    in_specs = (
        P(("dp", "edp"), None),
        P(("dp", "edp"), None),
        P(("dp", "edp"), None),
        P(("dp", "edp"), "tp", None),
        P(("dp", "edp"), "tp", None),
    )
    out_specs = (P(("dp", "edp"), "tp", None), P(("dp", "edp"), None))
    return jax.shard_map(
        per_device, mesh=mesh, in_specs=in_specs, out_specs=out_specs, check_vma=False
    )
```

```python
import functools
import math

import jax
import jax.numpy as jnp
from jax import lax
from jax.experimental import pallas as pl
from jax.experimental.pallas import tpu as pltpu
from jax.sharding import PartitionSpec as P

clip_ratio = 0.25

XS, HS, ZS, CS, YS = 4, 2, 8, 2, 4
NQ = 2
NR = 4
CAP = 20
AWAY = {8: [0, 1, -1, -2, 2, 3, -3, 4], 4: [0, 1, -1, 2], 2: [0, 1]}
MESH = pl.DeviceIdType.MESH
F32, BF16 = jnp.float32, jnp.bfloat16


def slot_groups():
    whole = CAP // 16 * 16
    rest = lambda parts: [(r, whole, CAP) for r in parts if CAP > whole]
    head = lambda parts: [(r, 0, whole) for r in parts]
    if ZS == 8:
        return [
            head([0]), head([1, 2]), head([3, 4]) + rest([0, 1, 2, 3]), head([5, 6]), head([7]) + rest([4, 5, 6, 7])]
    if ZS == 4:
        return [head([0]), head([1, 2]), head([3]) + rest([0, 1, 2, 3])]
    return [head([0]), head([1]) + rest([0, 1])]


def messages(q):
    count = len(slot_groups())
    if q == 0:
        return [(g, g) for g in range(count)]
    return [(0, 0), (1, 1), (2, 2), (3, 4)] if count == 5 else [(0, 1), (2, 2)] if count == 3 else [(0, 1)]


K_Q, K_GY, K_RY, K_RZ, K_GG = range(5)


def iota(shape, dim):
    return lax.broadcasted_iota(jnp.int32, shape, dim)


def kernel(
    routes_hbm, gates_hbm, grad_hbm, hid_hbm, w_hbm,
    out_hbm, factor_ref, gg_ref,
    routes_ref, gates_ref, tok, sel, sendb, rows, qsend, qrecv, gsy, gtab,
    hraw, perm, hx, hs, hxt, wv, wgs, gbk, acc, spread_t, rsend, ry, rzs, rz, gg,
    loc, zs, zr, ys, yr, ws, wr, hsn, hr, hfs, hfr, osn, orc, sms, smr,
):
    E8 = CS * YS
    TPS = XS * HS
    EXP = ZS * E8
    TOK, TOP = routes_ref.shape[1], routes_ref.shape[0]
    FFD = hid_hbm.shape[1]
    SLOTS = hid_hbm.shape[2]
    D = w_hbm.shape[2]
    DX = D // XS
    DQ = DX // NQ
    DR = DX // NR
    BLK = ZS * CAP
    HALF = ZS // 2
    away = AWAY[ZS]
    groups = slot_groups()
    GROUPS = len(groups)
    sizes = [sum(b - a for _, a, b in g) for g in groups]
    firsts = [sum(sizes[:i]) for i in range(GROUPS)]
    spans = [(min(r for r, _, _ in g), max(r for r, _, _ in g) + 1) for g in groups]

    def slot(d):
        return away.index(d + ZS if d <= -HALF else d)

    tp = lax.axis_index("tp")
    dp = lax.axis_index("dp")
    y = lax.axis_index("edp")
    x, h = lax.div(tp, HS), lax.rem(tp, HS)
    z, c = lax.div(dp, CS), lax.rem(dp, CS)
    yy = h * YS + y
    me8 = c * YS + y

    def at_y(delta, core):
        there = lax.rem(yy + delta + HS * YS, HS * YS)
        ylo = lax.rem(there, YS)
        return (x * HS + lax.div(there, YS), z * CS + core, ylo), core * YS + ylo

    def at_z(delta):
        zz = lax.rem(z + delta + ZS, ZS)
        return (tp, zz * CS + c, y), zz

    def at_x(delta):
        xx = lax.rem(x + delta, XS)
        return (xx * HS + h, dp, y), xx

    out_y = [at_y(2, 0), at_y(-2, 1), at_y(1, 0), at_y(-1, 0), at_y(1, 1), at_y(-1, 1), at_y(0, 1 - c)]
    all_y = [at_y(delta, core) for delta in (4, 3, -3, 2, -2, 1, -1) for core in range(CS)] + [at_y(0, 1 - c)]
    peers_z = [at_z(away[r]) for r in range(ZS - 1, 0, -1)]
    slots_z = list(range(ZS - 1, 0, -1))
    peers_x = [at_x(i) for i in ((2, 1, 3) if XS == 4 else range(1, XS))]
    near_x = [i for i in range(XS - 1) if XS < 4 or i > 0]

    barrier = pltpu.get_barrier_semaphore()
    hello = [d for d, _ in peers_z] + [d for d, _ in peers_x] + [d for d, _ in all_y]
    for d in hello:
        pl.semaphore_signal(barrier, inc=1, device_id=d, device_id_type=MESH)

    def col(start, size):
        return pl.ds(pl.multiple_of(start, size), size)

    def blk(start, size):
        return pl.ds(pl.multiple_of(start * size, size), size)

    get_r = pltpu.make_async_copy(routes_hbm, routes_ref, loc.at[1 + NR + 2 * NQ + NQ * GROUPS])
    get_r.start()
    get_g = pltpu.make_async_copy(gates_hbm, gates_ref, loc.at[2 + NR + 2 * NQ + NQ * GROUPS])
    get_g.start()
    get_t = [
        pltpu.make_async_copy(grad_hbm.at[:, col(x * DX + p * DR, DR)], tok.at[p, 0:TOK], loc.at[1 + p])
        for p in range(NR)
    ]
    for d in get_t:
        d.start()
    get_h = pltpu.make_async_copy(hid_hbm.at[0], hraw, loc.at[0])
    get_h.start()

    def own_w(q):
        return pltpu.make_async_copy(
            w_hbm.at[0, :, col(x * DX + q * DQ, DQ)], wv.at[q, blk(x, FFD)], loc.at[1 + NR + q])

    for q in range(NQ):
        own_w(q).start()

    get_r.wait()
    get_g.wait()
    eidx = iota((EXP, TOK), 0)
    chosen = jnp.zeros((EXP, TOK), F32)
    gate_t = jnp.zeros((EXP, TOK), F32)
    gates_f = gates_ref[...].astype(F32)
    for k in range(TOP):
        hit = routes_ref[k:k + 1, :] == eidx
        chosen = jnp.where(hit, 1.0, chosen)
        gate_t = jnp.where(hit, gates_f[k:k + 1, :], gate_t)
    earlier = (iota((TOK, TOK), 0) < iota((TOK, TOK), 1)).astype(F32).astype(BF16)
    count = jnp.dot(chosen.astype(BF16), earlier, preferred_element_type=F32)
    qt = jnp.where(chosen > 0.5, count, -1.0)
    table = jnp.zeros((EXP, TOK), F32)
    pidx = iota((EXP, TOK), 1)
    for p in range(CAP):
        value = jnp.sum(jnp.where(qt == float(p), gate_t, 0.0), axis=1, keepdims=True)
        table = jnp.where(pidx == p, value, table)
    for i in range(ZS):
        qsend[i, 0:E8] = qt[i * E8:(i + 1) * E8]
        qsend[i, E8:2 * E8] = table[i * E8:(i + 1) * E8]
    qrecv[0] = qsend[z]

    lane = (iota((1, SLOTS), 1).astype(F32) + 0.5)
    group = jnp.floor(lane * (1.0 / BLK))
    inner = (lane - group * BLK).astype(jnp.int32)
    group = group.astype(jnp.int32)
    part_z = jnp.zeros((1, SLOTS), jnp.int32)
    from_z = jnp.zeros((1, SLOTS), jnp.int32)
    place = jnp.zeros((1, SLOTS), jnp.int32)
    start = 0
    for r, a, b in [seg for g in groups for seg in g]:
        here = (inner >= start) & (inner < start + b - a)
        part_z = jnp.where(here, r, part_z)
        from_z = jnp.where(here, lax.rem(z + away[r] + ZS, ZS), from_z)
        place = jnp.where(here, inner - (start - a), place)
        start += b - a
    source = group * ZS + part_z
    native = from_z * (E8 * CAP) + group * CAP + place

    PB = 128

    def build_perm(i, carry):
        perm[pl.ds(pl.multiple_of(i * PB, PB), PB), :] = (
            (iota((PB, SLOTS), 0) + i * PB) == native).astype(F32).astype(BF16)
        return carry

    lax.fori_loop(0, SLOTS // PB, build_perm, 0)

    get_h.wait()
    hx[blk(x, FFD), :] = jnp.dot(hraw[...], perm[...], preferred_element_type=F32).astype(BF16)

    pl.semaphore_wait(barrier, len(hello))

    def remote(src, dst, send_sem, recv_sem, dev):
        return pltpu.make_async_remote_copy(
            src_ref=src, dst_ref=dst, send_sem=send_sem, recv_sem=recv_sem, device_id=dev, device_id_type=MESH)

    waited = set()

    def have(p, d):
        r = slot(d)
        if r > 0 and (p, r) not in waited:
            waited.add((p, r))
            part = tok.at[p, r * TOK:(r + 1) * TOK]
            remote(part, part, zs.at[p, 0], zr.at[p, r], peers_z[-1][0]).wait_recv()

    sent = []

    def ring(s, pieces):
        for p in pieces:
            if s > HALF:
                continue
            for right in ([True, False] if s < HALF else [p % 2 == 0]):
                d = -(s - 1) if right else s - 1
                have(p, d)
                to = slot(d - 1 if right else d + 1)
                a = slot(d)
                dev = at_z(1 if right else -1)[0]
                copy = remote(
                    tok.at[p, a * TOK:(a + 1) * TOK], tok.at[p, to * TOK:(to + 1) * TOK],
                    zs.at[p, to], zr.at[p, to], dev)
                copy.start()
                sent.append(copy)

    def q_copy(i):
        dev, there = peers_z[i]
        r = slot(-away[slots_z[i]])
        return remote(qsend.at[there], qrecv.at[r], sms.at[K_Q, i], smr.at[K_Q, r], dev)

    def send_w(q, i):
        dev, there = peers_x[i]
        return remote(
            w_hbm.at[0, :, col(there * DX + q * DQ, DQ)], wv.at[q, blk(x, FFD)], ws.at[q, i], wr.at[q, x], dev)

    def send_h(i):
        dev, there = peers_x[i]
        part = hx.at[blk(x, FFD)]
        return remote(part, part, hsn.at[i], hr.at[x], dev)

    pieces = list(range(NR))
    for p in pieces[:NR // 2]:
        get_t[p].wait()
    ring(1, pieces[:NR // 2])
    for i in range(ZS - 1):
        q_copy(i).start()
    for i in near_x:
        send_h(i).start()
    for p in pieces[NR // 2:]:
        get_t[p].wait()
    ring(1, pieces[NR // 2:])
    for q in range(NQ):
        for i in near_x + [i for i in range(XS - 1) if i not in near_x]:
            send_w(q, i).start()

    def got_h(i):
        dev, there = peers_x[i]
        part = hx.at[blk(there, FFD)]
        remote(part, part, hsn.at[0], hr.at[there], dev).wait_recv()

    def pass_h(i):
        frm = peers_x[1 if i == 1 else 2][1]
        part = hx.at[pl.ds(pl.multiple_of(frm * FFD + i * (FFD // 2), FFD // 2), FFD // 2)]
        return remote(part, part, hfs.at[i], hfr.at[i], peers_x[2 if i == 1 else 1][0])

    def far_h():
        if XS == 4:
            for i in range(2):
                got_h(2 - i)
                pass_h(i).start()

    heard = set()

    def build_sel(g):
        if g >= GROUPS:
            return
        lo, hi = spans[g]
        n = sizes[g]
        at = iota((n, TOK), 0)
        for r in range(lo, hi):
            if r > 0 and r not in heard:
                heard.add(r)
                remote(qsend.at[0], qrecv.at[r], sms.at[K_Q, 0], smr.at[K_Q, r], peers_z[0][0]).wait_recv()
            want = jnp.full((n, TOK), -7, jnp.int32)
            start = 0
            for rr, a, b in groups[g]:
                if rr == r:
                    want = jnp.where((at >= start) & (at < start + b - a), at - (start - a), want)
                start += b - a
            want = want.astype(F32)
            tile = qrecv[r, 0:E8]
            for e in range(E8):
                sel[g][e * n:(e + 1) * n, (r - lo) * TOK:(r - lo + 1) * TOK] = (
                    want == tile[e:e + 1, :]).astype(F32).astype(BF16)

    def span_of(m):
        return firsts[m[0]], firsts[m[1]] + sizes[m[1]]

    def part_of(expert, m):
        lo, hi = span_of(m)
        return pl.ds(pl.multiple_of(expert * BLK + lo, 16), hi - lo)

    def send_y(q, m, i):
        dev, there = out_y[i]
        lo, hi = span_of(m)
        return remote(
            sendb.at[q, there, lo:hi], rows.at[q, part_of(me8, m)], ys.at[q, m[1], i], yr.at[q, m[1], me8], dev)

    def own_rows(q, m):
        lo, hi = span_of(m)
        return pltpu.make_async_copy(
            sendb.at[q, me8, lo:hi], rows.at[q, part_of(me8, m)], loc.at[1 + NR + NQ + q * GROUPS + m[1]])

    def select(q, g):
        if g >= GROUPS:
            return
        lo, hi = spans[g]
        n = sizes[g]
        for p in range(q * NR // NQ, (q + 1) * NR // NQ):
            for r in range(lo, hi):
                have(p, away[r])
            got = jnp.dot(sel[g][...], tok[p, lo * TOK:hi * TOK, :], preferred_element_type=F32).astype(BF16)
            at = (p - q * NR // NQ) * DR
            for e in range(E8):
                sendb[q, e, firsts[g]:firsts[g] + n, at:at + DR] = got[e * n:(e + 1) * n]
        for m in messages(q):
            if m[1] == g:
                for i in range(E8 - 1):
                    send_y(q, m, i).start()
                own_rows(q, m).start()

    def gy_copy(i):
        dev, there = out_y[i]
        return remote(gsy.at[there], gtab.at[me8], sms.at[K_GY, i], smr.at[K_GY, me8], dev)

    def gates_on():
        for r in range(1, ZS):
            if r not in heard:
                heard.add(r)
                remote(qsend.at[0], qrecv.at[r], sms.at[K_Q, 0], smr.at[K_Q, r], peers_z[0][0]).wait_recv()
        for r in range(ZS):
            for e in range(E8):
                gsy[e, r:r + 1, :] = qrecv[r, E8 + e:E8 + e + 1, :]
        gtab[me8] = gsy[me8]
        for i in range(E8 - 1):
            gy_copy(i).start()

    first, second = pieces[:NR // 2], pieces[NR // 2:]
    build_sel(0)
    select(0, 0)
    select(1, 0)
    ring(2, first)
    build_sel(1)
    select(0, 1)
    ring(2, second)
    select(1, 1)
    ring(3, first)
    build_sel(2)
    select(0, 2)
    ring(3, second)
    select(1, 2)
    gates_on()
    build_sel(3)
    ring(4, first)
    select(0, 3)
    build_sel(4)
    ring(4, second)
    select(1, 3)
    select(0, 4)
    select(1, 4)
    far_h()

    def turn(there):
        for j in range(SLOTS // PB):
            hxt[there, j * PB:(j + 1) * PB, :] = hx[blk(there, FFD), j * PB:(j + 1) * PB].T

    def wait_w(q, i):
        dev, there = peers_x[i]
        remote(
            w_hbm.at[0, :, col(x * DX + q * DQ, DQ)], wv.at[q, blk(there, FFD)],
            ws.at[q, 0], wr.at[q, there], dev).wait_recv()

    def turned(q, there):
        return jnp.dot(hxt[there], wv[q, blk(there, FFD), :], preferred_element_type=F32)

    turn(x)
    for q in range(NQ):
        own_w(q).wait()
        gbk[q] = turned(q, x)
    for i in near_x:
        if XS < 4:
            got_h(i)
        turn(peers_x[i][1])
        for q in range(NQ):
            wait_w(q, i)
            gbk[q] = gbk[q] + turned(q, peers_x[i][1])
    for copy in sent:
        copy.wait_send()
    for i in range(ZS - 1):
        q_copy(i).wait_send()
    for i in near_x:
        send_h(i).wait_send()
        for q in range(NQ):
            send_w(q, i).wait_send()
    for dev, there in out_y:
        remote(gsy.at[there], gtab.at[there], sms.at[K_GY, 0], smr.at[K_GY, there], dev).wait_recv()
    spread = (iota((TOK, SLOTS), 0) == place).astype(F32)
    for j in range(SLOTS // PB):
        spread_t[j * PB:(j + 1) * PB, :] = spread[:, j * PB:(j + 1) * PB].T
    spread = spread.astype(BF16)
    gate_all = jnp.dot(gtab[...].reshape(EXP, TOK).astype(BF16), spread, preferred_element_type=F32)
    pick = iota((EXP, SLOTS), 0) == source
    gate_lane = jnp.sum(jnp.where(pick, gate_all, 0.0), axis=0, keepdims=True)

    def gated(there):
        part = blk(there, FFD)
        hs[part, :] = (hx[part, :].astype(F32) * gate_lane).astype(BF16)

    gated(x)
    for i in near_x:
        gated(peers_x[i][1])

    def get_far():
        for i in range(2):
            part = hx.at[pl.ds(pl.multiple_of(peers_x[0][1] * FFD + i * (FFD // 2), FFD // 2), FFD // 2)]
            remote(part, part, hfs.at[i], hfr.at[i], peers_x[1][0]).wait_recv()
        turn(peers_x[0][1])
        gated(peers_x[0][1])


    def wait_rows(q):
        for m in messages(q):
            own_rows(q, m).wait()
            lo, hi = span_of(m)
            for dev, there in out_y:
                remote(
                    sendb.at[q, there, lo:hi], rows.at[q, part_of(there, m)],
                    ys.at[q, m[1], 0], yr.at[q, m[1], there], dev).wait_recv()

    def send_o(q, i):
        dev, there = peers_x[i]
        return remote(
            wgs.at[q, blk(there, FFD)], out_hbm.at[0, :, col(x * DX + q * DQ, DQ)],
            osn.at[q, i], orc.at[q, x], dev)

    def own_o(q):
        return pltpu.make_async_copy(
            wgs.at[q, blk(x, FFD)], out_hbm.at[0, :, col(x * DX + q * DQ, DQ)],
            loc.at[1 + NR + NQ + NQ * GROUPS + q])

    def products(q, squares):
        wait_rows(q)
        for i in near_x + [XS - 1] + [i for i in range(XS - 1) if i not in near_x]:
            there = x if i == XS - 1 else peers_x[i][1]
            if i not in near_x and i < XS - 1 and q == 0:
                get_far()
            wg = jnp.dot(hs[blk(there, FFD), :], rows[q], preferred_element_type=F32)
            wgs[q, blk(there, FFD), :] = wg.astype(BF16)
            if i == XS - 1:
                own_o(q).start()
            else:
                send_o(q, i).start()
            squares = squares + jnp.sum((wg * wg).reshape(FFD // 8, 8, DQ), axis=0)
        return squares

    def fold(q):
        got = gbk[q]
        if XS == 4:
            wait_w(q, 0)
            got = got + turned(q, peers_x[0][1])
        both = got * rows[q].astype(F32)
        total = both[:, 0:128]
        for i in range(1, DQ // 128):
            total = total + both[:, i * 128:(i + 1) * 128]
        return total

    squares = products(0, jnp.zeros((8, DQ), F32))
    acc[...] = fold(0)
    for i in range(E8 - 1):
        gy_copy(i).wait_send()
        for m in messages(0):
            send_y(0, m, i).wait_send()
    for q in range(1, NQ):
        squares = products(q, squares)
    for q in range(1, NQ):
        acc[...] += fold(q)
    by_place = spread_t[...] * jnp.sum(acc[...], axis=1, keepdims=True)
    own_square = jnp.sum(jnp.sum(squares, axis=1, keepdims=True), axis=0, keepdims=True)

    high = by_place.astype(BF16)
    low = (by_place - high.astype(F32)).astype(BF16)
    pick_b = pick.astype(F32).astype(BF16)
    back = jnp.dot(pick_b, high, preferred_element_type=F32) + jnp.dot(pick_b, low, preferred_element_type=F32)
    back = jnp.where(iota((EXP, TOK), 1) == TOK - 1, own_square, back)
    for e in range(E8):
        rsend[e] = back[e * ZS:(e + 1) * ZS]

    def ry_copy(i):
        dev, there = all_y[i]
        return remote(rsend.at[there], ry.at[h * E8 + me8], sms.at[K_RY, i], smr.at[K_RY, h * E8 + me8], dev)

    def rz_copy(i):
        dev, there = peers_z[i]
        return remote(rzs.at[slots_z[i]], rz.at[z], sms.at[K_RZ, i], smr.at[K_RZ, z], dev)

    def gg_copy(i):
        dev, there = peers_x[i]
        return remote(gg.at[x], gg.at[x], sms.at[K_GG, i], smr.at[K_GG, x], dev)

    for i in range(len(all_y)):
        ry_copy(i).start()
    ry[h * E8 + me8] = rsend[me8]

    for q in range(1, NQ):
        for m in messages(q):
            for i in range(E8 - 1):
                send_y(q, m, i).wait_send()
    if XS == 4:
        for q in range(NQ):
            send_w(q, 0).wait_send()
        for i in range(2):
            pass_h(i).wait_send()

    for dev, there in all_y:
        there = lax.rem(dev[0], HS) * E8 + there
        remote(rsend.at[0], ry.at[there], sms.at[K_RY, 0], smr.at[K_RY, there], dev).wait_recv()

    for r in range(ZS):
        for e in range(E8):
            rzs[r, e:e + 1, :] = ry[e, r:r + 1, :] + ry[E8 + e, r:r + 1, :]
    for i in range(ZS - 1):
        rz_copy(i).start()
    rz[z] = rzs[0]
    for dev, there in peers_z:
        remote(rzs.at[0], rz.at[there], sms.at[K_RZ, 0], smr.at[K_RZ, there], dev).wait_recv()

    by_expert = rz[...].reshape(EXP, TOK)
    qt2 = qsend[:, 0:E8, :].reshape(EXP, TOK)
    value = jnp.zeros((EXP, TOK), F32)
    for p in range(CAP):
        value = jnp.where(qt2 == float(p), by_expert[:, p:p + 1], value)
    for k in range(TOP):
        gg[x, k:k + 1, :] = jnp.sum(
            jnp.where(routes_ref[k:k + 1, :] == eidx, value, 0.0), axis=0, keepdims=True)
    gg[x, 8:16, :] = jnp.broadcast_to(
        jnp.sum(by_expert[:, TOK - 1:TOK], axis=0, keepdims=True), (8, TOK))
    for i in range(XS - 1):
        gg_copy(i).start()
    for dev, there in peers_x:
        remote(gg.at[x], gg.at[there], sms.at[K_GG, 0], smr.at[K_GG, there], dev).wait_recv()

    total = jnp.sum(gg[:, 8:16, :], axis=0)[0:1, 0:1]
    limit = clip_ratio * math.sqrt(FFD * D * TPS * EXP)
    factor = jnp.minimum(1.0, limit / (jnp.sqrt(total) + 1e-06))
    factor_ref[...] = factor
    gg_ref[...] = jnp.sum(gg[:, 0:TOP, :], axis=0)

    for q in range(NQ):
        own_o(q).wait()
        for i in range(XS - 1):
            dev, there = peers_x[i]
            remote(
                wgs.at[q, blk(there, FFD)], out_hbm.at[0, :, col(there * DX + q * DQ, DQ)],
                osn.at[q, 0], orc.at[q, there], dev).wait_recv()
            send_o(q, i).wait_send()
    for i in range(ZS - 1):
        rz_copy(i).wait_send()
    for i in range(len(all_y)):
        ry_copy(i).wait_send()
    for i in range(XS - 1):
        gg_copy(i).wait_send()


def per_device(grad_out, routes, gates, hidden, w_down):
    E8, TPS = CS * YS, XS * HS
    TOK, D = grad_out.shape
    TOP = routes.shape[1]
    FFD, SLOTS = hidden.shape[1], hidden.shape[2]
    DX = D // XS
    DQ, DR = DX // NQ, DX // NR
    groups = slot_groups()
    GROUPS = len(groups)
    sizes = [sum(b - a for _, a, b in g) for g in groups]
    reach = [max(r for r, _, _ in g) + 1 - min(r for r, _, _ in g) for g in groups]
    vm = pltpu.VMEM
    dma = pltpu.SemaphoreType.DMA
    most = max(TPS, HS * E8, ZS)
    any_space = pl.BlockSpec(memory_space=pl.ANY)
    in_hbm = pl.BlockSpec(memory_space=pltpu.HBM)
    in_vmem = pl.BlockSpec(memory_space=pltpu.VMEM)
    part, factor, gate_grad = pl.pallas_call(
        kernel,
        out_shape=(
            jax.ShapeDtypeStruct((1, FFD, D), BF16),
            jax.ShapeDtypeStruct((1, 1), F32),
            jax.ShapeDtypeStruct((TOP, TOK), F32),
        ),
        in_specs=[in_hbm] * 5,
        out_specs=(any_space, in_vmem, in_vmem),
        scratch_shapes=[
            vm((TOP, TOK), jnp.int32),
            vm((TOP, TOK), BF16),
            vm((NR, ZS * TOK, DR), BF16),
            [vm((E8 * n, k * TOK), BF16) for n, k in zip(sizes, reach)],
            vm((NQ, E8, ZS * CAP, DQ), BF16),
            vm((NQ, SLOTS, DQ), BF16),
            vm((ZS, 2 * E8, TOK), F32),
            vm((ZS, 2 * E8, TOK), F32),
            vm((E8, ZS, TOK), F32),
            vm((E8, ZS, TOK), F32),
            vm((FFD, SLOTS), BF16),
            vm((SLOTS, SLOTS), BF16),
            vm((XS * FFD, SLOTS), BF16),
            vm((XS * FFD, SLOTS), BF16),
            vm((XS, SLOTS, FFD), BF16),
            vm((NQ, XS * FFD, DQ), BF16),
            vm((NQ, XS * FFD, DQ), BF16),
            vm((NQ, SLOTS, DQ), F32),
            vm((SLOTS, 128), F32),
            vm((SLOTS, TOK), F32),
            vm((E8, ZS, TOK), F32),
            vm((HS * E8, ZS, TOK), F32),
            vm((ZS, E8, TOK), F32),
            vm((ZS, E8, TOK), F32),
            vm((XS, 16, TOK), F32),
            dma((3 + NR + 2 * NQ + NQ * GROUPS,)),
            dma((NR, ZS)),
            dma((NR, ZS)),
            dma((NQ, GROUPS, E8)),
            dma((NQ, GROUPS, E8)),
            dma((NQ, XS)),
            dma((NQ, XS)),
            dma((XS,)),
            dma((XS,)),
            dma((2,)),
            dma((2,)),
            dma((NQ, XS)),
            dma((NQ, XS)),
            dma((5, most)),
            dma((5, most)),
        ],
        compiler_params=pltpu.CompilerParams(
            collective_id=0, has_side_effects=True, vmem_limit_bytes=40 * 1024 * 1024),
        cost_estimate=pl.CostEstimate(
            flops=2 * 2 * SLOTS * FFD * D, bytes_accessed=8 * 1024 * 1024, transcendentals=0),
        name="moe_down_backward",
    )(*[pltpu.with_memory_space_constraint(a, pltpu.HBM) for a in (routes.T, gates.T, grad_out, hidden, w_down)])
    down_grad = (part.astype(F32) * factor[0, 0]).astype(BF16)
    return (down_grad, gate_grad.T)


def solution(mesh):
    in_specs = (
        P(("dp", "edp"), None),
        P(("dp", "edp"), None),
        P(("dp", "edp"), None),
        P(("dp", "edp"), "tp", None),
        P(("dp", "edp"), "tp", None),
    )
    out_specs = (P(("dp", "edp"), "tp", None), P(("dp", "edp"), None))
    return jax.shard_map(
        per_device, mesh=mesh, in_specs=in_specs, out_specs=out_specs, check_vma=False
    )
```

```python
import functools
import math

import jax
import jax.numpy as jnp
from jax import lax
from jax.experimental import pallas as pl
from jax.experimental.pallas import tpu as pltpu
from jax.sharding import PartitionSpec as P

clip_ratio = 0.25

XS, HS, ZS, CS, YS = 4, 2, 8, 2, 4
NQ = 2
NR = 4
CAP = 20
AWAY = {8: [0, 1, -1, -2, 2, 3, -3, 4], 4: [0, 1, -1, 2], 2: [0, 1]}
MESH = pl.DeviceIdType.MESH
F32, BF16 = jnp.float32, jnp.bfloat16


def slot_groups():
    whole = CAP // 16 * 16
    rest = lambda parts: [(r, whole, CAP) for r in parts if CAP > whole]
    head = lambda parts: [(r, 0, whole) for r in parts]
    if ZS == 8:
        return [
            head([0]), head([1, 2]), head([3, 4]) + rest([0, 1, 2, 3]), head([5, 6]), head([7]) + rest([4, 5, 6, 7])]
    if ZS == 4:
        return [head([0]), head([1, 2]), head([3]) + rest([0, 1, 2, 3])]
    return [head([0]), head([1]) + rest([0, 1])]


def messages(q):
    count = len(slot_groups())
    if q == 0:
        return [(g, g) for g in range(count)]
    return [(0, 0), (1, 1), (2, 2), (3, 4)] if count == 5 else [(0, 1), (2, 2)] if count == 3 else [(0, 1)]


K_Q, K_GY, K_RY, K_RZ, K_GG = range(5)


def iota(shape, dim):
    return lax.broadcasted_iota(jnp.int32, shape, dim)


def kernel(
    routes_hbm, gates_hbm, grad_hbm, hid_hbm, w_hbm,
    out_hbm, factor_ref, gg_ref,
    routes_ref, gates_ref, tok, sel, sendb, rows, qsend, qrecv, gsy, gtab,
    hraw, perm, hx, hs, hxt, wv, wgs, gbk, acc, spread_t, rsend, ry, rzs, rz, gg,
    loc, zs, zr, ys, yr, ws, wr, hsn, hr, hfs, hfr, osn, orc, sms, smr,
):
    E8 = CS * YS
    TPS = XS * HS
    EXP = ZS * E8
    TOK, TOP = routes_ref.shape[1], routes_ref.shape[0]
    FFD = hid_hbm.shape[1]
    SLOTS = hid_hbm.shape[2]
    D = w_hbm.shape[2]
    DX = D // XS
    DQ = DX // NQ
    DR = DX // NR
    BLK = ZS * CAP
    HALF = ZS // 2
    away = AWAY[ZS]
    groups = slot_groups()
    GROUPS = len(groups)
    sizes = [sum(b - a for _, a, b in g) for g in groups]
    firsts = [sum(sizes[:i]) for i in range(GROUPS)]
    spans = [(min(r for r, _, _ in g), max(r for r, _, _ in g) + 1) for g in groups]

    def slot(d):
        return away.index(d + ZS if d <= -HALF else d)

    tp = lax.axis_index("tp")
    dp = lax.axis_index("dp")
    y = lax.axis_index("edp")
    x, h = lax.div(tp, HS), lax.rem(tp, HS)
    z, c = lax.div(dp, CS), lax.rem(dp, CS)
    yy = h * YS + y
    me8 = c * YS + y

    def at_y(delta, core):
        there = lax.rem(yy + delta + HS * YS, HS * YS)
        ylo = lax.rem(there, YS)
        return (x * HS + lax.div(there, YS), z * CS + core, ylo), core * YS + ylo

    def at_z(delta):
        zz = lax.rem(z + delta + ZS, ZS)
        return (tp, zz * CS + c, y), zz

    def at_x(delta):
        xx = lax.rem(x + delta, XS)
        return (xx * HS + h, dp, y), xx

    out_y = [at_y(2, 0), at_y(-2, 1), at_y(1, 0), at_y(-1, 0), at_y(1, 1), at_y(-1, 1), at_y(0, 1 - c)]
    all_y = [at_y(delta, core) for delta in (4, 3, -3, 2, -2, 1, -1) for core in range(CS)] + [at_y(0, 1 - c)]
    peers_z = [at_z(away[r]) for r in range(ZS - 1, 0, -1)]
    slots_z = list(range(ZS - 1, 0, -1))
    peers_x = [at_x(i) for i in ((2, 1, 3) if XS == 4 else range(1, XS))]
    near_x = [i for i in range(XS - 1) if XS < 4 or i > 0]

    barrier = pltpu.get_barrier_semaphore()
    hello = [d for d, _ in peers_z] + [d for d, _ in peers_x] + [d for d, _ in all_y]
    for d in hello:
        pl.semaphore_signal(barrier, inc=1, device_id=d, device_id_type=MESH)

    def col(start, size):
        return pl.ds(pl.multiple_of(start, size), size)

    def blk(start, size):
        return pl.ds(pl.multiple_of(start * size, size), size)

    get_r = pltpu.make_async_copy(routes_hbm, routes_ref, loc.at[1 + NR + 2 * NQ + NQ * GROUPS])
    get_r.start()
    get_g = pltpu.make_async_copy(gates_hbm, gates_ref, loc.at[2 + NR + 2 * NQ + NQ * GROUPS])
    get_g.start()
    get_t = [
        pltpu.make_async_copy(grad_hbm.at[:, col(x * DX + p * DR, DR)], tok.at[p, 0:TOK], loc.at[1 + p])
        for p in range(NR)
    ]
    for d in get_t:
        d.start()
    get_h = pltpu.make_async_copy(hid_hbm.at[0], hraw, loc.at[0])
    get_h.start()

    def own_w(q):
        return pltpu.make_async_copy(
            w_hbm.at[0, :, col(x * DX + q * DQ, DQ)], wv.at[q, blk(x, FFD)], loc.at[1 + NR + q])

    for q in range(NQ):
        own_w(q).start()

    get_r.wait()
    get_g.wait()
    eidx = iota((EXP, TOK), 0)
    chosen = jnp.zeros((EXP, TOK), F32)
    gate_t = jnp.zeros((EXP, TOK), F32)
    gates_f = gates_ref[...].astype(F32)
    for k in range(TOP):
        hit = routes_ref[k:k + 1, :] == eidx
        chosen = jnp.where(hit, 1.0, chosen)
        gate_t = jnp.where(hit, gates_f[k:k + 1, :], gate_t)
    earlier = (iota((TOK, TOK), 0) < iota((TOK, TOK), 1)).astype(F32).astype(BF16)
    count = jnp.dot(chosen.astype(BF16), earlier, preferred_element_type=F32)
    qt = jnp.where(chosen > 0.5, count, -1.0)
    table = jnp.zeros((EXP, TOK), F32)
    pidx = iota((EXP, TOK), 1)
    for p in range(CAP):
        value = jnp.sum(jnp.where(qt == float(p), gate_t, 0.0), axis=1, keepdims=True)
        table = jnp.where(pidx == p, value, table)
    for i in range(ZS):
        qsend[i, 0:E8] = qt[i * E8:(i + 1) * E8]
        qsend[i, E8:2 * E8] = table[i * E8:(i + 1) * E8]
    qrecv[0] = qsend[z]

    lane = (iota((1, SLOTS), 1).astype(F32) + 0.5)
    group = jnp.floor(lane * (1.0 / BLK))
    inner = (lane - group * BLK).astype(jnp.int32)
    group = group.astype(jnp.int32)
    part_z = jnp.zeros((1, SLOTS), jnp.int32)
    from_z = jnp.zeros((1, SLOTS), jnp.int32)
    place = jnp.zeros((1, SLOTS), jnp.int32)
    start = 0
    for r, a, b in [seg for g in groups for seg in g]:
        here = (inner >= start) & (inner < start + b - a)
        part_z = jnp.where(here, r, part_z)
        from_z = jnp.where(here, lax.rem(z + away[r] + ZS, ZS), from_z)
        place = jnp.where(here, inner - (start - a), place)
        start += b - a
    source = group * ZS + part_z
    native = from_z * (E8 * CAP) + group * CAP + place

    PB = 128

    def build_perm(i, carry):
        perm[pl.ds(pl.multiple_of(i * PB, PB), PB), :] = (
            (iota((PB, SLOTS), 0) + i * PB) == native).astype(F32).astype(BF16)
        return carry

    lax.fori_loop(0, SLOTS // PB, build_perm, 0)

    get_h.wait()
    hx[blk(x, FFD), :] = jnp.dot(hraw[...], perm[...], preferred_element_type=F32).astype(BF16)

    pl.semaphore_wait(barrier, len(hello))

    def remote(src, dst, send_sem, recv_sem, dev):
        return pltpu.make_async_remote_copy(
            src_ref=src, dst_ref=dst, send_sem=send_sem, recv_sem=recv_sem, device_id=dev, device_id_type=MESH)

    waited = set()

    def have(p, d):
        r = slot(d)
        if r > 0 and (p, r) not in waited:
            waited.add((p, r))
            part = tok.at[p, r * TOK:(r + 1) * TOK]
            remote(part, part, zs.at[p, 0], zr.at[p, r], peers_z[-1][0]).wait_recv()

    sent = []

    def ring(s, pieces):
        for p in pieces:
            if s > HALF:
                continue
            for right in ([True, False] if s < HALF else [p % 2 == 0]):
                d = -(s - 1) if right else s - 1
                have(p, d)
                to = slot(d - 1 if right else d + 1)
                a = slot(d)
                dev = at_z(1 if right else -1)[0]
                copy = remote(
                    tok.at[p, a * TOK:(a + 1) * TOK], tok.at[p, to * TOK:(to + 1) * TOK],
                    zs.at[p, to], zr.at[p, to], dev)
                copy.start()
                sent.append(copy)

    def q_copy(i):
        dev, there = peers_z[i]
        r = slot(-away[slots_z[i]])
        return remote(qsend.at[there], qrecv.at[r], sms.at[K_Q, i], smr.at[K_Q, r], dev)

    def send_w(q, i):
        dev, there = peers_x[i]
        return remote(
            w_hbm.at[0, :, col(there * DX + q * DQ, DQ)], wv.at[q, blk(x, FFD)], ws.at[q, i], wr.at[q, x], dev)

    def send_h(i):
        dev, there = peers_x[i]
        part = hx.at[blk(x, FFD)]
        return remote(part, part, hsn.at[i], hr.at[x], dev)

    pieces = list(range(NR))
    for p in pieces[:NR // 2]:
        get_t[p].wait()
    ring(1, pieces[:NR // 2])
    for i in range(ZS - 1):
        q_copy(i).start()
    for i in near_x:
        send_h(i).start()
    for p in pieces[NR // 2:]:
        get_t[p].wait()
    ring(1, pieces[NR // 2:])
    for q in range(NQ):
        for i in near_x + [i for i in range(XS - 1) if i not in near_x]:
            send_w(q, i).start()

    def got_h(i):
        dev, there = peers_x[i]
        part = hx.at[blk(there, FFD)]
        remote(part, part, hsn.at[0], hr.at[there], dev).wait_recv()

    def pass_h(i):
        frm = peers_x[1 if i == 1 else 2][1]
        part = hx.at[pl.ds(pl.multiple_of(frm * FFD + i * (FFD // 2), FFD // 2), FFD // 2)]
        return remote(part, part, hfs.at[i], hfr.at[i], peers_x[2 if i == 1 else 1][0])

    def far_h():
        if XS == 4:
            for i in range(2):
                got_h(2 - i)
                pass_h(i).start()

    heard = set()

    def build_sel(g):
        if g >= GROUPS:
            return
        lo, hi = spans[g]
        n = sizes[g]
        at = iota((n, TOK), 0)
        for r in range(lo, hi):
            if r > 0 and r not in heard:
                heard.add(r)
                remote(qsend.at[0], qrecv.at[r], sms.at[K_Q, 0], smr.at[K_Q, r], peers_z[0][0]).wait_recv()
            want = jnp.full((n, TOK), -7, jnp.int32)
            start = 0
            for rr, a, b in groups[g]:
                if rr == r:
                    want = jnp.where((at >= start) & (at < start + b - a), at - (start - a), want)
                start += b - a
            want = want.astype(F32)
            tile = qrecv[r, 0:E8]
            for e in range(E8):
                sel[g][e * n:(e + 1) * n, (r - lo) * TOK:(r - lo + 1) * TOK] = (
                    want == tile[e:e + 1, :]).astype(F32).astype(BF16)

    def span_of(m):
        return firsts[m[0]], firsts[m[1]] + sizes[m[1]]

    def part_of(expert, m):
        lo, hi = span_of(m)
        return pl.ds(pl.multiple_of(expert * BLK + lo, 16), hi - lo)

    def send_y(q, m, i):
        dev, there = out_y[i]
        lo, hi = span_of(m)
        return remote(
            sendb.at[q, there, lo:hi], rows.at[q, part_of(me8, m)], ys.at[q, m[1], i], yr.at[q, m[1], me8], dev)

    def own_rows(q, m):
        lo, hi = span_of(m)
        return pltpu.make_async_copy(
            sendb.at[q, me8, lo:hi], rows.at[q, part_of(me8, m)], loc.at[1 + NR + NQ + q * GROUPS + m[1]])

    def select(q, g):
        if g >= GROUPS:
            return
        lo, hi = spans[g]
        n = sizes[g]
        for p in range(q * NR // NQ, (q + 1) * NR // NQ):
            for r in range(lo, hi):
                have(p, away[r])
            got = jnp.dot(sel[g][...], tok[p, lo * TOK:hi * TOK, :], preferred_element_type=F32).astype(BF16)
            at = (p - q * NR // NQ) * DR
            for e in range(E8):
                sendb[q, e, firsts[g]:firsts[g] + n, at:at + DR] = got[e * n:(e + 1) * n]
        for m in messages(q):
            if m[1] == g:
                for i in range(E8 - 1):
                    send_y(q, m, i).start()
                own_rows(q, m).start()

    def gy_copy(i):
        dev, there = out_y[i]
        return remote(gsy.at[there], gtab.at[me8], sms.at[K_GY, i], smr.at[K_GY, me8], dev)

    def gates_on():
        for r in range(1, ZS):
            if r not in heard:
                heard.add(r)
                remote(qsend.at[0], qrecv.at[r], sms.at[K_Q, 0], smr.at[K_Q, r], peers_z[0][0]).wait_recv()
        for r in range(ZS):
            for e in range(E8):
                gsy[e, r:r + 1, :] = qrecv[r, E8 + e:E8 + e + 1, :]
        gtab[me8] = gsy[me8]
        for i in range(E8 - 1):
            gy_copy(i).start()

    first, second = pieces[:NR // 2], pieces[NR // 2:]
    build_sel(0)
    select(0, 0)
    select(1, 0)
    ring(2, first)
    build_sel(1)
    select(0, 1)
    ring(2, second)
    select(1, 1)
    ring(3, first)
    build_sel(2)
    select(0, 2)
    ring(3, second)
    select(1, 2)
    gates_on()
    build_sel(3)
    ring(4, first)
    select(0, 3)
    build_sel(4)
    ring(4, second)
    select(1, 3)
    select(0, 4)
    select(1, 4)
    far_h()

    def turn(there):
        for j in range(SLOTS // PB):
            hxt[there, j * PB:(j + 1) * PB, :] = hx[blk(there, FFD), j * PB:(j + 1) * PB].T

    def wait_w(q, i):
        dev, there = peers_x[i]
        remote(
            w_hbm.at[0, :, col(x * DX + q * DQ, DQ)], wv.at[q, blk(there, FFD)],
            ws.at[q, 0], wr.at[q, there], dev).wait_recv()

    def turned(q, there):
        return jnp.dot(hxt[there], wv[q, blk(there, FFD), :], preferred_element_type=F32)

    turn(x)
    for q in range(NQ):
        own_w(q).wait()
        gbk[q] = turned(q, x)
    for i in near_x:
        if XS < 4:
            got_h(i)
        turn(peers_x[i][1])
        for q in range(NQ):
            wait_w(q, i)
            gbk[q] = gbk[q] + turned(q, peers_x[i][1])
    for copy in sent:
        copy.wait_send()
    for i in range(ZS - 1):
        q_copy(i).wait_send()
    for i in near_x:
        send_h(i).wait_send()
        for q in range(NQ):
            send_w(q, i).wait_send()
    for dev, there in out_y:
        remote(gsy.at[there], gtab.at[there], sms.at[K_GY, 0], smr.at[K_GY, there], dev).wait_recv()
    spread = (iota((TOK, SLOTS), 0) == place).astype(F32)
    for j in range(SLOTS // PB):
        spread_t[j * PB:(j + 1) * PB, :] = spread[:, j * PB:(j + 1) * PB].T
    spread = spread.astype(BF16)
    gate_all = jnp.dot(gtab[...].reshape(EXP, TOK).astype(BF16), spread, preferred_element_type=F32)
    pick = iota((EXP, SLOTS), 0) == source
    gate_lane = jnp.sum(jnp.where(pick, gate_all, 0.0), axis=0, keepdims=True)

    def gated(there):
        part = blk(there, FFD)
        hs[part, :] = (hx[part, :].astype(F32) * gate_lane).astype(BF16)

    gated(x)
    for i in near_x:
        gated(peers_x[i][1])

    def get_far():
        for i in range(2):
            part = hx.at[pl.ds(pl.multiple_of(peers_x[0][1] * FFD + i * (FFD // 2), FFD // 2), FFD // 2)]
            remote(part, part, hfs.at[i], hfr.at[i], peers_x[1][0]).wait_recv()
        turn(peers_x[0][1])
        gated(peers_x[0][1])


    def wait_rows(q):
        for m in messages(q):
            own_rows(q, m).wait()
            lo, hi = span_of(m)
            for dev, there in out_y:
                remote(
                    sendb.at[q, there, lo:hi], rows.at[q, part_of(there, m)],
                    ys.at[q, m[1], 0], yr.at[q, m[1], there], dev).wait_recv()

    def send_o(q, i):
        dev, there = peers_x[i]
        return remote(
            wgs.at[q, blk(there, FFD)], out_hbm.at[0, :, col(x * DX + q * DQ, DQ)],
            osn.at[q, i], orc.at[q, x], dev)

    def own_o(q):
        return pltpu.make_async_copy(
            wgs.at[q, blk(x, FFD)], out_hbm.at[0, :, col(x * DX + q * DQ, DQ)],
            loc.at[1 + NR + NQ + NQ * GROUPS + q])

    def products(q, squares):
        wait_rows(q)
        for i in near_x + [XS - 1] + [i for i in range(XS - 1) if i not in near_x]:
            there = x if i == XS - 1 else peers_x[i][1]
            if i not in near_x and i < XS - 1 and q == 0:
                get_far()
            wg = jnp.dot(hs[blk(there, FFD), :], rows[q], preferred_element_type=F32)
            wgs[q, blk(there, FFD), :] = wg.astype(BF16)
            if i == XS - 1:
                own_o(q).start()
            else:
                send_o(q, i).start()
            squares = squares + jnp.sum((wg * wg).reshape(FFD // 8, 8, DQ), axis=0)
        return squares

    def fold(q):
        got = gbk[q]
        if XS == 4:
            wait_w(q, 0)
            got = got + turned(q, peers_x[0][1])
        both = got * rows[q].astype(F32)
        total = both[:, 0:128]
        for i in range(1, DQ // 128):
            total = total + both[:, i * 128:(i + 1) * 128]
        return total

    squares = products(0, jnp.zeros((8, DQ), F32))
    acc[...] = fold(0)
    for i in range(E8 - 1):
        gy_copy(i).wait_send()
        for m in messages(0):
            send_y(0, m, i).wait_send()
    for q in range(1, NQ):
        squares = products(q, squares)
    for q in range(1, NQ):
        acc[...] += fold(q)
    by_place = spread_t[...] * jnp.sum(acc[...], axis=1, keepdims=True)
    own_square = jnp.sum(jnp.sum(squares, axis=1, keepdims=True), axis=0, keepdims=True)

    high = by_place.astype(BF16)
    low = (by_place - high.astype(F32)).astype(BF16)
    pick_b = pick.astype(F32).astype(BF16)
    back = jnp.dot(pick_b, high, preferred_element_type=F32) + jnp.dot(pick_b, low, preferred_element_type=F32)
    back = jnp.where(iota((EXP, TOK), 1) == TOK - 1, own_square, back)
    for e in range(E8):
        rsend[e] = back[e * ZS:(e + 1) * ZS]

    def ry_copy(i):
        dev, there = all_y[i]
        return remote(rsend.at[there], ry.at[h * E8 + me8], sms.at[K_RY, i], smr.at[K_RY, h * E8 + me8], dev)

    def rz_copy(i):
        dev, there = peers_z[i]
        return remote(rzs.at[slots_z[i]], rz.at[z], sms.at[K_RZ, i], smr.at[K_RZ, z], dev)

    def gg_copy(i):
        dev, there = peers_x[i]
        return remote(gg.at[x], gg.at[x], sms.at[K_GG, i], smr.at[K_GG, x], dev)

    for i in range(len(all_y)):
        ry_copy(i).start()
    ry[h * E8 + me8] = rsend[me8]

    for q in range(1, NQ):
        for m in messages(q):
            for i in range(E8 - 1):
                send_y(q, m, i).wait_send()
    if XS == 4:
        for q in range(NQ):
            send_w(q, 0).wait_send()
        for i in range(2):
            pass_h(i).wait_send()

    for dev, there in all_y:
        there = lax.rem(dev[0], HS) * E8 + there
        remote(rsend.at[0], ry.at[there], sms.at[K_RY, 0], smr.at[K_RY, there], dev).wait_recv()

    for r in range(ZS):
        for e in range(E8):
            rzs[r, e:e + 1, :] = ry[e, r:r + 1, :] + ry[E8 + e, r:r + 1, :]
    for i in range(ZS - 1):
        rz_copy(i).start()
    rz[z] = rzs[0]
    for dev, there in peers_z:
        remote(rzs.at[0], rz.at[there], sms.at[K_RZ, 0], smr.at[K_RZ, there], dev).wait_recv()

    by_expert = rz[...].reshape(EXP, TOK)
    qt2 = qsend[:, 0:E8, :].reshape(EXP, TOK)
    value = jnp.zeros((EXP, TOK), F32)
    for p in range(CAP):
        value = jnp.where(qt2 == float(p), by_expert[:, p:p + 1], value)
    for k in range(TOP):
        gg[x, k:k + 1, :] = jnp.sum(
            jnp.where(routes_ref[k:k + 1, :] == eidx, value, 0.0), axis=0, keepdims=True)
    gg[x, 8:16, :] = jnp.broadcast_to(
        jnp.sum(by_expert[:, TOK - 1:TOK], axis=0, keepdims=True), (8, TOK))
    for i in range(XS - 1):
        gg_copy(i).start()
    for q in range(NQ):
        own_o(q).wait()
        for i in range(XS - 1):
            dev, there = peers_x[i]
            remote(
                wgs.at[q, blk(there, FFD)], out_hbm.at[0, :, col(there * DX + q * DQ, DQ)],
                osn.at[q, 0], orc.at[q, there], dev).wait_recv()
            send_o(q, i).wait_send()
    for i in range(ZS - 1):
        rz_copy(i).wait_send()
    for i in range(len(all_y)):
        ry_copy(i).wait_send()

    for dev, there in peers_x:
        remote(gg.at[x], gg.at[there], sms.at[K_GG, 0], smr.at[K_GG, there], dev).wait_recv()

    total = jnp.sum(gg[:, 8:16, :], axis=0)[0:1, 0:1]
    limit = clip_ratio * math.sqrt(FFD * D * TPS * EXP)
    factor = jnp.minimum(1.0, limit / (jnp.sqrt(total) + 1e-06))
    factor_ref[...] = jnp.broadcast_to(factor, factor_ref.shape)
    gg_ref[...] = jnp.sum(gg[:, 0:TOP, :], axis=0)
    for i in range(XS - 1):
        gg_copy(i).wait_send()


def scale_kernel(part_ref, factor_ref, gg_in, out_hbm, gg_out, buf, done, gg_done):
    gg_copy = pltpu.make_async_copy(gg_in, gg_out, gg_done)
    gg_copy.start()
    factor = factor_ref[0:1, 0:1]
    high = buf.shape[1]
    copies = []
    for i in range(buf.shape[0]):
        at = slice(i * high, (i + 1) * high)
        buf[i] = (part_ref[0, at, :].astype(F32) * factor).astype(BF16)
        copies.append(pltpu.make_async_copy(buf.at[i], out_hbm.at[0, at, :], done.at[i]))
        copies[-1].start()
    gg_copy.wait()
    for copy in copies:
        copy.wait()


def per_device(grad_out, routes, gates, hidden, w_down):
    E8, TPS = CS * YS, XS * HS
    TOK, D = grad_out.shape
    TOP = routes.shape[1]
    FFD, SLOTS = hidden.shape[1], hidden.shape[2]
    DX = D // XS
    DQ, DR = DX // NQ, DX // NR
    groups = slot_groups()
    GROUPS = len(groups)
    sizes = [sum(b - a for _, a, b in g) for g in groups]
    reach = [max(r for r, _, _ in g) + 1 - min(r for r, _, _ in g) for g in groups]
    vm = pltpu.VMEM
    dma = pltpu.SemaphoreType.DMA
    most = max(TPS, HS * E8, ZS)
    any_space = pl.BlockSpec(memory_space=pl.ANY)
    in_hbm = pl.BlockSpec(memory_space=pltpu.HBM)
    in_vmem = pl.BlockSpec(memory_space=pltpu.VMEM)
    part, factor, gate_grad = pl.pallas_call(
        kernel,
        out_shape=(
            jax.ShapeDtypeStruct((1, FFD, D), BF16),
            jax.ShapeDtypeStruct((8, 128), F32),
            jax.ShapeDtypeStruct((TOP, TOK), F32),
        ),
        in_specs=[in_hbm] * 5,
        out_specs=(any_space, in_vmem, in_vmem),
        scratch_shapes=[
            vm((TOP, TOK), jnp.int32),
            vm((TOP, TOK), BF16),
            vm((NR, ZS * TOK, DR), BF16),
            [vm((E8 * n, k * TOK), BF16) for n, k in zip(sizes, reach)],
            vm((NQ, E8, ZS * CAP, DQ), BF16),
            vm((NQ, SLOTS, DQ), BF16),
            vm((ZS, 2 * E8, TOK), F32),
            vm((ZS, 2 * E8, TOK), F32),
            vm((E8, ZS, TOK), F32),
            vm((E8, ZS, TOK), F32),
            vm((FFD, SLOTS), BF16),
            vm((SLOTS, SLOTS), BF16),
            vm((XS * FFD, SLOTS), BF16),
            vm((XS * FFD, SLOTS), BF16),
            vm((XS, SLOTS, FFD), BF16),
            vm((NQ, XS * FFD, DQ), BF16),
            vm((NQ, XS * FFD, DQ), BF16),
            vm((NQ, SLOTS, DQ), F32),
            vm((SLOTS, 128), F32),
            vm((SLOTS, TOK), F32),
            vm((E8, ZS, TOK), F32),
            vm((HS * E8, ZS, TOK), F32),
            vm((ZS, E8, TOK), F32),
            vm((ZS, E8, TOK), F32),
            vm((XS, 16, TOK), F32),
            dma((3 + NR + 2 * NQ + NQ * GROUPS,)),
            dma((NR, ZS)),
            dma((NR, ZS)),
            dma((NQ, GROUPS, E8)),
            dma((NQ, GROUPS, E8)),
            dma((NQ, XS)),
            dma((NQ, XS)),
            dma((XS,)),
            dma((XS,)),
            dma((2,)),
            dma((2,)),
            dma((NQ, XS)),
            dma((NQ, XS)),
            dma((5, most)),
            dma((5, most)),
        ],
        compiler_params=pltpu.CompilerParams(
            collective_id=0, has_side_effects=True, vmem_limit_bytes=40 * 1024 * 1024),
        cost_estimate=pl.CostEstimate(
            flops=2 * 2 * SLOTS * FFD * D, bytes_accessed=8 * 1024 * 1024, transcendentals=0),
        name="moe_down_backward",
    )(*[pltpu.with_memory_space_constraint(a, pltpu.HBM) for a in (routes.T, gates.T, grad_out, hidden, w_down)])
    high = 32 if FFD % 32 == 0 else FFD
    down_grad, gate_grad = pl.pallas_call(
        scale_kernel,
        out_shape=(
            jax.ShapeDtypeStruct((1, FFD, D), BF16),
            jax.ShapeDtypeStruct((TOP, TOK), F32),
        ),
        in_specs=[in_vmem, in_vmem, in_vmem],
        out_specs=(any_space, any_space),
        scratch_shapes=[vm((FFD // high, high, D), BF16), dma((FFD // high,)), dma(())],
        compiler_params=pltpu.CompilerParams(vmem_limit_bytes=8 * 1024 * 1024),
        cost_estimate=pl.CostEstimate(flops=FFD * D, bytes_accessed=4 * FFD * D, transcendentals=0),
        name="scale_products",
    )(part, factor, gate_grad)
    return (down_grad, gate_grad.T)


def solution(mesh):
    in_specs = (
        P(("dp", "edp"), None),
        P(("dp", "edp"), None),
        P(("dp", "edp"), None),
        P(("dp", "edp"), "tp", None),
        P(("dp", "edp"), "tp", None),
    )
    out_specs = (P(("dp", "edp"), "tp", None), P(("dp", "edp"), None))
    return jax.shard_map(
        per_device, mesh=mesh, in_specs=in_specs, out_specs=out_specs, check_vma=False
    )
```

```python
import functools
import math

import jax
import jax.numpy as jnp
from jax import lax
from jax.experimental import pallas as pl
from jax.experimental.pallas import tpu as pltpu
from jax.sharding import PartitionSpec as P

clip_ratio = 0.25

XS, HS, ZS, CS, YS = 4, 2, 8, 2, 4
NQ = 2
NR = 4
CAP = 20
AWAY = {8: [0, 1, -1, -2, 2, 3, -3, 4], 4: [0, 1, -1, 2], 2: [0, 1]}
MESH = pl.DeviceIdType.MESH
F32, BF16 = jnp.float32, jnp.bfloat16


def slot_groups():
    whole = CAP // 16 * 16
    rest = lambda parts: [(r, whole, CAP) for r in parts if CAP > whole]
    head = lambda parts: [(r, 0, whole) for r in parts]
    if ZS == 8:
        return [
            head([0]), head([1, 2]), head([3, 4]) + rest([0, 1, 2, 3]), head([5, 6]), head([7]) + rest([4, 5, 6, 7])]
    if ZS == 4:
        return [head([0]), head([1, 2]), head([3]) + rest([0, 1, 2, 3])]
    return [head([0]), head([1]) + rest([0, 1])]


def messages(q):
    count = len(slot_groups())
    if q == 0:
        return [(g, g) for g in range(count)]
    return [(0, 0), (1, 1), (2, 2), (3, 4)] if count == 5 else [(0, 1), (2, 2)] if count == 3 else [(0, 1)]


K_Q, K_GY, K_RY, K_RZ, K_GG = range(5)


def iota(shape, dim):
    return lax.broadcasted_iota(jnp.int32, shape, dim)


def kernel(
    routes_hbm, gates_ref, grad_hbm, hid_hbm, w_hbm,
    out_hbm, factor_ref, gg_ref,
    routes_ref, tok, sel, sendb, rows, qsend, qrecv, gsy, gtab,
    hraw, perm, hx, hs, hxt, wv, wgs, gbk, acc, spread_t, rsend, ry, rzs, rz, gg,
    loc, zs, zr, ys, yr, ws, wr, hsn, hr, hfs, hfr, osn, orc, sms, smr,
):
    E8 = CS * YS
    TPS = XS * HS
    EXP = ZS * E8
    TOK, TOP = routes_ref.shape[1], routes_ref.shape[0]
    FFD = hid_hbm.shape[1]
    SLOTS = hid_hbm.shape[2]
    D = w_hbm.shape[2]
    DX = D // XS
    DQ = DX // NQ
    DR = DX // NR
    BLK = ZS * CAP
    HALF = ZS // 2
    away = AWAY[ZS]
    groups = slot_groups()
    GROUPS = len(groups)
    sizes = [sum(b - a for _, a, b in g) for g in groups]
    firsts = [sum(sizes[:i]) for i in range(GROUPS)]
    spans = [(min(r for r, _, _ in g), max(r for r, _, _ in g) + 1) for g in groups]

    def slot(d):
        return away.index(d + ZS if d <= -HALF else d)

    tp = lax.axis_index("tp")
    dp = lax.axis_index("dp")
    y = lax.axis_index("edp")
    x, h = lax.div(tp, HS), lax.rem(tp, HS)
    z, c = lax.div(dp, CS), lax.rem(dp, CS)
    yy = h * YS + y
    me8 = c * YS + y

    def at_y(delta, core):
        there = lax.rem(yy + delta + HS * YS, HS * YS)
        ylo = lax.rem(there, YS)
        return (x * HS + lax.div(there, YS), z * CS + core, ylo), core * YS + ylo

    def at_z(delta):
        zz = lax.rem(z + delta + ZS, ZS)
        return (tp, zz * CS + c, y), zz

    def at_x(delta):
        xx = lax.rem(x + delta, XS)
        return (xx * HS + h, dp, y), xx

    out_y = [at_y(2, 0), at_y(-2, 1), at_y(1, 0), at_y(-1, 0), at_y(1, 1), at_y(-1, 1), at_y(0, 1 - c)]
    all_y = [at_y(delta, core) for delta in (4, 3, -3, 2, -2, 1, -1) for core in range(CS)] + [at_y(0, 1 - c)]
    peers_z = [at_z(away[r]) for r in range(ZS - 1, 0, -1)]
    slots_z = list(range(ZS - 1, 0, -1))
    peers_x = [at_x(i) for i in ((2, 1, 3) if XS == 4 else range(1, XS))]
    near_x = [i for i in range(XS - 1) if XS < 4 or i > 0]

    barrier = pltpu.get_barrier_semaphore()
    hello = [d for d, _ in peers_z] + [d for d, _ in peers_x] + [d for d, _ in all_y]
    for d in hello:
        pl.semaphore_signal(barrier, inc=1, device_id=d, device_id_type=MESH)

    def col(start, size):
        return pl.ds(pl.multiple_of(start, size), size)

    def blk(start, size):
        return pl.ds(pl.multiple_of(start * size, size), size)

    get_r = pltpu.make_async_copy(routes_hbm, routes_ref, loc.at[1 + NR + 2 * NQ + NQ * GROUPS])
    get_r.start()
    get_t = [
        pltpu.make_async_copy(grad_hbm.at[:, col(x * DX + p * DR, DR)], tok.at[p, 0:TOK], loc.at[1 + p])
        for p in range(NR)
    ]
    for d in get_t:
        d.start()
    get_h = pltpu.make_async_copy(hid_hbm.at[0], hraw, loc.at[0])
    get_h.start()

    def own_w(q):
        return pltpu.make_async_copy(
            w_hbm.at[0, :, col(x * DX + q * DQ, DQ)], wv.at[q, blk(x, FFD)], loc.at[1 + NR + q])

    for q in range(NQ):
        own_w(q).start()

    get_r.wait()
    routes_v = routes_ref[...]
    eidx = iota((EXP, TOK), 0)
    chosen = jnp.zeros((EXP, TOK), F32)
    gate_t = jnp.zeros((EXP, TOK), F32)
    gates_f = gates_ref[...].astype(F32)
    for k in range(TOP):
        hit = routes_v[k:k + 1, :] == eidx
        chosen = jnp.where(hit, 1.0, chosen)
        gate_t = jnp.where(hit, gates_f[k:k + 1, :], gate_t)
    earlier = (iota((TOK, TOK), 0) < iota((TOK, TOK), 1)).astype(F32).astype(BF16)
    count = jnp.dot(chosen.astype(BF16), earlier, preferred_element_type=F32)
    qt = jnp.where(chosen > 0.5, count, -1.0)
    table = jnp.zeros((EXP, TOK), F32)
    pidx = iota((EXP, TOK), 1)
    for p in range(CAP):
        value = jnp.sum(jnp.where(qt == float(p), gate_t, 0.0), axis=1, keepdims=True)
        table = jnp.where(pidx == p, value, table)
    for i in range(ZS):
        qsend[i, 0:E8] = qt[i * E8:(i + 1) * E8]
        qsend[i, E8:2 * E8] = table[i * E8:(i + 1) * E8]
    qrecv[0] = qsend[z]

    lane = (iota((1, SLOTS), 1).astype(F32) + 0.5)
    group = jnp.floor(lane * (1.0 / BLK))
    inner = (lane - group * BLK).astype(jnp.int32)
    group = group.astype(jnp.int32)
    part_z = jnp.zeros((1, SLOTS), jnp.int32)
    from_z = jnp.zeros((1, SLOTS), jnp.int32)
    place = jnp.zeros((1, SLOTS), jnp.int32)
    start = 0
    for r, a, b in [seg for g in groups for seg in g]:
        here = (inner >= start) & (inner < start + b - a)
        part_z = jnp.where(here, r, part_z)
        from_z = jnp.where(here, lax.rem(z + away[r] + ZS, ZS), from_z)
        place = jnp.where(here, inner - (start - a), place)
        start += b - a
    source = group * ZS + part_z
    native = from_z * (E8 * CAP) + group * CAP + place

    PB = 128

    def build_perm(i, carry):
        perm[pl.ds(pl.multiple_of(i * PB, PB), PB), :] = (
            (iota((PB, SLOTS), 0) + i * PB) == native).astype(F32).astype(BF16)
        return carry

    lax.fori_loop(0, SLOTS // PB, build_perm, 0)

    get_h.wait()
    hx[blk(x, FFD), :] = jnp.dot(hraw[...], perm[...], preferred_element_type=F32).astype(BF16)

    pl.semaphore_wait(barrier, len(hello))

    def remote(src, dst, send_sem, recv_sem, dev):
        return pltpu.make_async_remote_copy(
            src_ref=src, dst_ref=dst, send_sem=send_sem, recv_sem=recv_sem, device_id=dev, device_id_type=MESH)

    waited = set()

    def have(p, d):
        r = slot(d)
        if r > 0 and (p, r) not in waited:
            waited.add((p, r))
            part = tok.at[p, r * TOK:(r + 1) * TOK]
            remote(part, part, zs.at[p, 0], zr.at[p, r], peers_z[-1][0]).wait_recv()

    sent = []

    def ring(s, pieces):
        for p in pieces:
            if s > HALF:
                continue
            for right in ([True, False] if s < HALF else [p % 2 == 0]):
                d = -(s - 1) if right else s - 1
                have(p, d)
                to = slot(d - 1 if right else d + 1)
                a = slot(d)
                dev = at_z(1 if right else -1)[0]
                copy = remote(
                    tok.at[p, a * TOK:(a + 1) * TOK], tok.at[p, to * TOK:(to + 1) * TOK],
                    zs.at[p, to], zr.at[p, to], dev)
                copy.start()
                sent.append(copy)

    def q_copy(i):
        dev, there = peers_z[i]
        r = slot(-away[slots_z[i]])
        return remote(qsend.at[there], qrecv.at[r], sms.at[K_Q, i], smr.at[K_Q, r], dev)

    def send_w(q, i):
        dev, there = peers_x[i]
        return remote(
            w_hbm.at[0, :, col(there * DX + q * DQ, DQ)], wv.at[q, blk(x, FFD)], ws.at[q, i], wr.at[q, x], dev)

    def send_h(i):
        dev, there = peers_x[i]
        part = hx.at[blk(x, FFD)]
        return remote(part, part, hsn.at[i], hr.at[x], dev)

    pieces = list(range(NR))
    for p in pieces[:NR // 2]:
        get_t[p].wait()
    ring(1, pieces[:NR // 2])
    for i in range(ZS - 1):
        q_copy(i).start()
    for i in near_x:
        send_h(i).start()
    for p in pieces[NR // 2:]:
        get_t[p].wait()
    ring(1, pieces[NR // 2:])
    for q in range(NQ):
        for i in near_x + [i for i in range(XS - 1) if i not in near_x]:
            send_w(q, i).start()

    def got_h(i):
        dev, there = peers_x[i]
        part = hx.at[blk(there, FFD)]
        remote(part, part, hsn.at[0], hr.at[there], dev).wait_recv()

    def pass_h(i):
        frm = peers_x[1 if i == 1 else 2][1]
        part = hx.at[pl.ds(pl.multiple_of(frm * FFD + i * (FFD // 2), FFD // 2), FFD // 2)]
        return remote(part, part, hfs.at[i], hfr.at[i], peers_x[2 if i == 1 else 1][0])

    def far_h():
        if XS == 4:
            for i in range(2):
                got_h(2 - i)
                pass_h(i).start()

    heard = set()

    def build_sel(g):
        if g >= GROUPS:
            return
        lo, hi = spans[g]
        n = sizes[g]
        at = iota((n, TOK), 0)
        for r in range(lo, hi):
            if r > 0 and r not in heard:
                heard.add(r)
                remote(qsend.at[0], qrecv.at[r], sms.at[K_Q, 0], smr.at[K_Q, r], peers_z[0][0]).wait_recv()
            want = jnp.full((n, TOK), -7, jnp.int32)
            start = 0
            for rr, a, b in groups[g]:
                if rr == r:
                    want = jnp.where((at >= start) & (at < start + b - a), at - (start - a), want)
                start += b - a
            want = want.astype(F32)
            tile = qrecv[r, 0:E8]
            for e in range(E8):
                sel[g][e * n:(e + 1) * n, (r - lo) * TOK:(r - lo + 1) * TOK] = (
                    want == tile[e:e + 1, :]).astype(F32).astype(BF16)

    def span_of(m):
        return firsts[m[0]], firsts[m[1]] + sizes[m[1]]

    def part_of(expert, m):
        lo, hi = span_of(m)
        return pl.ds(pl.multiple_of(expert * BLK + lo, 16), hi - lo)

    def send_y(q, m, i):
        dev, there = out_y[i]
        lo, hi = span_of(m)
        return remote(
            sendb.at[q, there, lo:hi], rows.at[q, part_of(me8, m)], ys.at[q, m[1], i], yr.at[q, m[1], me8], dev)

    def own_rows(q, m):
        lo, hi = span_of(m)
        return pltpu.make_async_copy(
            sendb.at[q, me8, lo:hi], rows.at[q, part_of(me8, m)], loc.at[1 + NR + NQ + q * GROUPS + m[1]])

    def select(q, g):
        if g >= GROUPS:
            return
        lo, hi = spans[g]
        n = sizes[g]
        for p in range(q * NR // NQ, (q + 1) * NR // NQ):
            for r in range(lo, hi):
                have(p, away[r])
            got = jnp.dot(sel[g][...], tok[p, lo * TOK:hi * TOK, :], preferred_element_type=F32).astype(BF16)
            at = (p - q * NR // NQ) * DR
            for e in range(E8):
                sendb[q, e, firsts[g]:firsts[g] + n, at:at + DR] = got[e * n:(e + 1) * n]
        for m in messages(q):
            if m[1] == g:
                for i in range(E8 - 1):
                    send_y(q, m, i).start()
                own_rows(q, m).start()

    def gy_copy(i):
        dev, there = out_y[i]
        return remote(gsy.at[there], gtab.at[me8], sms.at[K_GY, i], smr.at[K_GY, me8], dev)

    def gates_on():
        for r in range(1, ZS):
            if r not in heard:
                heard.add(r)
                remote(qsend.at[0], qrecv.at[r], sms.at[K_Q, 0], smr.at[K_Q, r], peers_z[0][0]).wait_recv()
        by_source = [qrecv[r, E8:2 * E8] for r in range(ZS)]
        for e in range(E8):
            gsy[e] = jnp.concatenate([tile[e:e + 1] for tile in by_source], axis=0)
        gtab[me8] = gsy[me8]
        for i in range(E8 - 1):
            gy_copy(i).start()

    first, second = pieces[:NR // 2], pieces[NR // 2:]
    build_sel(0)
    select(0, 0)
    select(1, 0)
    ring(2, first)
    build_sel(1)
    select(0, 1)
    ring(2, second)
    select(1, 1)
    ring(3, first)
    build_sel(2)
    select(0, 2)
    ring(3, second)
    select(1, 2)
    gates_on()
    build_sel(3)
    ring(4, first)
    select(0, 3)
    build_sel(4)
    ring(4, second)
    select(1, 3)
    select(0, 4)
    select(1, 4)
    far_h()

    def turn(there):
        for j in range(SLOTS // PB):
            hxt[there, j * PB:(j + 1) * PB, 0:FFD] = hx[blk(there, FFD), j * PB:(j + 1) * PB].T

    def wait_w(q, i):
        dev, there = peers_x[i]
        remote(
            w_hbm.at[0, :, col(x * DX + q * DQ, DQ)], wv.at[q, blk(there, FFD)],
            ws.at[q, 0], wr.at[q, there], dev).wait_recv()

    def turned(q, there):
        return jnp.dot(hxt[there, :, 0:FFD], wv[q, blk(there, FFD), :], preferred_element_type=F32)

    turn(x)
    for q in range(NQ):
        own_w(q).wait()
        gbk[q] = turned(q, x)
    for i in near_x:
        if XS < 4:
            got_h(i)
        turn(peers_x[i][1])
        for q in range(NQ):
            wait_w(q, i)
            gbk[q] = gbk[q] + turned(q, peers_x[i][1])
    for copy in sent:
        copy.wait_send()
    for i in range(ZS - 1):
        q_copy(i).wait_send()
    for i in near_x:
        send_h(i).wait_send()
        for q in range(NQ):
            send_w(q, i).wait_send()
    for dev, there in out_y:
        remote(gsy.at[there], gtab.at[there], sms.at[K_GY, 0], smr.at[K_GY, there], dev).wait_recv()
    spread = (iota((TOK, SLOTS), 0) == place).astype(F32)
    for j in range(SLOTS // PB):
        spread_t[j * PB:(j + 1) * PB, :] = spread[:, j * PB:(j + 1) * PB].T
    spread = spread.astype(BF16)
    gate_all = jnp.dot(gtab[...].reshape(EXP, TOK).astype(BF16), spread, preferred_element_type=F32)
    pick = iota((EXP, SLOTS), 0) == source
    gate_lane = jnp.sum(jnp.where(pick, gate_all, 0.0), axis=0, keepdims=True)

    def gated(there):
        part = blk(there, FFD)
        hs[part, :] = (hx[part, :].astype(F32) * gate_lane).astype(BF16)

    gated(x)
    for i in near_x:
        gated(peers_x[i][1])

    def get_far():
        for i in range(2):
            part = hx.at[pl.ds(pl.multiple_of(peers_x[0][1] * FFD + i * (FFD // 2), FFD // 2), FFD // 2)]
            remote(part, part, hfs.at[i], hfr.at[i], peers_x[1][0]).wait_recv()
        turn(peers_x[0][1])
        gated(peers_x[0][1])


    def wait_rows(q):
        for m in messages(q):
            own_rows(q, m).wait()
            lo, hi = span_of(m)
            for dev, there in out_y:
                remote(
                    sendb.at[q, there, lo:hi], rows.at[q, part_of(there, m)],
                    ys.at[q, m[1], 0], yr.at[q, m[1], there], dev).wait_recv()

    def send_o(q, i):
        dev, there = peers_x[i]
        return remote(
            wgs.at[q, blk(there, FFD)], out_hbm.at[0, :, col(x * DX + q * DQ, DQ)],
            osn.at[q, i], orc.at[q, x], dev)

    def own_o(q):
        return pltpu.make_async_copy(
            wgs.at[q, blk(x, FFD)], out_hbm.at[0, :, col(x * DX + q * DQ, DQ)],
            loc.at[1 + NR + NQ + NQ * GROUPS + q])

    def products(q, squares):
        wait_rows(q)
        for i in near_x + [XS - 1] + [i for i in range(XS - 1) if i not in near_x]:
            there = x if i == XS - 1 else peers_x[i][1]
            if i not in near_x and i < XS - 1 and q == 0:
                get_far()
            wg = jnp.dot(hs[blk(there, FFD), :], rows[q], preferred_element_type=F32)
            wgs[q, blk(there, FFD), :] = wg.astype(BF16)
            if i == XS - 1:
                own_o(q).start()
            else:
                send_o(q, i).start()
            squares = squares + jnp.sum((wg * wg).reshape(FFD // 8, 8, DQ), axis=0)
        return squares

    def fold(q):
        got = gbk[q]
        if XS == 4:
            wait_w(q, 0)
            got = got + turned(q, peers_x[0][1])
        both = got * rows[q].astype(F32)
        total = both[:, 0:128]
        for i in range(1, DQ // 128):
            total = total + both[:, i * 128:(i + 1) * 128]
        return total

    squares = products(0, jnp.zeros((8, DQ), F32))
    acc[...] = fold(0)
    for i in range(E8 - 1):
        gy_copy(i).wait_send()
        for m in messages(0):
            send_y(0, m, i).wait_send()
    for q in range(1, NQ):
        squares = products(q, squares)
    for q in range(1, NQ):
        acc[...] += fold(q)
    by_place = spread_t[...] * jnp.sum(acc[...], axis=1, keepdims=True)
    own_square = jnp.sum(jnp.sum(squares, axis=1, keepdims=True), axis=0, keepdims=True)

    high = by_place.astype(BF16)
    low = (by_place - high.astype(F32)).astype(BF16)
    pick_b = pick.astype(F32).astype(BF16)
    back = jnp.dot(pick_b, high, preferred_element_type=F32) + jnp.dot(pick_b, low, preferred_element_type=F32)
    back = jnp.where(iota((EXP, TOK), 1) == TOK - 1, own_square, back)
    for e in range(E8):
        rsend[e] = back[e * ZS:(e + 1) * ZS]

    def ry_copy(i):
        dev, there = all_y[i]
        return remote(rsend.at[there], ry.at[h * E8 + me8], sms.at[K_RY, i], smr.at[K_RY, h * E8 + me8], dev)

    def rz_copy(i):
        dev, there = peers_z[i]
        return remote(rzs.at[slots_z[i]], rz.at[z], sms.at[K_RZ, i], smr.at[K_RZ, z], dev)

    def gg_copy(i):
        dev, there = peers_x[i]
        return remote(gg.at[x], gg.at[x], sms.at[K_GG, i], smr.at[K_GG, x], dev)

    for i in range(len(all_y)):
        ry_copy(i).start()
    ry[h * E8 + me8] = rsend[me8]

    for q in range(1, NQ):
        for m in messages(q):
            for i in range(E8 - 1):
                send_y(q, m, i).wait_send()
    if XS == 4:
        for q in range(NQ):
            send_w(q, 0).wait_send()
        for i in range(2):
            pass_h(i).wait_send()

    for dev, there in all_y:
        there = lax.rem(dev[0], HS) * E8 + there
        remote(rsend.at[0], ry.at[there], sms.at[K_RY, 0], smr.at[K_RY, there], dev).wait_recv()

    by_sender = [ry[e] + ry[E8 + e] for e in range(E8)]
    for r in range(ZS):
        rzs[r] = jnp.concatenate([tile[r:r + 1] for tile in by_sender], axis=0)
    for i in range(ZS - 1):
        rz_copy(i).start()
    rz[z] = rzs[0]
    for dev, there in peers_z:
        remote(rzs.at[0], rz.at[there], sms.at[K_RZ, 0], smr.at[K_RZ, there], dev).wait_recv()

    by_expert = rz[...].reshape(EXP, TOK)
    qt2 = qsend[:, 0:E8, :].reshape(EXP, TOK)
    value = jnp.zeros((EXP, TOK), F32)
    for p in range(CAP):
        value = jnp.where(qt2 == float(p), by_expert[:, p:p + 1], value)
    found = [
        jnp.sum(jnp.where(routes_v[k:k + 1, :] == eidx, value, 0.0), axis=0, keepdims=True) for k in range(TOP)]
    gg[x, 0:TOP, :] = jnp.concatenate(found, axis=0)
    gg[x, 8:16, :] = jnp.broadcast_to(
        jnp.sum(by_expert[:, TOK - 1:TOK], axis=0, keepdims=True), (8, TOK))
    for i in range(XS - 1):
        gg_copy(i).start()
    for q in range(NQ):
        own_o(q).wait()
        for i in range(XS - 1):
            dev, there = peers_x[i]
            remote(
                wgs.at[q, blk(there, FFD)], out_hbm.at[0, :, col(there * DX + q * DQ, DQ)],
                osn.at[q, 0], orc.at[q, there], dev).wait_recv()
            send_o(q, i).wait_send()
    for i in range(ZS - 1):
        rz_copy(i).wait_send()
    for i in range(len(all_y)):
        ry_copy(i).wait_send()

    for dev, there in peers_x:
        remote(gg.at[x], gg.at[there], sms.at[K_GG, 0], smr.at[K_GG, there], dev).wait_recv()

    total = jnp.sum(gg[:, 8:16, :], axis=0)[0:1, 0:1]
    limit = clip_ratio * math.sqrt(FFD * D * TPS * EXP)
    factor = jnp.minimum(1.0, limit / (jnp.sqrt(total) + 1e-06))
    factor_ref[...] = jnp.broadcast_to(factor, factor_ref.shape)
    gg_ref[...] = jnp.sum(gg[:, 0:TOP, :], axis=0)
    for i in range(XS - 1):
        gg_copy(i).wait_send()


def scale_kernel(part_ref, factor_ref, gg_in, out_hbm, gg_out, buf, done, gg_done):
    gg_copy = pltpu.make_async_copy(gg_in, gg_out, gg_done)
    gg_copy.start()
    factor = factor_ref[0:1, 0:1]
    high = buf.shape[1]
    copies = []
    for i in range(buf.shape[0]):
        at = slice(i * high, (i + 1) * high)
        buf[i] = (part_ref[0, at, :].astype(F32) * factor).astype(BF16)
        copies.append(pltpu.make_async_copy(buf.at[i], out_hbm.at[0, at, :], done.at[i]))
        copies[-1].start()
    gg_copy.wait()
    for copy in copies:
        copy.wait()


def per_device(grad_out, routes, gates, hidden, w_down):
    E8, TPS = CS * YS, XS * HS
    TOK, D = grad_out.shape
    TOP = routes.shape[1]
    FFD, SLOTS = hidden.shape[1], hidden.shape[2]
    DX = D // XS
    DQ, DR = DX // NQ, DX // NR
    groups = slot_groups()
    GROUPS = len(groups)
    sizes = [sum(b - a for _, a, b in g) for g in groups]
    reach = [max(r for r, _, _ in g) + 1 - min(r for r, _, _ in g) for g in groups]
    vm = pltpu.VMEM
    dma = pltpu.SemaphoreType.DMA
    most = max(TPS, HS * E8, ZS)
    any_space = pl.BlockSpec(memory_space=pl.ANY)
    in_hbm = pl.BlockSpec(memory_space=pltpu.HBM)
    held = lambda a: pltpu.with_memory_space_constraint(a, pltpu.HBM)
    in_vmem = pl.BlockSpec(memory_space=pltpu.VMEM)
    part, factor, gate_grad = pl.pallas_call(
        kernel,
        out_shape=(
            jax.ShapeDtypeStruct((1, FFD, D), BF16),
            jax.ShapeDtypeStruct((8, 128), F32),
            jax.ShapeDtypeStruct((TOP, TOK), F32),
        ),
        in_specs=[in_hbm, in_vmem, in_hbm, in_hbm, in_hbm],
        out_specs=(any_space, in_vmem, in_vmem),
        scratch_shapes=[
            vm((TOP, TOK), jnp.int32),
            vm((NR, ZS * TOK, DR), BF16),
            [vm((E8 * n, k * TOK), BF16) for n, k in zip(sizes, reach)],
            vm((NQ, E8, ZS * CAP, DQ), BF16),
            vm((NQ, SLOTS, DQ), BF16),
            vm((ZS, 2 * E8, TOK), F32),
            vm((ZS, 2 * E8, TOK), F32),
            vm((E8, ZS, TOK), F32),
            vm((E8, ZS, TOK), F32),
            vm((FFD, SLOTS), BF16),
            vm((SLOTS, SLOTS), BF16),
            vm((XS * FFD, SLOTS), BF16),
            vm((XS * FFD, SLOTS), BF16),
            vm((XS, SLOTS, -(-FFD // 128) * 128), BF16),
            vm((NQ, XS * FFD, DQ), BF16),
            vm((NQ, XS * FFD, DQ), BF16),
            vm((NQ, SLOTS, DQ), F32),
            vm((SLOTS, 128), F32),
            vm((SLOTS, TOK), F32),
            vm((E8, ZS, TOK), F32),
            vm((HS * E8, ZS, TOK), F32),
            vm((ZS, E8, TOK), F32),
            vm((ZS, E8, TOK), F32),
            vm((XS, 16, TOK), F32),
            dma((2 + NR + 2 * NQ + NQ * GROUPS,)),
            dma((NR, ZS)),
            dma((NR, ZS)),
            dma((NQ, GROUPS, E8)),
            dma((NQ, GROUPS, E8)),
            dma((NQ, XS)),
            dma((NQ, XS)),
            dma((XS,)),
            dma((XS,)),
            dma((2,)),
            dma((2,)),
            dma((NQ, XS)),
            dma((NQ, XS)),
            dma((5, most)),
            dma((5, most)),
        ],
        compiler_params=pltpu.CompilerParams(
            collective_id=0, has_side_effects=True, vmem_limit_bytes=40 * 1024 * 1024),
        cost_estimate=pl.CostEstimate(
            flops=2 * 2 * SLOTS * FFD * D, bytes_accessed=8 * 1024 * 1024, transcendentals=0),
        name="moe_down_backward",
    )(
        held(routes.T), gates.T, held(grad_out), held(hidden), held(w_down))
    high = 32 if FFD % 32 == 0 else FFD
    down_grad, gate_grad = pl.pallas_call(
        scale_kernel,
        out_shape=(
            jax.ShapeDtypeStruct((1, FFD, D), BF16),
            jax.ShapeDtypeStruct((TOP, TOK), F32),
        ),
        in_specs=[in_vmem, in_vmem, in_vmem],
        out_specs=(any_space, any_space),
        scratch_shapes=[vm((FFD // high, high, D), BF16), dma((FFD // high,)), dma(())],
        compiler_params=pltpu.CompilerParams(vmem_limit_bytes=8 * 1024 * 1024),
        cost_estimate=pl.CostEstimate(flops=FFD * D, bytes_accessed=4 * FFD * D, transcendentals=0),
        name="scale_products",
    )(part, factor, gate_grad)
    return (down_grad, gate_grad.T)


def solution(mesh):
    in_specs = (
        P(("dp", "edp"), None),
        P(("dp", "edp"), None),
        P(("dp", "edp"), None),
        P(("dp", "edp"), "tp", None),
        P(("dp", "edp"), "tp", None),
    )
    out_specs = (P(("dp", "edp"), "tp", None), P(("dp", "edp"), None))
    return jax.shard_map(
        per_device, mesh=mesh, in_specs=in_specs, out_specs=out_specs, check_vma=False
    )
```

```python
import functools
import math

import jax
import jax.numpy as jnp
from jax import lax
from jax.experimental import pallas as pl
from jax.experimental.pallas import tpu as pltpu
from jax.sharding import PartitionSpec as P

clip_ratio = 0.25

XS, HS, ZS, CS, YS = 4, 2, 8, 2, 4
NQ = 2
NR = 4
CAP = 20
AWAY = {8: [0, 1, -1, -2, 2, 3, -3, 4], 4: [0, 1, -1, 2], 2: [0, 1]}
MESH = pl.DeviceIdType.MESH
F32, BF16 = jnp.float32, jnp.bfloat16


def slot_groups():
    whole = CAP // 16 * 16
    rest = lambda parts: [(r, whole, CAP) for r in parts if CAP > whole]
    head = lambda parts: [(r, 0, whole) for r in parts]
    if ZS == 8:
        return [
            head([0]), head([1, 2]), head([3, 4]) + rest([0, 1, 2, 3]), head([5, 6]), head([7]) + rest([4, 5, 6, 7])]
    if ZS == 4:
        return [head([0]), head([1, 2]), head([3]) + rest([0, 1, 2, 3])]
    return [head([0]), head([1]) + rest([0, 1])]


def messages(q):
    count = len(slot_groups())
    if q == 0:
        return [(g, g) for g in range(count)]
    return [(0, 0), (1, 1), (2, 2), (3, 4)] if count == 5 else [(0, 1), (2, 2)] if count == 3 else [(0, 1)]


K_Q, K_GY, K_RY, K_RZ, K_GG = range(5)


def iota(shape, dim):
    return lax.broadcasted_iota(jnp.int32, shape, dim)


def kernel(
    routes_hbm, gates_ref, grad_hbm, hid_hbm, w_hbm,
    out_hbm, factor_ref, gg_ref,
    routes_ref, tok, sel, sendb, rows, qsend, qrecv, gsy, gtab,
    hraw, perm, hx, hs, hxt, wv, wgs, gbk, acc, spread_t, rsend, ry, rzs, rz, gg,
    loc, zs, zr, ys, yr, ws, wr, hsn, hr, hfs, hfr, osn, orc, sms, smr,
):
    E8 = CS * YS
    TPS = XS * HS
    EXP = ZS * E8
    TOK, TOP = routes_ref.shape[1], routes_ref.shape[0]
    FFD = hid_hbm.shape[1]
    SLOTS = hid_hbm.shape[2]
    D = w_hbm.shape[2]
    DX = D // XS
    DQ = DX // NQ
    DR = DX // NR
    BLK = ZS * CAP
    HALF = ZS // 2
    away = AWAY[ZS]
    groups = slot_groups()
    GROUPS = len(groups)
    sizes = [sum(b - a for _, a, b in g) for g in groups]
    firsts = [sum(sizes[:i]) for i in range(GROUPS)]
    spans = [(min(r for r, _, _ in g), max(r for r, _, _ in g) + 1) for g in groups]

    def slot(d):
        return away.index(d + ZS if d <= -HALF else d)

    tp = lax.axis_index("tp")
    dp = lax.axis_index("dp")
    y = lax.axis_index("edp")
    x, h = lax.div(tp, HS), lax.rem(tp, HS)
    z, c = lax.div(dp, CS), lax.rem(dp, CS)
    yy = h * YS + y
    me8 = c * YS + y

    def at_y(delta, core):
        there = lax.rem(yy + delta + HS * YS, HS * YS)
        ylo = lax.rem(there, YS)
        return (x * HS + lax.div(there, YS), z * CS + core, ylo), core * YS + ylo

    def at_z(delta):
        zz = lax.rem(z + delta + ZS, ZS)
        return (tp, zz * CS + c, y), zz

    def at_x(delta):
        xx = lax.rem(x + delta, XS)
        return (xx * HS + h, dp, y), xx

    out_y = [at_y(2, 0), at_y(-2, 1), at_y(1, 0), at_y(-1, 0), at_y(1, 1), at_y(-1, 1), at_y(0, 1 - c)]
    all_y = [at_y(delta, core) for delta in (4, 3, -3, 2, -2, 1, -1) for core in range(CS)] + [at_y(0, 1 - c)]
    peers_z = [at_z(away[r]) for r in range(ZS - 1, 0, -1)]
    slots_z = list(range(ZS - 1, 0, -1))
    peers_x = [at_x(i) for i in ((2, 1, 3) if XS == 4 else range(1, XS))]
    near_x = [i for i in range(XS - 1) if XS < 4 or i > 0]

    barrier = pltpu.get_barrier_semaphore()
    hello = [d for d, _ in peers_z] + [d for d, _ in peers_x] + [d for d, _ in all_y]
    for d in hello:
        pl.semaphore_signal(barrier, inc=1, device_id=d, device_id_type=MESH)

    def col(start, size):
        return pl.ds(pl.multiple_of(start, size), size)

    def blk(start, size):
        return pl.ds(pl.multiple_of(start * size, size), size)

    get_r = pltpu.make_async_copy(routes_hbm, routes_ref, loc.at[1 + NR + 2 * NQ + NQ * GROUPS])
    get_r.start()
    get_t = [
        pltpu.make_async_copy(grad_hbm.at[:, col(x * DX + p * DR, DR)], tok.at[p, 0:TOK], loc.at[1 + p])
        for p in range(NR)
    ]
    for d in get_t:
        d.start()
    get_h = pltpu.make_async_copy(hid_hbm.at[0], hraw, loc.at[0])
    get_h.start()

    def own_w(q):
        return pltpu.make_async_copy(
            w_hbm.at[0, :, col(x * DX + q * DQ, DQ)], wv.at[q, blk(x, FFD)], loc.at[1 + NR + q])

    for q in range(NQ):
        own_w(q).start()

    get_r.wait()
    routes_v = routes_ref[...]
    eidx = iota((EXP, TOK), 0)
    chosen = jnp.zeros((EXP, TOK), F32)
    gate_t = jnp.zeros((EXP, TOK), F32)
    gates_f = gates_ref[...].astype(F32)
    for k in range(TOP):
        hit = routes_v[k:k + 1, :] == eidx
        chosen = jnp.where(hit, 1.0, chosen)
        gate_t = jnp.where(hit, gates_f[k:k + 1, :], gate_t)
    earlier = (iota((TOK, TOK), 0) < iota((TOK, TOK), 1)).astype(F32).astype(BF16)
    count = jnp.dot(chosen.astype(BF16), earlier, preferred_element_type=F32)
    qt = jnp.where(chosen > 0.5, count, -1.0)
    table = jnp.zeros((EXP, TOK), F32)
    pidx = iota((EXP, TOK), 1)
    for p in range(CAP):
        value = jnp.sum(jnp.where(qt == float(p), gate_t, 0.0), axis=1, keepdims=True)
        table = jnp.where(pidx == p, value, table)
    for i in range(ZS):
        qsend[i, 0:E8] = qt[i * E8:(i + 1) * E8]
        qsend[i, E8:2 * E8] = table[i * E8:(i + 1) * E8]
    qrecv[0] = qsend[z]

    lane = (iota((1, SLOTS), 1).astype(F32) + 0.5)
    group = jnp.floor(lane * (1.0 / BLK))
    inner = (lane - group * BLK).astype(jnp.int32)
    group = group.astype(jnp.int32)
    part_z = jnp.zeros((1, SLOTS), jnp.int32)
    from_z = jnp.zeros((1, SLOTS), jnp.int32)
    place = jnp.zeros((1, SLOTS), jnp.int32)
    start = 0
    for r, a, b in [seg for g in groups for seg in g]:
        here = (inner >= start) & (inner < start + b - a)
        part_z = jnp.where(here, r, part_z)
        from_z = jnp.where(here, lax.rem(z + away[r] + ZS, ZS), from_z)
        place = jnp.where(here, inner - (start - a), place)
        start += b - a
    source = group * ZS + part_z
    native = from_z * (E8 * CAP) + group * CAP + place

    PB = 128

    def build_perm(i, carry):
        perm[pl.ds(pl.multiple_of(i * PB, PB), PB), :] = (
            (iota((PB, SLOTS), 0) + i * PB) == native).astype(F32).astype(BF16)
        return carry

    lax.fori_loop(0, SLOTS // PB, build_perm, 0)

    get_h.wait()
    hx[blk(x, FFD), :] = jnp.dot(hraw[...], perm[...], preferred_element_type=F32).astype(BF16)

    pl.semaphore_wait(barrier, len(hello))

    def remote(src, dst, send_sem, recv_sem, dev):
        return pltpu.make_async_remote_copy(
            src_ref=src, dst_ref=dst, send_sem=send_sem, recv_sem=recv_sem, device_id=dev, device_id_type=MESH)

    waited = set()

    def have(p, d):
        r = slot(d)
        if r > 0 and (p, r) not in waited:
            waited.add((p, r))
            part = tok.at[p, r * TOK:(r + 1) * TOK]
            remote(part, part, zs.at[p, 0], zr.at[p, r], peers_z[-1][0]).wait_recv()

    sent = []

    def ring(s, pieces):
        for p in pieces:
            if s > HALF:
                continue
            for right in ([True, False] if s < HALF else [p % 2 == 0]):
                d = -(s - 1) if right else s - 1
                have(p, d)
                to = slot(d - 1 if right else d + 1)
                a = slot(d)
                dev = at_z(1 if right else -1)[0]
                copy = remote(
                    tok.at[p, a * TOK:(a + 1) * TOK], tok.at[p, to * TOK:(to + 1) * TOK],
                    zs.at[p, to], zr.at[p, to], dev)
                copy.start()
                sent.append(copy)

    def q_copy(i):
        dev, there = peers_z[i]
        r = slot(-away[slots_z[i]])
        return remote(qsend.at[there], qrecv.at[r], sms.at[K_Q, i], smr.at[K_Q, r], dev)

    def send_w(q, i):
        dev, there = peers_x[i]
        return remote(
            w_hbm.at[0, :, col(there * DX + q * DQ, DQ)], wv.at[q, blk(x, FFD)], ws.at[q, i], wr.at[q, x], dev)

    def send_h(i):
        dev, there = peers_x[i]
        part = hx.at[blk(x, FFD)]
        return remote(part, part, hsn.at[i], hr.at[x], dev)

    pieces = list(range(NR))
    for p in pieces[:NR // 2]:
        get_t[p].wait()
    ring(1, pieces[:NR // 2])
    for i in range(ZS - 1):
        q_copy(i).start()
    for i in near_x:
        send_h(i).start()
    for p in pieces[NR // 2:]:
        get_t[p].wait()
    ring(1, pieces[NR // 2:])
    for q in range(NQ):
        for i in near_x + [i for i in range(XS - 1) if i not in near_x]:
            send_w(q, i).start()

    def got_h(i):
        dev, there = peers_x[i]
        part = hx.at[blk(there, FFD)]
        remote(part, part, hsn.at[0], hr.at[there], dev).wait_recv()

    def pass_h(i):
        frm = peers_x[1 if i == 1 else 2][1]
        part = hx.at[pl.ds(pl.multiple_of(frm * FFD + i * (FFD // 2), FFD // 2), FFD // 2)]
        return remote(part, part, hfs.at[i], hfr.at[i], peers_x[2 if i == 1 else 1][0])

    def far_h():
        if XS == 4:
            for i in range(2):
                got_h(2 - i)
                pass_h(i).start()

    heard = set()

    def build_sel(g):
        if g >= GROUPS:
            return
        lo, hi = spans[g]
        n = sizes[g]
        at = iota((n, TOK), 0)
        for r in range(lo, hi):
            if r > 0 and r not in heard:
                heard.add(r)
                remote(qsend.at[0], qrecv.at[r], sms.at[K_Q, 0], smr.at[K_Q, r], peers_z[0][0]).wait_recv()
            want = jnp.full((n, TOK), -7, jnp.int32)
            start = 0
            for rr, a, b in groups[g]:
                if rr == r:
                    want = jnp.where((at >= start) & (at < start + b - a), at - (start - a), want)
                start += b - a
            want = want.astype(F32)
            tile = qrecv[r, 0:E8]
            for e in range(E8):
                sel[g][e * n:(e + 1) * n, (r - lo) * TOK:(r - lo + 1) * TOK] = (
                    want == tile[e:e + 1, :]).astype(F32).astype(BF16)

    def span_of(m):
        return firsts[m[0]], firsts[m[1]] + sizes[m[1]]

    def part_of(expert, m):
        lo, hi = span_of(m)
        return pl.ds(pl.multiple_of(expert * BLK + lo, 16), hi - lo)

    def send_y(q, m, i):
        dev, there = out_y[i]
        lo, hi = span_of(m)
        return remote(
            sendb.at[q, there, lo:hi], rows.at[q, part_of(me8, m)], ys.at[q, m[1], i], yr.at[q, m[1], me8], dev)

    def own_rows(q, m):
        lo, hi = span_of(m)
        return pltpu.make_async_copy(
            sendb.at[q, me8, lo:hi], rows.at[q, part_of(me8, m)], loc.at[1 + NR + NQ + q * GROUPS + m[1]])

    def select(q, g):
        if g >= GROUPS:
            return
        lo, hi = spans[g]
        n = sizes[g]
        for p in range(q * NR // NQ, (q + 1) * NR // NQ):
            for r in range(lo, hi):
                have(p, away[r])
            got = jnp.dot(sel[g][...], tok[p, lo * TOK:hi * TOK, :], preferred_element_type=F32).astype(BF16)
            at = (p - q * NR // NQ) * DR
            for e in range(E8):
                sendb[q, e, firsts[g]:firsts[g] + n, at:at + DR] = got[e * n:(e + 1) * n]
        for m in messages(q):
            if m[1] == g:
                for i in range(E8 - 1):
                    send_y(q, m, i).start()
                own_rows(q, m).start()

    def gy_copy(i):
        dev, there = out_y[i]
        return remote(gsy.at[there], gtab.at[me8], sms.at[K_GY, i], smr.at[K_GY, me8], dev)

    def gates_on():
        for r in range(1, ZS):
            if r not in heard:
                heard.add(r)
                remote(qsend.at[0], qrecv.at[r], sms.at[K_Q, 0], smr.at[K_Q, r], peers_z[0][0]).wait_recv()
        by_source = [qrecv[r, E8:2 * E8] for r in range(ZS)]
        for e in range(E8):
            gsy[e] = jnp.concatenate([tile[e:e + 1] for tile in by_source], axis=0)
        gtab[me8] = gsy[me8]
        for i in range(E8 - 1):
            gy_copy(i).start()

    first, second = pieces[:NR // 2], pieces[NR // 2:]
    build_sel(0)
    select(0, 0)
    select(1, 0)
    ring(2, first)
    build_sel(1)
    select(0, 1)
    ring(2, second)
    select(1, 1)
    ring(3, first)
    build_sel(2)
    select(0, 2)
    ring(3, second)
    select(1, 2)
    gates_on()
    build_sel(3)
    ring(4, first)
    select(0, 3)
    build_sel(4)
    ring(4, second)
    select(1, 3)
    select(0, 4)
    select(1, 4)
    far_h()

    def turn(there):
        for j in range(SLOTS // PB):
            hxt[there, j * PB:(j + 1) * PB, 0:FFD] = hx[blk(there, FFD), j * PB:(j + 1) * PB].T

    def wait_w(q, i):
        dev, there = peers_x[i]
        remote(
            w_hbm.at[0, :, col(x * DX + q * DQ, DQ)], wv.at[q, blk(there, FFD)],
            ws.at[q, 0], wr.at[q, there], dev).wait_recv()

    def turned(q, there):
        return jnp.dot(hxt[there, :, 0:FFD], wv[q, blk(there, FFD), :], preferred_element_type=F32)

    turn(x)
    for q in range(NQ):
        own_w(q).wait()
        gbk[q] = turned(q, x)
    for i in near_x:
        if XS < 4:
            got_h(i)
        turn(peers_x[i][1])
        for q in range(NQ):
            wait_w(q, i)
            gbk[q] = gbk[q] + turned(q, peers_x[i][1])
    for copy in sent:
        copy.wait_send()
    for i in range(ZS - 1):
        q_copy(i).wait_send()
    for i in near_x:
        send_h(i).wait_send()
        for q in range(NQ):
            send_w(q, i).wait_send()
    for dev, there in out_y:
        remote(gsy.at[there], gtab.at[there], sms.at[K_GY, 0], smr.at[K_GY, there], dev).wait_recv()
    spread = (iota((TOK, SLOTS), 0) == place).astype(F32)
    for j in range(SLOTS // PB):
        spread_t[j * PB:(j + 1) * PB, :] = spread[:, j * PB:(j + 1) * PB].T
    spread = spread.astype(BF16)
    gate_all = jnp.dot(gtab[...].reshape(EXP, TOK).astype(BF16), spread, preferred_element_type=F32)
    pick = iota((EXP, SLOTS), 0) == source
    gate_lane = jnp.sum(jnp.where(pick, gate_all, 0.0), axis=0, keepdims=True)

    def gated(there):
        part = blk(there, FFD)
        hs[part, :] = (hx[part, :].astype(F32) * gate_lane).astype(BF16)

    gated(x)
    for i in near_x:
        gated(peers_x[i][1])

    def get_far():
        for i in range(2):
            part = hx.at[pl.ds(pl.multiple_of(peers_x[0][1] * FFD + i * (FFD // 2), FFD // 2), FFD // 2)]
            remote(part, part, hfs.at[i], hfr.at[i], peers_x[1][0]).wait_recv()
        turn(peers_x[0][1])
        gated(peers_x[0][1])


    def wait_rows(q):
        for m in messages(q):
            own_rows(q, m).wait()
            lo, hi = span_of(m)
            for dev, there in out_y:
                remote(
                    sendb.at[q, there, lo:hi], rows.at[q, part_of(there, m)],
                    ys.at[q, m[1], 0], yr.at[q, m[1], there], dev).wait_recv()

    def send_o(q, i):
        dev, there = peers_x[i]
        return remote(
            wgs.at[q, blk(there, FFD)], out_hbm.at[0, :, col(x * DX + q * DQ, DQ)],
            osn.at[q, i], orc.at[q, x], dev)

    def own_o(q):
        return pltpu.make_async_copy(
            wgs.at[q, blk(x, FFD)], out_hbm.at[0, :, col(x * DX + q * DQ, DQ)],
            loc.at[1 + NR + NQ + NQ * GROUPS + q])

    def products(q, squares):
        wait_rows(q)
        far_x = [i for i in range(XS - 1) if i not in near_x]
        for i in near_x + [XS - 1] + far_x if q == 0 else far_x + near_x + [XS - 1]:
            there = x if i == XS - 1 else peers_x[i][1]
            if i not in near_x and i < XS - 1 and q == 0:
                get_far()
            wg = jnp.dot(hs[blk(there, FFD), :], rows[q], preferred_element_type=F32)
            wgs[q, blk(there, FFD), :] = wg.astype(BF16)
            if i == XS - 1:
                own_o(q).start()
            else:
                send_o(q, i).start()
            squares = squares + jnp.sum((wg * wg).reshape(FFD // 8, 8, DQ), axis=0)
        return squares

    def fold(q):
        got = gbk[q]
        if XS == 4:
            wait_w(q, 0)
            got = got + turned(q, peers_x[0][1])
        both = got * rows[q].astype(F32)
        total = both[:, 0:128]
        for i in range(1, DQ // 128):
            total = total + both[:, i * 128:(i + 1) * 128]
        return total

    squares = products(0, jnp.zeros((8, DQ), F32))
    acc[...] = fold(0)
    for i in range(E8 - 1):
        gy_copy(i).wait_send()
        for m in messages(0):
            send_y(0, m, i).wait_send()
    for q in range(1, NQ):
        squares = products(q, squares)
    for q in range(1, NQ):
        acc[...] += fold(q)
    by_place = spread_t[...] * jnp.sum(acc[...], axis=1, keepdims=True)
    own_square = jnp.sum(jnp.sum(squares, axis=1, keepdims=True), axis=0, keepdims=True)

    high = by_place.astype(BF16)
    low = (by_place - high.astype(F32)).astype(BF16)
    pick_b = pick.astype(F32).astype(BF16)
    back = jnp.dot(pick_b, high, preferred_element_type=F32) + jnp.dot(pick_b, low, preferred_element_type=F32)
    back = jnp.where(iota((EXP, TOK), 1) == TOK - 1, own_square, back)
    for e in range(E8):
        rsend[e] = back[e * ZS:(e + 1) * ZS]

    def ry_copy(i):
        dev, there = all_y[i]
        return remote(rsend.at[there], ry.at[h * E8 + me8], sms.at[K_RY, i], smr.at[K_RY, h * E8 + me8], dev)

    def rz_copy(i):
        dev, there = peers_z[i]
        return remote(rzs.at[slots_z[i]], rz.at[z], sms.at[K_RZ, i], smr.at[K_RZ, z], dev)

    def gg_copy(i):
        dev, there = peers_x[i]
        return remote(gg.at[x], gg.at[x], sms.at[K_GG, i], smr.at[K_GG, x], dev)

    for i in range(len(all_y)):
        ry_copy(i).start()
    ry[h * E8 + me8] = rsend[me8]

    for q in range(1, NQ):
        for m in messages(q):
            for i in range(E8 - 1):
                send_y(q, m, i).wait_send()
    if XS == 4:
        for q in range(NQ):
            send_w(q, 0).wait_send()
        for i in range(2):
            pass_h(i).wait_send()

    for dev, there in all_y:
        there = lax.rem(dev[0], HS) * E8 + there
        remote(rsend.at[0], ry.at[there], sms.at[K_RY, 0], smr.at[K_RY, there], dev).wait_recv()

    by_sender = [ry[e] + ry[E8 + e] for e in range(E8)]
    for r in range(ZS):
        rzs[r] = jnp.concatenate([tile[r:r + 1] for tile in by_sender], axis=0)
    for i in range(ZS - 1):
        rz_copy(i).start()
    rz[z] = rzs[0]
    for dev, there in peers_z:
        remote(rzs.at[0], rz.at[there], sms.at[K_RZ, 0], smr.at[K_RZ, there], dev).wait_recv()

    by_expert = rz[...].reshape(EXP, TOK)
    qt2 = qsend[:, 0:E8, :].reshape(EXP, TOK)
    value = jnp.zeros((EXP, TOK), F32)
    for p in range(CAP):
        value = jnp.where(qt2 == float(p), by_expert[:, p:p + 1], value)
    found = [
        jnp.sum(jnp.where(routes_v[k:k + 1, :] == eidx, value, 0.0), axis=0, keepdims=True) for k in range(TOP)]
    gg[x, 0:TOP, :] = jnp.concatenate(found, axis=0)
    gg[x, 8:16, :] = jnp.broadcast_to(
        jnp.sum(by_expert[:, TOK - 1:TOK], axis=0, keepdims=True), (8, TOK))
    for i in range(XS - 1):
        gg_copy(i).start()
    for q in range(NQ):
        own_o(q).wait()
        for i in range(XS - 1):
            dev, there = peers_x[i]
            remote(
                wgs.at[q, blk(there, FFD)], out_hbm.at[0, :, col(there * DX + q * DQ, DQ)],
                osn.at[q, 0], orc.at[q, there], dev).wait_recv()
            send_o(q, i).wait_send()
    for i in range(ZS - 1):
        rz_copy(i).wait_send()
    for i in range(len(all_y)):
        ry_copy(i).wait_send()

    for dev, there in peers_x:
        remote(gg.at[x], gg.at[there], sms.at[K_GG, 0], smr.at[K_GG, there], dev).wait_recv()

    total = jnp.sum(gg[:, 8:16, :], axis=0)[0:1, 0:1]
    limit = clip_ratio * math.sqrt(FFD * D * TPS * EXP)
    factor = jnp.minimum(1.0, limit / (jnp.sqrt(total) + 1e-06))
    factor_ref[...] = jnp.broadcast_to(factor, factor_ref.shape)
    gg_ref[...] = jnp.sum(gg[:, 0:TOP, :], axis=0)
    for i in range(XS - 1):
        gg_copy(i).wait_send()


def scale_kernel(part_ref, factor_ref, gg_in, out_hbm, gg_out, buf, done, gg_done):
    gg_copy = pltpu.make_async_copy(gg_in, gg_out, gg_done)
    gg_copy.start()
    factor = factor_ref[0:1, 0:1]
    high = buf.shape[1]
    copies = []
    for i in range(buf.shape[0]):
        at = slice(i * high, (i + 1) * high)
        buf[i] = (part_ref[0, at, :].astype(F32) * factor).astype(BF16)
        copies.append(pltpu.make_async_copy(buf.at[i], out_hbm.at[0, at, :], done.at[i]))
        copies[-1].start()
    gg_copy.wait()
    for copy in copies:
        copy.wait()


def per_device(grad_out, routes, gates, hidden, w_down):
    E8, TPS = CS * YS, XS * HS
    TOK, D = grad_out.shape
    TOP = routes.shape[1]
    FFD, SLOTS = hidden.shape[1], hidden.shape[2]
    DX = D // XS
    DQ, DR = DX // NQ, DX // NR
    groups = slot_groups()
    GROUPS = len(groups)
    sizes = [sum(b - a for _, a, b in g) for g in groups]
    reach = [max(r for r, _, _ in g) + 1 - min(r for r, _, _ in g) for g in groups]
    vm = pltpu.VMEM
    dma = pltpu.SemaphoreType.DMA
    most = max(TPS, HS * E8, ZS)
    any_space = pl.BlockSpec(memory_space=pl.ANY)
    in_hbm = pl.BlockSpec(memory_space=pltpu.HBM)
    held = lambda a: pltpu.with_memory_space_constraint(a, pltpu.HBM)
    in_vmem = pl.BlockSpec(memory_space=pltpu.VMEM)
    part, factor, gate_grad = pl.pallas_call(
        kernel,
        out_shape=(
            jax.ShapeDtypeStruct((1, FFD, D), BF16),
            jax.ShapeDtypeStruct((8, 128), F32),
            jax.ShapeDtypeStruct((TOP, TOK), F32),
        ),
        in_specs=[in_hbm, in_vmem, in_hbm, in_hbm, in_hbm],
        out_specs=(any_space, in_vmem, in_vmem),
        scratch_shapes=[
            vm((TOP, TOK), jnp.int32),
            vm((NR, ZS * TOK, DR), BF16),
            [vm((E8 * n, k * TOK), BF16) for n, k in zip(sizes, reach)],
            vm((NQ, E8, ZS * CAP, DQ), BF16),
            vm((NQ, SLOTS, DQ), BF16),
            vm((ZS, 2 * E8, TOK), F32),
            vm((ZS, 2 * E8, TOK), F32),
            vm((E8, ZS, TOK), F32),
            vm((E8, ZS, TOK), F32),
            vm((FFD, SLOTS), BF16),
            vm((SLOTS, SLOTS), BF16),
            vm((XS * FFD, SLOTS), BF16),
            vm((XS * FFD, SLOTS), BF16),
            vm((XS, SLOTS, -(-FFD // 128) * 128), BF16),
            vm((NQ, XS * FFD, DQ), BF16),
            vm((NQ, XS * FFD, DQ), BF16),
            vm((NQ, SLOTS, DQ), F32),
            vm((SLOTS, 128), F32),
            vm((SLOTS, TOK), F32),
            vm((E8, ZS, TOK), F32),
            vm((HS * E8, ZS, TOK), F32),
            vm((ZS, E8, TOK), F32),
            vm((ZS, E8, TOK), F32),
            vm((XS, 16, TOK), F32),
            dma((2 + NR + 2 * NQ + NQ * GROUPS,)),
            dma((NR, ZS)),
            dma((NR, ZS)),
            dma((NQ, GROUPS, E8)),
            dma((NQ, GROUPS, E8)),
            dma((NQ, XS)),
            dma((NQ, XS)),
            dma((XS,)),
            dma((XS,)),
            dma((2,)),
            dma((2,)),
            dma((NQ, XS)),
            dma((NQ, XS)),
            dma((5, most)),
            dma((5, most)),
        ],
        compiler_params=pltpu.CompilerParams(
            collective_id=0, has_side_effects=True, vmem_limit_bytes=40 * 1024 * 1024),
        cost_estimate=pl.CostEstimate(
            flops=2 * 2 * SLOTS * FFD * D, bytes_accessed=8 * 1024 * 1024, transcendentals=0),
        name="moe_down_backward",
    )(
        held(routes.T), gates.T, held(grad_out), held(hidden), held(w_down))
    high = 32 if FFD % 32 == 0 else FFD
    down_grad, gate_grad = pl.pallas_call(
        scale_kernel,
        out_shape=(
            jax.ShapeDtypeStruct((1, FFD, D), BF16),
            jax.ShapeDtypeStruct((TOP, TOK), F32),
        ),
        in_specs=[in_vmem, in_vmem, in_vmem],
        out_specs=(any_space, any_space),
        scratch_shapes=[vm((FFD // high, high, D), BF16), dma((FFD // high,)), dma(())],
        compiler_params=pltpu.CompilerParams(vmem_limit_bytes=8 * 1024 * 1024),
        cost_estimate=pl.CostEstimate(flops=FFD * D, bytes_accessed=4 * FFD * D, transcendentals=0),
        name="scale_products",
    )(part, factor, gate_grad)
    return (down_grad, gate_grad.T)


def solution(mesh):
    in_specs = (
        P(("dp", "edp"), None),
        P(("dp", "edp"), None),
        P(("dp", "edp"), None),
        P(("dp", "edp"), "tp", None),
        P(("dp", "edp"), "tp", None),
    )
    out_specs = (P(("dp", "edp"), "tp", None), P(("dp", "edp"), None))
    return jax.shard_map(
        per_device, mesh=mesh, in_specs=in_specs, out_specs=out_specs, check_vma=False
    )
```
